32 devices in a mesh: fsdp: 2 (over core), context: 4 (over y, x), tensor: 4 (over z).
Axes of the slice: x: 2, y: 2, z: 4, core: 2. Of those that a mesh axis runs over, the one named last changes fastest.
Arguments:
- tokens: bfloat16 [8192, 1024], P(('fsdp', 'context')), may hold values from -6 to 6
- encoder: bfloat16 [16384, 1024], P(('fsdp', 'context')), may hold values from -6 to 6
- cotangent: bfloat16 [8192, 1024], P(('fsdp', 'context')), may hold values from -6 to 6
- lengths: int32 [2, 2], P('fsdp'), may hold values from 1024 to 3072, as said below
- order: int32 [2, 4096], P('fsdp'), may hold values from 0 to 4095, as said below
- in_proj: float32 [6, 1024, 1024], P(None, ('fsdp', 'context'), 'tensor'), may hold values from -0.5625 to 0.5625
- out_proj: float32 [2, 1024, 1024], P(None, 'tensor', ('fsdp', 'context')), may hold values from -1.5 to 1.5
- w_up: float32 [1024, 4096], P(('fsdp', 'context'), 'tensor'), may hold values from -0.1875 to 0.1875
- w_down: float32 [4096, 1024], P('tensor', ('fsdp', 'context')), may hold values from -0.09375 to 0.09375
- head_bias: float32 [4, 128, 8], P(None, 'tensor', ('fsdp', 'context')), may hold values from -4 to 4
- up_bias: float32 [512, 8], P('tensor', ('fsdp', 'context')), may hold values from -4 to 4
- vectors: float32 [9, 1024], P(None, ('fsdp', 'context')), may hold values from -2 to 2
- in_first: float32 [6, 1024, 1024], P(None, ('fsdp', 'context'), 'tensor'), may hold values from -256 to 256
- out_first: float32 [2, 1024, 1024], P(None, 'tensor', ('fsdp', 'context')), may hold values from -80 to 80
- up_first: float32 [1024, 4096], P(('fsdp', 'context'), 'tensor'), may hold values from -224 to 224
- down_first: float32 [4096, 1024], P('tensor', ('fsdp', 'context')), may hold values from -256 to 256
- hbias_first: float32 [4, 128, 8], P(None, 'tensor', ('fsdp', 'context')), may hold values from -512 to 512
- ubias_first: float32 [512, 8], P('tensor', ('fsdp', 'context')), may hold values from -224 to 224
- vec_first: float32 [9, 1024], P(None, ('fsdp', 'context')), may hold values from -384 to 384
- in_second: float32 [6, 1024, 1024], P(None, ('fsdp', 'context'), 'tensor'), may hold values from 1024 to 8192
- out_second: float32 [2, 1024, 1024], P(None, 'tensor', ('fsdp', 'context')), may hold values from 92.16 to 737.28
- up_second: float32 [1024, 4096], P(('fsdp', 'context'), 'tensor'), may hold values from 655.36 to 5242.88
- down_second: float32 [4096, 1024], P('tensor', ('fsdp', 'context')), may hold values from 1024 to 8192
- hbias_second: float32 [4, 128, 8], P(None, 'tensor', ('fsdp', 'context')), may hold values from 4096 to 32768
- ubias_second: float32 [512, 8], P('tensor', ('fsdp', 'context')), may hold values from 655.36 to 5242.88
- vec_second: float32 [9, 1024], P(None, ('fsdp', 'context')), may hold values from 2007.04 to 16056.32
Outputs:
- out: float32 [8192, 1024], P(('fsdp', 'context'))
- grad_tokens: float32 [8192, 1024], P(('fsdp', 'context'), 'tensor')
- grad_encoder: float32 [16384, 1024], P(('fsdp', 'context'), 'tensor')
- clip_factors: float32 [16], P('tensor')
- in_proj_new: float32 [6, 1024, 1024], P(None, ('fsdp', 'context'), 'tensor')
- in_first_new: float32 [6, 1024, 1024], P(None, ('fsdp', 'context'), 'tensor')
- in_second_new: float32 [6, 1024, 1024], P(None, ('fsdp', 'context'), 'tensor')
- in_proj_copy: bfloat16 [6, 1024, 1024], P(None, ('fsdp', 'context'), 'tensor')
- out_proj_new: float32 [2, 1024, 1024], P(None, 'tensor', ('fsdp', 'context'))
- out_first_new: float32 [2, 1024, 1024], P(None, 'tensor', ('fsdp', 'context'))
- out_second_new: float32 [2, 1024, 1024], P(None, 'tensor', ('fsdp', 'context'))
- out_proj_copy: bfloat16 [2, 1024, 1024], P(None, 'tensor', ('fsdp', 'context'))
- w_up_new: float32 [1024, 4096], P(('fsdp', 'context'), 'tensor')
- up_first_new: float32 [1024, 4096], P(('fsdp', 'context'), 'tensor')
- up_second_new: float32 [1024, 4096], P(('fsdp', 'context'), 'tensor')
- w_up_copy: bfloat16 [1024, 4096], P(('fsdp', 'context'), 'tensor')
- w_down_new: float32 [4096, 1024], P('tensor', ('fsdp', 'context'))
- down_first_new: float32 [4096, 1024], P('tensor', ('fsdp', 'context'))
- down_second_new: float32 [4096, 1024], P('tensor', ('fsdp', 'context'))
- w_down_copy: bfloat16 [4096, 1024], P('tensor', ('fsdp', 'context'))
- head_bias_new: float32 [4, 128, 8], P(None, 'tensor', ('fsdp', 'context'))
- hbias_first_new: float32 [4, 128, 8], P(None, 'tensor', ('fsdp', 'context'))
- hbias_second_new: float32 [4, 128, 8], P(None, 'tensor', ('fsdp', 'context'))
- head_bias_copy: bfloat16 [4, 128, 8], P(None, 'tensor', ('fsdp', 'context'))
- up_bias_new: float32 [512, 8], P('tensor', ('fsdp', 'context'))
- ubias_first_new: float32 [512, 8], P('tensor', ('fsdp', 'context'))
- ubias_second_new: float32 [512, 8], P('tensor', ('fsdp', 'context'))
- up_bias_copy: bfloat16 [512, 8], P('tensor', ('fsdp', 'context'))
- vectors_new: float32 [9, 1024], P(None, ('fsdp', 'context'))
- vec_first_new: float32 [9, 1024], P(None, ('fsdp', 'context'))
- vec_second_new: float32 [9, 1024], P(None, ('fsdp', 'context'))
- vectors_copy: bfloat16 [9, 1024], P(None, ('fsdp', 'context'))
The draws below stay inside these ranges and needn't reach their ends.
Inputs may be any that keep to these rules, and one draw needn't show every extreme that they name: Each pack holds 2 sequences, in order, whose lengths sum to 4096. `order`: each row is a permutation of its pack's positions that deals rounds of 4 blocks of 128 positions: dealt row d * 1024 + r * 128 + k holds position (r * 4 + b) * 128 + k, where b runs over all blocks of round r as d runs over 0 to 3.
All inputs are finite; a program needn't handle non-finite values.
Results may differ from the reference program's by a relative error of at most 0.029.
Values may be sent and summed in bfloat16 or wider, within the bound.
No kernel may reach another device: no remote copies, remote signals or barrier semaphores. Data moves between devices by JAX's collectives and lax.ppermute only.
A program may use at most 256 MiB of HBM per device.

```python
import math
import jax
import jax.numpy as jnp
from jax import lax

D = 1024
H = 16
HEAD = 64
FF = 4096
TOK_DEV = 1024
ENC = 4096
BLK = 128
MINLEN = 1024
NSEQ = 2
STEP = 10
PACK = 4096
PACKS = 2
TOKENS = 8192
ENC_ROWS = 16384
SHARDS = 8
N_TENSOR = 4


def draw_lengths(key, part):
    key = jax.random.fold_in(key, 11)
    first_key, pick_key = jax.random.split(key)
    leading = jax.random.randint(first_key, (PACKS,), MINLEN, PACK - MINLEN + 1)
    chosen = jax.random.randint(pick_key, (), 0, PACKS)
    leading = jnp.where(jnp.arange(PACKS) == chosen, MINLEN, leading)
    return jnp.stack([leading, PACK - leading], axis=1).astype(jnp.int32)


def shuffle_round(round_key):
    return jax.random.permutation(round_key, PACK // TOK_DEV)


def draw_order(key, part):
    key = jax.random.fold_in(key, 12)
    devices = PACK // TOK_DEV
    rounds = TOK_DEV // BLK
    choosing = jax.vmap(shuffle_round)(jax.random.split(key, PACKS * rounds))
    slot_blocks = choosing.reshape(PACKS, rounds, devices).transpose(0, 2, 1)
    starts = (jnp.arange(rounds)[None, None, :] * devices + slot_blocks) * BLK
    return (starts[:, :, :, None] + jnp.arange(BLK)[None, None, None, :]).reshape(PACKS, PACK).astype(jnp.int32)


def draw_in_proj(key, part):
    key = jax.random.fold_in(key, 13)
    entry_key, head_key = jax.random.split(key)
    entries = jnp.clip(jax.random.normal(entry_key, (6, D, D), jnp.float32), -6.0, 6.0)
    head_scale = jnp.exp(jax.random.uniform(head_key, (H,), jnp.float32, 0.0, 1.0986123))
    columns = jnp.repeat(head_scale, HEAD)
    layers = jnp.concatenate([columns[None], jnp.ones((5, D), jnp.float32)], axis=0)
    return entries * layers[:, None, :] * D ** (-0.5)


def draw_vectors(key, part):
    key = jax.random.fold_in(key, 14)
    noise = jnp.clip(jax.random.normal(key, (9, D), jnp.float32), -5.0, 5.0)
    rows_index = jnp.arange(9)
    is_gain = (rows_index >= 3) & (rows_index % 2 == 1)
    return jnp.where(is_gain[:, None], 1.0 + 0.1 * noise, 0.3 * noise)


def steps_of(own_key, extent, cuts, low, largest):
    gain = 1.0
    for position, blocks in cuts:
        heights = jax.random.uniform(jax.random.fold_in(jax.random.fold_in(own_key, 6), position), (blocks,), jnp.float32, low / len(cuts), largest / len(cuts))
        gain = gain * jnp.repeat(jnp.exp(heights), extent[position] // blocks).reshape((-1,) + (1,) * (len(extent) - 1 - position))
    return gain


def normal_values(stream_key, dims, deviation, reach, shards=(), held_as=jnp.bfloat16):
    values = jax.random.normal(stream_key, dims, jnp.float32) * deviation
    if len(shards) > 0:
        values = steps_of(stream_key, dims, shards, -0.22, 0.18) * values
    return jnp.clip(values, min=-reach, max=reach).astype(held_as)


def setup_inputs(seed: int = 0) -> dict:
    key_of = jax.random.split(jax.random.key(seed), 27)
    return {
        "tokens": normal_values(key_of[0], (TOKENS, D), 1.0, 6.0, ((0, 8),)),
        "encoder": normal_values(key_of[1], (ENC_ROWS, D), 1.0, 6.0, ((0, 8),)),
        "cotangent": normal_values(key_of[2], (TOKENS, D), 1.0, 6.0, ((0, 8),)),
        "lengths": draw_lengths(jax.random.fold_in(key_of[26], 71), 0),
        "order": draw_order(jax.random.fold_in(key_of[26], 71), 0),
        "in_proj": draw_in_proj(jax.random.fold_in(key_of[26], 71), 0),
        "out_proj": normal_values(key_of[6], (2, D, D), (D // 64) ** -0.5, 1.5, ((1, 4), (2, 8)), jnp.float32),
        "w_up": normal_values(key_of[7], (D, FF), D ** -0.5, 0.1875, ((0, 8), (1, 4)), jnp.float32),
        "w_down": normal_values(key_of[8], (FF, D), FF ** -0.5, 0.09375, ((0, 4), (1, 8)), jnp.float32),
        "head_bias": normal_values(key_of[9], (4, D // SHARDS, SHARDS), 0.3, 4.0, ((1, 4), (2, 8)), jnp.float32),
        "up_bias": normal_values(key_of[10], (FF // SHARDS, SHARDS), 0.3, 4.0, ((0, 4), (1, 8)), jnp.float32),
        "vectors": draw_vectors(jax.random.fold_in(key_of[26], 71), 0),
        "in_first": normal_values(key_of[12], (6, D, D), (0.5 * TOKENS ** 0.5), 256.0, ((1, 8), (2, 4)), jnp.float32),
        "out_first": normal_values(key_of[13], (2, D, D), (0.15 * TOKENS ** 0.5), 80.0, ((1, 4), (2, 8)), jnp.float32),
        "up_first": normal_values(key_of[14], (D, FF), (0.4 * TOKENS ** 0.5), 224.0, ((0, 8), (1, 4)), jnp.float32),
        "down_first": normal_values(key_of[15], (FF, D), (0.5 * TOKENS ** 0.5), 256.0, ((0, 4), (1, 8)), jnp.float32),
        "hbias_first": normal_values(key_of[16], (4, D // SHARDS, SHARDS), (1.0 * TOKENS ** 0.5), 512.0, ((1, 4), (2, 8)), jnp.float32),
        "ubias_first": normal_values(key_of[17], (FF // SHARDS, SHARDS), (0.4 * TOKENS ** 0.5), 224.0, ((0, 4), (1, 8)), jnp.float32),
        "vec_first": normal_values(key_of[18], (9, D), (0.7 * TOKENS ** 0.5), 384.0, ((1, 8),), jnp.float32),
        "in_second": jnp.clip(jnp.exp(math.log(8192.0) - 2.0794415 * jax.random.uniform(key_of[19], (6, D, D), jnp.float32) ** steps_of(key_of[19], (6, D, D), ((1, 8), (2, 4)), -0.2, 0.2)), 1024.0, 8192.0),
        "out_second": jnp.clip(jnp.exp(math.log(737.28) - 2.0794415 * jax.random.uniform(key_of[20], (2, D, D), jnp.float32) ** steps_of(key_of[20], (2, D, D), ((1, 4), (2, 8)), -0.2, 0.2)), 92.16, 737.28),
        "up_second": jnp.clip(jnp.exp(math.log(5242.88) - 2.0794415 * jax.random.uniform(key_of[21], (D, FF), jnp.float32) ** steps_of(key_of[21], (D, FF), ((0, 8), (1, 4)), -0.2, 0.2)), 655.36, 5242.88),
        "down_second": jnp.clip(jnp.exp(math.log(8192.0) - 2.0794415 * jax.random.uniform(key_of[22], (FF, D), jnp.float32) ** steps_of(key_of[22], (FF, D), ((0, 4), (1, 8)), -0.2, 0.2)), 1024.0, 8192.0),
        "hbias_second": jnp.clip(jnp.exp(math.log(32768.0) - 2.0794415 * jax.random.uniform(key_of[23], (4, D // SHARDS, SHARDS), jnp.float32) ** steps_of(key_of[23], (4, D // SHARDS, SHARDS), ((1, 4), (2, 8)), -0.2, 0.2)), 4096.0, 32768.0),
        "ubias_second": jnp.clip(jnp.exp(math.log(5242.88) - 2.0794415 * jax.random.uniform(key_of[24], (FF // SHARDS, SHARDS), jnp.float32) ** steps_of(key_of[24], (FF // SHARDS, SHARDS), ((0, 4), (1, 8)), -0.2, 0.2)), 655.36, 5242.88),
        "vec_second": jnp.clip(jnp.exp(math.log(16056.32) - 2.0794415 * jax.random.uniform(key_of[25], (9, D), jnp.float32) ** steps_of(key_of[25], (9, D), ((1, 8),), -0.2, 0.2)), 2007.04, 16056.32),
    }


@jax.custom_vjp
def low(v):
    return lax.optimization_barrier(v.astype(jnp.bfloat16)).astype(jnp.float32)

@jax.custom_vjp
def low_back(v):
    return v

def low_keep(v):
    return (low(v), None)

def low_pass(kept, grad):
    return (grad,)

def back_keep(v):
    return (v, None)

def back_low(kept, grad):
    return (low(grad),)
low.defvjp(low_keep, low_pass)
low_back.defvjp(back_keep, back_low)
NEGATIVE = -1e+30
NORM_EPS = 1e-05
ADAM_EPS = 1e-08
BETA = 0.5
CLIP_LIMIT = 10.0
RATES = (0.05, 0.3, 0.05, 0.03, 0.3, 0.3, 0.3)
DECAYS = (0.1, 0.1, 0.1, 0.1, 0.0, 0.0, 0.0)

def highest_dot(left_side, right_side):
    return jnp.dot(left_side, right_side, precision=lax.Precision.HIGHEST)

def grouped_sum(left_side, right_side, groups):
    rows_left = left_side.shape[0]
    inner_width = left_side.shape[1] // groups
    pieces = left_side.reshape(rows_left, groups, inner_width).transpose(1, 0, 2)
    blocks = right_side.reshape(groups, inner_width, right_side.shape[1])
    partials = jnp.einsum('grk,gkd->grd', pieces, blocks, precision=lax.Precision.HIGHEST)
    return lax.optimization_barrier(jnp.sum(low(partials), axis=0))

def normalize(hidden, gain_row, shift_row):
    centred = hidden - lax.optimization_barrier(jnp.mean(hidden, axis=-1, keepdims=True))
    factor = lax.rsqrt(lax.optimization_barrier(jnp.mean(centred * centred, axis=-1, keepdims=True)) + NORM_EPS)
    return centred * factor * gain_row + shift_row

def split_heads(matrix):
    return matrix.reshape(matrix.shape[0], H, HEAD).transpose(1, 0, 2)

def attention(queries, keys, values, allowed):

    def one_head(packed):
        head_queries, head_keys, head_values = packed
        scores = low_back(highest_dot(head_queries, head_keys.T) * HEAD ** (-0.5))
        masked = jnp.where(allowed, scores, NEGATIVE)
        peak = lax.optimization_barrier(jnp.max(masked, axis=1, keepdims=True))
        weights = jnp.where(allowed, jnp.exp(masked - peak), 0.0)
        probs = weights / lax.optimization_barrier(jnp.sum(weights, axis=1, keepdims=True))
        return (highest_dot(low(probs), head_values), jnp.max(masked))
    outputs, tops = lax.map(jax.checkpoint(one_head), (split_heads(queries), split_heads(keys), split_heads(values)))
    return (outputs.transpose(1, 0, 2).reshape(queries.shape[0], H * HEAD), tops)

def decoder_layer(params, tokens_in, encoder_in, self_allowed, cross_allowed):
    w_in, w_out, w_one, w_two, bias_heads, bias_up, vec_all = [low(param) for param in params]
    bias_heads = bias_heads.reshape(4, D)
    bias_up = bias_up.reshape(FF)
    queries = low_back(low(highest_dot(tokens_in, w_in[0]) + bias_heads[0]))
    self_keys = low_back(low(highest_dot(tokens_in, w_in[1])))
    self_values = low_back(low(highest_dot(tokens_in, w_in[2]) + bias_heads[1]))
    context, tops = attention(queries, self_keys, self_values, self_allowed)
    context = low_back(low(context))
    hidden_one = tokens_in + low_back(grouped_sum(context, w_out[0], N_TENSOR)) + vec_all[0]
    normed_one = normalize(hidden_one, vec_all[3], vec_all[4])
    low_one = low(normed_one)
    cross_queries = low_back(low(highest_dot(low_one, w_in[3]) + bias_heads[2]))
    cross_keys = low_back(low(highest_dot(encoder_in, w_in[4])))
    cross_values = low_back(low(highest_dot(encoder_in, w_in[5]) + bias_heads[3]))
    cross_context, cross_tops = attention(cross_queries, cross_keys, cross_values, cross_allowed)
    cross_context = low_back(low(cross_context))
    hidden_two = normed_one + low_back(grouped_sum(cross_context, w_out[1], N_TENSOR)) + vec_all[1]
    normed_two = normalize(hidden_two, vec_all[5], vec_all[6])
    upward = low_back(highest_dot(low(normed_two), w_one) + bias_up)
    activated = low_back(low(jax.nn.gelu(upward, approximate=False)))
    hidden_three = normed_two + low_back(grouped_sum(activated, w_two, N_TENSOR)) + vec_all[2]
    return (normalize(hidden_three, vec_all[7], vec_all[8]), tops)

def adamw_step(master, gradient, first_moment, second_moment, step_rate, weight_decay):
    first_moment = BETA * first_moment + (1.0 - BETA) * gradient
    second_moment = BETA * second_moment + (1.0 - BETA) * gradient * gradient
    correction = 1.0 - BETA ** STEP
    update = first_moment / correction / (jnp.sqrt(second_moment / correction) + ADAM_EPS)
    return (master - step_rate * (update + weight_decay * master), first_moment, second_moment)

def reference(tokens, encoder, cotangent, lengths, order, in_proj, out_proj, w_up, w_down, head_bias, up_bias, vectors, in_first, out_first, up_first, down_first, hbias_first, ubias_first, vec_first, in_second, out_second, up_second, down_second, hbias_second, ubias_second, vec_second):
    masters = (in_proj, out_proj, w_up, w_down, head_bias, up_bias, vectors)
    firsts = (in_first, out_first, up_first, down_first, hbias_first, ubias_first, vec_first)
    seconds = (in_second, out_second, up_second, down_second, hbias_second, ubias_second, vec_second)
    positions = jnp.arange(PACK).astype(jnp.int32)
    enc_sequence = (jnp.arange(NSEQ * ENC) // ENC).astype(jnp.int32)

    def per_pack(running, packed):
        grads_sum, top_sum = running
        pack_tokens, pack_encoder, pack_cot, pack_lengths, pack_order = packed
        inverse = jnp.zeros((PACK,), jnp.int32).at[pack_order].set(positions)
        ordered = pack_tokens.astype(jnp.float32)[inverse]
        starts = jnp.cumsum(pack_lengths) - pack_lengths
        segment = lax.optimization_barrier(jnp.sum((positions[:, None] >= starts[None, 1:]).astype(jnp.int32), axis=1))
        self_allowed = (segment[:, None] == segment[None, :]) & (positions[None, :] <= positions[:, None])
        cross_allowed = segment[:, None] == enc_sequence[None, :]

        def forward(params, tokens_in, encoder_in):
            return decoder_layer(params, tokens_in, encoder_in, self_allowed, cross_allowed)
        result, backward, tops = jax.vjp(forward, masters, ordered, pack_encoder.astype(jnp.float32), has_aux=True)
        grad_params, grad_ordered, grad_encoder = backward(pack_cot.astype(jnp.float32))
        grads_sum = jax.tree.map(jnp.add, grads_sum, grad_params)
        return ((grads_sum, jnp.maximum(top_sum, tops)), (result, grad_ordered[pack_order], grad_encoder))
    initial = (jax.tree.map(jnp.zeros_like, masters), jnp.full((H,), NEGATIVE, jnp.float32))
    stacked = (tokens.reshape(PACKS, PACK, D), encoder.reshape(PACKS, NSEQ * ENC, D), cotangent.reshape(PACKS, PACK, D), lengths, order)
    (grads_total, top_all), (outputs, grad_tokens, grad_encoder) = lax.scan(per_pack, initial, stacked)
    clip_factor = CLIP_LIMIT / jnp.maximum(top_all, CLIP_LIMIT)
    column_roots = jnp.repeat(jnp.sqrt(clip_factor), HEAD)
    unit_rows = jnp.ones((4, D), jnp.float32)
    in_scale = jnp.concatenate([column_roots[None], column_roots[None], unit_rows], axis=0)[:, None, :]
    bias_scale = jnp.concatenate([column_roots[None], unit_rows[:3]], axis=0).reshape(4, D // SHARDS, SHARDS)
    scale_list = (in_scale, 1.0, 1.0, 1.0, bias_scale, 1.0, 1.0)
    results = [outputs.reshape(TOKENS, D), grad_tokens.reshape(TOKENS, D), grad_encoder.reshape(ENC_ROWS, D), clip_factor]
    for param_index in range(7):
        new_master, new_first, new_second = adamw_step(masters[param_index], grads_total[param_index], firsts[param_index], seconds[param_index], RATES[param_index], DECAYS[param_index])
        new_master = new_master * scale_list[param_index]
        results += [new_master, new_first, new_second, new_master.astype(jnp.bfloat16)]
    return tuple(results)
```

```python
from functools import partial, reduce

import jax
import jax.numpy as jnp
from jax import lax
from jax.experimental import pallas as pl
from jax.experimental.pallas import tpu as pltpu
from jax.sharding import PartitionSpec as P

HEAD = 64
ENC = 4096
STEP = 10
BLK = 128

NEGATIVE = -1e30
NORM_EPS = 1e-05
ADAM_EPS = 1e-08
BETA = 0.5
CLIP_LIMIT = 10.0
RATES = (0.05, 0.3, 0.05, 0.03, 0.3, 0.3, 0.3)
DECAYS = (0.1, 0.1, 0.1, 0.1, 0.0, 0.0, 0.0)
SCALE = HEAD ** (-0.5)
VMEM_BYTES = 56 * 1024 * 1024
F, C, T = "fsdp", "context", "tensor"
SHARD = (F, C)
NO_COST = pl.CostEstimate(flops=0, bytes_accessed=0, transcendentals=0)


def product(left_side, right_side):
    return jnp.dot(left_side, right_side, preferred_element_type=jnp.float32)


def contract_rows(left_side, right_side):
    return lax.dot_general(
        left_side, right_side, (((0,), (0,)), ((), ())), preferred_element_type=jnp.float32
    )


def contract_cols(left_side, right_side):
    return lax.dot_general(
        left_side, right_side, (((1,), (1,)), ((), ())), preferred_element_type=jnp.float32
    )


def stack_heads(block, heads):
    lanes = lax.broadcasted_iota(jnp.int32, block.shape, 1) // HEAD
    zero = jnp.zeros_like(block)
    return jnp.concatenate([jnp.where(lanes == h, block, zero) for h in range(heads)], axis=0)


def merge_heads(stacked, heads):
    rows = stacked.shape[0] // heads
    lanes = lax.broadcasted_iota(jnp.int32, (rows, stacked.shape[1]), 1) // HEAD
    merged = stacked[:rows]
    for h in range(1, heads):
        merged = jnp.where(lanes == h, stacked[h * rows : (h + 1) * rows], merged)
    return merged


def col_to_row(column):
    return jnp.transpose(jnp.broadcast_to(column, (column.shape[0], 128)))[0:1]


def fold_lanes(tile, combine):
    return reduce(combine, [tile[:, j : j + 128] for j in range(0, tile.shape[1], 128)])


def whole(shape):
    return pl.BlockSpec(shape, lambda i, s: (0,) * len(shape), pipeline_mode=pl.Buffered(1))


def fetch_kv(sources, places, sems):
    copies = [
        pltpu.make_async_copy(source, place, sems.at[i])
        for i, (source, place) in enumerate(zip(sources, places))
    ]

    @pl.when(pl.program_id(0) == 0)
    def _():
        for copy in copies:
            copy.start()
        for copy in copies:
            copy.wait()


def piece_bounds(pieces):
    full, half = pieces[0].shape[0], pieces[3].shape[0]
    return [(0, 0, full), (1, 0, full), (2, 0, full), (3, 0, half), (3, half, half)]


def member_rows(order_ref, row, bounds, full):
    return [
        pl.ds(pl.multiple_of(order_ref[row, j] * full + start, size), size)
        for j, start, size in bounds
    ]


def gate_body(*refs):
    pass


def after(values, others):
    count, every = len(values), [*values, *others]
    return pl.pallas_call(
        gate_body,
        in_specs=[pl.BlockSpec(memory_space=pl.ANY)] * len(every),
        out_specs=[pl.BlockSpec(memory_space=pl.ANY)] * count,
        out_shape=[jax.ShapeDtypeStruct(value.shape, value.dtype) for value in values],
        input_output_aliases={i: i for i in range(count)},
        cost_estimate=NO_COST,
        name="gate",
    )(*every)


def cross_fwd_body(heads, bounds, seg_ref, q_ref, *refs):
    sources, (o_ref, lse_ref, kv_ref, s_ref, sems) = refs[: len(bounds)], refs[len(bounds) :]
    places = member_rows(seg_ref, 3, bounds, sources[0].shape[0])
    fetch_kv(sources, [kv_ref.at[place] for place in places], sems)
    block = pl.program_id(0)
    low, high, cut = seg_ref[0, block], seg_ref[1, block], seg_ref[2, block]
    queries = stack_heads(q_ref[...] * jnp.bfloat16(SCALE), heads)
    rows, width = queries.shape
    tiles, _, step = s_ref.shape

    def attend(sequence):
        def scores(t, highest):
            at = pl.ds(pl.multiple_of(sequence * ENC + t * step, step), step)
            tile = contract_cols(queries, kv_ref[at, :width])
            s_ref[t] = tile
            return jnp.maximum(highest, fold_lanes(tile, jnp.maximum))

        highest = lax.fori_loop(0, tiles, scores, jnp.full((rows, 128), NEGATIVE, jnp.float32))
        peak = jnp.max(highest, axis=1, keepdims=True)

        def weigh(t, running):
            total, summed = running
            at = pl.ds(pl.multiple_of(sequence * ENC + t * step, step), step)
            weights = jnp.exp(s_ref[t] - peak)
            summed = summed + product(weights.astype(jnp.bfloat16), kv_ref[at, width:])
            return total + fold_lanes(weights, jnp.add), summed

        total, summed = lax.fori_loop(
            0,
            tiles,
            weigh,
            (jnp.zeros((rows, 128), jnp.float32), jnp.zeros((rows, width), jnp.float32)),
        )
        total = jnp.sum(total, axis=1, keepdims=True)
        merged = merge_heads(summed / total, heads)
        lse = col_to_row(peak + jnp.log(total))
        place = lax.broadcasted_iota(jnp.int32, merged.shape, 0)
        own = jnp.where(place >= cut, 1, 0) == sequence
        o_ref[...] = jnp.where(own, merged, o_ref[...].astype(jnp.float32)).astype(o_ref.dtype)
        place = lax.broadcasted_iota(jnp.int32, lse.shape, 1) % BLK
        own = jnp.where(place >= cut, 1, 0) == sequence
        lse_ref[0] = jnp.where(own, lse, lse_ref[0])

    o_ref[...] = jnp.zeros_like(o_ref)
    lse_ref[...] = jnp.zeros_like(lse_ref)
    pl.loop(low, high + 1)(attend)


def cross_fwd(queries, enc_kv, seg):
    count, width = queries.shape
    heads, blocks, step = width // HEAD, count // BLK, 1024
    rows, bounds = heads * BLK, piece_bounds(enc_kv)
    enc_all = sum(piece.shape[0] for piece in enc_kv)
    return pl.pallas_call(
        partial(cross_fwd_body, heads, bounds),
        grid_spec=pltpu.PrefetchScalarGridSpec(
            num_scalar_prefetch=1,
            grid=(blocks,),
            in_specs=[pl.BlockSpec((BLK, width), lambda i, s: (i, 0))]
            + [pl.BlockSpec(memory_space=pl.ANY)] * len(bounds),
            out_specs=[
                pl.BlockSpec((BLK, width), lambda i, s: (i, 0)),
                pl.BlockSpec((1, 1, rows), lambda i, s: (i, 0, 0)),
            ],
            scratch_shapes=[
                pltpu.VMEM((enc_all, 2 * width), jnp.bfloat16),
                pltpu.VMEM((ENC // step, rows, step), jnp.float32),
                pltpu.SemaphoreType.DMA((len(bounds),)),
            ],
        ),
        out_shape=[
            jax.ShapeDtypeStruct((count, width), jnp.bfloat16),
            jax.ShapeDtypeStruct((blocks, 1, rows), jnp.float32),
        ],
        compiler_params=pltpu.CompilerParams(vmem_limit_bytes=VMEM_BYTES),
        cost_estimate=NO_COST,
        name="cross_fwd",
    )(seg, queries, *enc_kv)


def cross_bwd_body(heads, bounds, waits, step, seg_ref, q_ref, g_ref, o_ref, lse_ref, *refs):
    count = len(bounds)
    sources, (dq_ref, *outs) = refs[:count], refs[count + waits : 2 * count + waits + 1]
    kv_ref, acc_ref, sems = refs[2 * count + waits + 1 :]
    places = member_rows(seg_ref, 3, bounds, sources[0].shape[0])
    fetch_kv(sources, [kv_ref.at[place] for place in places], sems)
    block = pl.program_id(0)

    @pl.when(block == 0)
    def _():
        acc_ref[...] = jnp.zeros_like(acc_ref)

    low, high, cut = seg_ref[0, block], seg_ref[1, block], seg_ref[2, block]
    queries = stack_heads(q_ref[...] * jnp.bfloat16(SCALE), heads)
    rows, width = queries.shape
    grads = stack_heads(g_ref[...], heads)
    dots = g_ref[...].astype(jnp.float32) * o_ref[...].astype(jnp.float32)
    dot_row = col_to_row(jnp.sum(stack_heads(dots, heads), axis=1, keepdims=True))
    all_lse = lse_ref[0]
    place = lax.broadcasted_iota(jnp.int32, all_lse.shape, 1) % BLK
    own_seq = jnp.where(place >= cut, 1, 0)

    def sequence_terms(sequence, q_grad):
        lse = jnp.where(own_seq == sequence, all_lse, -NEGATIVE)

        def tile_terms(t, q_grad):
            at = pl.ds(pl.multiple_of(sequence * ENC + t * step, step), step)
            keys, values = kv_ref[at, :width], kv_ref[at, width:]
            probs = jnp.exp(contract_cols(keys, queries) - lse)
            s_grad = (probs * (contract_cols(values, grads) - dot_row)).astype(jnp.bfloat16)
            acc_ref[at, width:] += product(probs.astype(jnp.bfloat16), grads)
            acc_ref[at, :width] += product(s_grad, queries)
            return q_grad + contract_rows(s_grad, keys)

        return lax.fori_loop(0, ENC // step, tile_terms, q_grad)

    q_grad = lax.fori_loop(low, high + 1, sequence_terms, jnp.zeros((rows, width), jnp.float32))
    dq_ref[...] = (merge_heads(q_grad, heads) * SCALE).astype(dq_ref.dtype)

    @pl.when(block == pl.num_programs(0) - 1)
    def _():
        for out, place in zip(outs, places):
            out[...] = acc_ref[place, :].astype(out.dtype)


def cross_bwd(queries, enc_kv, seg, grads, context, lse, others):
    count, width = queries.shape
    heads, blocks, step = width // HEAD, count // BLK, 512
    rows, bounds = heads * BLK, piece_bounds(enc_kv)
    enc_all = sum(piece.shape[0] for piece in enc_kv)
    row = pl.BlockSpec((BLK, width), lambda i, s: (i, 0))
    return pl.pallas_call(
        partial(cross_bwd_body, heads, bounds, len(others), step),
        grid_spec=pltpu.PrefetchScalarGridSpec(
            num_scalar_prefetch=1,
            grid=(blocks,),
            in_specs=[row, row, row, pl.BlockSpec((1, 1, rows), lambda i, s: (i, 0, 0))]
            + [pl.BlockSpec(memory_space=pl.ANY)] * (len(bounds) + len(others)),
            out_specs=[row] + [whole(piece.shape) for piece in enc_kv],
            scratch_shapes=[
                pltpu.VMEM((enc_all, 2 * width), jnp.bfloat16),
                pltpu.VMEM((enc_all, 2 * width), jnp.float32),
                pltpu.SemaphoreType.DMA((len(bounds),)),
            ],
        ),
        out_shape=[jax.ShapeDtypeStruct((count, width), jnp.bfloat16)]
        + [jax.ShapeDtypeStruct(piece.shape, jnp.bfloat16) for piece in enc_kv],
        compiler_params=pltpu.CompilerParams(vmem_limit_bytes=VMEM_BYTES),
        cost_estimate=NO_COST,
        name="cross_bwd",
    )(seg, queries, grads, context, lse, *enc_kv, *others)


def gather_tile(kv_ref, t, columns):
    at = pl.ds(pl.multiple_of(t * BLK, BLK), BLK)
    return jnp.concatenate([kv_ref[j, at, columns] for j in range(kv_ref.shape[0])], axis=0)


def self_fwd_body(heads, bounds, meta_ref, q_ref, *refs):
    sources, (o_ref, lse_ref, top_ref, kv_refs, sems) = refs[: len(bounds)], refs[len(bounds) :]
    fetch_kv(sources, [kv_refs.at[j, pl.ds(at, size)] for j, at, size in bounds], sems)
    groups = kv_refs.shape[0]
    block = pl.program_id(0)
    base, first, last = [meta_ref[groups + k, block] for k in range(3)]
    cut = meta_ref[groups + 3, 0]
    queries = stack_heads(q_ref[...] * jnp.bfloat16(SCALE), heads)
    rows, width = queries.shape
    q_pos = base + lax.broadcasted_iota(jnp.int32, (rows, BLK), 0) % BLK
    q_start = jnp.where(q_pos >= cut, cut, 0)
    lane = lax.broadcasted_iota(jnp.int32, (rows, BLK), 1)

    def visit(t, running):
        peak, total, summed = running
        raw = contract_cols(queries, gather_tile(kv_refs, t, slice(0, width)))
        parts = []
        for d in range(groups):
            k_pos = lane + meta_ref[d, t]
            seen = (k_pos <= q_pos) & (k_pos >= q_start)
            parts.append(jnp.where(seen, raw[:, d * BLK : (d + 1) * BLK], NEGATIVE))
        new_peak = jnp.maximum(peak, jnp.max(reduce(jnp.maximum, parts), axis=1, keepdims=True))
        weights = [jnp.exp(part - new_peak) for part in parts]
        shrink = jnp.exp(peak - new_peak)
        total = total * shrink + jnp.sum(reduce(jnp.add, weights), axis=1, keepdims=True)
        low_weights = jnp.concatenate(weights, axis=1).astype(jnp.bfloat16)
        values = gather_tile(kv_refs, t, slice(width, 2 * width))
        return new_peak, total, summed * shrink + product(low_weights, values)

    peak, total, summed = lax.fori_loop(
        first,
        last + 1,
        visit,
        (
            jnp.full((rows, 1), NEGATIVE, jnp.float32),
            jnp.zeros((rows, 1), jnp.float32),
            jnp.zeros((rows, width), jnp.float32),
        ),
    )
    o_ref[...] = merge_heads(summed / total, heads).astype(o_ref.dtype)
    lse_ref[0] = col_to_row(peak + jnp.log(total))
    top_ref[0] = col_to_row(peak)


def self_fwd(queries, kv, meta):
    count, width = queries.shape
    heads, blocks, bounds = width // HEAD, count // BLK, piece_bounds(kv)
    rows, kept = heads * BLK, (bounds[-1][0] + 1,) + kv[0].shape
    row = pl.BlockSpec((BLK, width), lambda i, s: (i, 0))
    stat = pl.BlockSpec((1, 1, rows), lambda i, s: (i, 0, 0))
    return pl.pallas_call(
        partial(self_fwd_body, heads, bounds),
        grid_spec=pltpu.PrefetchScalarGridSpec(
            num_scalar_prefetch=1,
            grid=(blocks,),
            in_specs=[row] + [pl.BlockSpec(memory_space=pl.ANY)] * len(bounds),
            out_specs=[row, stat, stat],
            scratch_shapes=[
                pltpu.VMEM(kept, jnp.bfloat16),
                pltpu.SemaphoreType.DMA((len(bounds),)),
            ],
        ),
        out_shape=[jax.ShapeDtypeStruct((count, width), jnp.bfloat16)]
        + [jax.ShapeDtypeStruct((blocks, 1, rows), jnp.float32)] * 2,
        compiler_params=pltpu.CompilerParams(vmem_limit_bytes=VMEM_BYTES),
        cost_estimate=NO_COST,
        name="self_fwd",
    )(meta, queries, *kv)


def self_bwd_body(heads, bounds, waits, meta_ref, q_ref, g_ref, o_ref, lse_ref, *refs):
    count = len(bounds)
    sources, (dq_ref, *outs) = refs[:count], refs[count + waits : 2 * count + waits + 1]
    kv_refs, acc_ref, sems = refs[2 * count + waits + 1 :]
    fetch_kv(sources, [kv_refs.at[j, pl.ds(at, size)] for j, at, size in bounds], sems)
    groups = kv_refs.shape[0]
    block = pl.program_id(0)

    @pl.when(block == 0)
    def _():
        acc_ref[...] = jnp.zeros_like(acc_ref)

    base, first, last = [meta_ref[groups + k, block] for k in range(3)]
    cut = meta_ref[groups + 3, 0]
    queries = stack_heads(q_ref[...] * jnp.bfloat16(SCALE), heads)
    rows, width = queries.shape
    grads = stack_heads(g_ref[...], heads)
    dots = g_ref[...].astype(jnp.float32) * o_ref[...].astype(jnp.float32)
    dot_row = col_to_row(jnp.sum(stack_heads(dots, heads), axis=1, keepdims=True))
    lse = lse_ref[0]
    q_pos = base + lax.broadcasted_iota(jnp.int32, lse.shape, 1) % BLK
    q_start = jnp.where(q_pos >= cut, cut, 0)
    sub = lax.broadcasted_iota(jnp.int32, (BLK, rows), 0)

    def tile_terms(t, q_grad):
        at = pl.ds(pl.multiple_of(t * BLK, BLK), BLK)
        keys = gather_tile(kv_refs, t, slice(0, width))
        values = gather_tile(kv_refs, t, slice(width, 2 * width))
        raw = contract_cols(keys, queries)
        parts = []
        for d in range(groups):
            k_base = meta_ref[d, t]
            seen = (sub <= q_pos - k_base) & (sub >= q_start - k_base)
            parts.append(jnp.where(seen, jnp.exp(raw[d * BLK : (d + 1) * BLK] - lse), 0.0))
        probs = jnp.concatenate(parts, axis=0)
        s_grad = (probs * (contract_cols(values, grads) - dot_row)).astype(jnp.bfloat16)
        acc_ref[:, at, width:] += product(probs.astype(jnp.bfloat16), grads).reshape(
            groups, BLK, width
        )
        acc_ref[:, at, :width] += product(s_grad, queries).reshape(groups, BLK, width)
        return q_grad + contract_rows(s_grad, keys)

    q_grad = lax.fori_loop(first, last + 1, tile_terms, jnp.zeros((rows, width), jnp.float32))
    dq_ref[...] = (merge_heads(q_grad, heads) * SCALE).astype(dq_ref.dtype)

    @pl.when(block == pl.num_programs(0) - 1)
    def _():
        for out, (j, at, size) in zip(outs, bounds):
            out[...] = acc_ref[j, at : at + size].astype(out.dtype)


def self_bwd(queries, kv, meta, grads, context, lse, others):
    count, width = queries.shape
    heads, blocks, bounds = width // HEAD, count // BLK, piece_bounds(kv)
    rows, kept = heads * BLK, (bounds[-1][0] + 1,) + kv[0].shape
    row = pl.BlockSpec((BLK, width), lambda i, s: (i, 0))
    stat = pl.BlockSpec((1, 1, rows), lambda i, s: (i, 0, 0))
    return pl.pallas_call(
        partial(self_bwd_body, heads, bounds, len(others)),
        grid_spec=pltpu.PrefetchScalarGridSpec(
            num_scalar_prefetch=1,
            grid=(blocks,),
            in_specs=[row, row, row, stat]
            + [pl.BlockSpec(memory_space=pl.ANY)] * (len(bounds) + len(others)),
            out_specs=[row] + [whole(piece.shape) for piece in kv],
            scratch_shapes=[
                pltpu.VMEM(kept, jnp.bfloat16),
                pltpu.VMEM(kept, jnp.float32),
                pltpu.SemaphoreType.DMA((len(bounds),)),
            ],
        ),
        out_shape=[jax.ShapeDtypeStruct((count, width), jnp.bfloat16)]
        + [jax.ShapeDtypeStruct(piece.shape, jnp.bfloat16) for piece in kv],
        compiler_params=pltpu.CompilerParams(vmem_limit_bytes=VMEM_BYTES),
        cost_estimate=NO_COST,
        name="self_bwd",
    )(meta, queries, grads, context, lse, *kv, *others)


def move_body(index_ref, in_ref, out_ref):
    out_ref[...] = in_ref[...].astype(out_ref.dtype)


def put_blocks(rows, index, dtype):
    count, width = rows.shape
    return pl.pallas_call(
        move_body,
        grid_spec=pltpu.PrefetchScalarGridSpec(
            num_scalar_prefetch=1,
            grid=(count // BLK,),
            in_specs=[pl.BlockSpec((BLK, width), lambda i, s: (i, 0))],
            out_specs=pl.BlockSpec((BLK, width), lambda i, s: (s[i], 0)),
        ),
        out_shape=jax.ShapeDtypeStruct((count, width), dtype),
        cost_estimate=NO_COST,
        name="put_blocks",
    )(index, rows)


def normalize(hidden, gain_row, shift_row):
    centred = hidden - jnp.mean(hidden, axis=-1, keepdims=True)
    factor = lax.rsqrt(jnp.mean(centred * centred, axis=-1, keepdims=True) + NORM_EPS)
    unit_rows = centred * factor
    return (unit_rows * gain_row + shift_row, unit_rows, factor)


def normalize_back(incoming, unit_rows, factor, gain_row):
    scaled = incoming * gain_row
    centred_grad = (
        scaled
        - jnp.mean(scaled, axis=-1, keepdims=True)
        - unit_rows * jnp.mean(scaled * unit_rows, axis=-1, keepdims=True)
    )
    return (factor * centred_grad, jnp.sum(incoming * unit_rows, axis=0), jnp.sum(incoming, axis=0))


def adamw_step(master, gradient, first_moment, second_moment, step_rate, weight_decay):
    first_moment = BETA * first_moment + (1.0 - BETA) * gradient
    second_moment = BETA * second_moment + (1.0 - BETA) * gradient * gradient
    correction = 1.0 - BETA**STEP
    update = first_moment / correction / (jnp.sqrt(second_moment / correction) + ADAM_EPS)
    return (master - step_rate * (update + weight_decay * master), first_moment, second_moment)
def swap(value, axis, j):
    return lax.ppermute(value, axis, [(i, i ^ j) for i in range(lax.axis_size(axis))])


def spread(blocks, axis):
    return [blocks[0]] + [swap(blocks[j], axis, j) for j in range(1, len(blocks))]


def total(blocks):
    return reduce(jnp.add, [block.astype(jnp.float32) for block in blocks])


def column_blocks(array, count):
    size = array.shape[1] // count
    return [array[:, j * size : (j + 1) * size] for j in range(count)]


def row_blocks(array, count):
    size = array.shape[0] // count
    return [array[j * size : (j + 1) * size] for j in range(count)]


def pick_rows(array, index, size):
    return lax.dynamic_slice_in_dim(array, index * size, size, 0)


def by_shard(flat, shard_rows):
    shards, used = flat.shape
    return jnp.pad(flat, ((0, 0), (0, shard_rows * 128 - used))).reshape(-1, 128)


def relay_gather(block, others=()):
    near, far = swap(block, C, 1), swap(block, C, 2)
    if others:
        near, far = after([near, far], others)
    half = block.shape[0] // 2
    return [block, near, far, swap(far[:half], C, 1), swap(near[half:], C, 2)]


def relay_start(terms):
    return swap(terms[3], C, 1), swap(terms[4], C, 2)


def relay_join(terms, passed):
    own, near, far = terms[:3]
    half, low = own.shape[0] // 2, own.dtype
    near = jnp.concatenate([near[:half], (total([near[half:], passed[1]])).astype(low)])
    far = jnp.concatenate([(total([far[:half], passed[0]])).astype(low), far[half:]])
    return own, near, far


def relay_finish(joined):
    own, near, far = joined
    return [own, swap(near, C, 1), swap(far, C, 2)]


def per_device(tokens, encoder, cotangent, lengths, order, *params):
    masters, firsts, seconds = params[:7], params[7:14], params[14:]
    in_proj, out_proj, w_up, w_down, head_bias, up_bias, vectors = masters
    low, wide = jnp.bfloat16, jnp.float32
    groups, member = lax.axis_size(C), lax.axis_index(C)
    depth, plane = lax.axis_size(T), lax.axis_index(T)
    shards, shard_index = lax.axis_size(SHARD), lax.axis_index(SHARD)
    row_count, model_width = tokens.shape
    head_width, hidden_width = in_proj.shape[2], w_up.shape[1]
    heads = head_width // HEAD
    shard_rows = in_proj.shape[1]
    rounds = row_count // BLK
    rows = row_count // depth
    per_slice, per_member = rows // BLK, rounds // groups
    all_heads, all_hidden = depth * head_width, depth * hidden_width

    n_vec, n_head, n_up = vectors.size, head_bias.size, up_bias.size
    small = jnp.concatenate([vectors.reshape(-1), head_bias.reshape(-1)])
    first_part = jnp.concatenate(
        [in_proj[0], in_proj[1], in_proj[2], by_shard(small[None], shard_rows)], axis=1
    )
    first_part = lax.all_gather(first_part.astype(low), SHARD, axis=0, tiled=True)
    biases = jnp.concatenate([head_bias[2].reshape(-1), up_bias.reshape(-1)])
    proj_pack = jnp.concatenate(
        [out_proj[0].T, out_proj[1].T, in_proj[3], by_shard(biases[None], shard_rows)], axis=1
    ).astype(low)
    ffn_pack = jnp.concatenate([w_up, w_down.T], axis=1).astype(low)

    def from_planes(array):
        return [array] + [swap(array, T, j) for j in range(1, depth)]

    proj_packs = from_planes(proj_pack)
    w_enc = jnp.concatenate([in_proj[4], in_proj[5]], axis=1).astype(low)
    (w_enc,) = after([w_enc], proj_packs[1:])
    w_enc = lax.all_gather(w_enc, SHARD, axis=0, tiled=True)
    w_self = first_part[:, : 3 * head_width]
    used = -(-(n_vec + n_head) // 128)
    small = first_part.reshape(shards, shard_rows, -1)[:, :used, 3 * head_width :]
    small = small.reshape(shards, -1)
    vec_all = small[:, :n_vec].reshape(shards, 9, -1).transpose(1, 0, 2).reshape(9, -1)
    vec_all = vec_all.astype(wide)

    def by_columns(flat, count):
        return flat.reshape(shards, count, -1).transpose(1, 2, 0).reshape(count, -1).astype(wide)

    bias_heads = by_columns(small[:, n_vec : n_vec + n_head], 4)

    bases = order[0].reshape(groups, rounds, BLK)[:, :, 0]
    cut = lengths[0, 0]
    near = member ^ jnp.arange(groups)
    spot = jnp.arange(rounds)
    q_rounds = (plane ^ (spot // per_slice)) * per_slice + spot % per_slice
    q_bases = jnp.take(lax.dynamic_index_in_dim(bases, member, 0, keepdims=False), q_rounds)
    seg = jnp.stack(
        [
            (q_bases >= cut).astype(jnp.int32),
            (q_bases + BLK - 1 >= cut).astype(jnp.int32),
            jnp.clip(cut - q_bases, 0, BLK),
            jnp.pad(near, (0, rounds - groups)),
        ]
    ).astype(jnp.int32)
    near_bases = jnp.take(bases, near, axis=0)
    meta = jnp.concatenate(
        [
            near_bases,
            q_bases[None],
            jnp.where(q_bases >= cut, cut // (groups * BLK), 0)[None],
            q_rounds[None],
            jnp.full((1, rounds), cut),
        ],
        axis=0,
    ).astype(jnp.int32)
    places = (
        lax.dynamic_slice_in_dim(near_bases, member * per_member, per_member, 1) // BLK
        - member * rounds
    ).reshape(-1)

    qkv = product(tokens, w_self)
    queries = (qkv[:, :head_width] + bias_heads[0]).astype(low)
    queries = jnp.concatenate([pick_rows(queries, plane ^ j, rows) for j in range(depth)])
    no_bias = jnp.zeros((head_width,), wide)
    kv = (qkv[:, head_width:] + jnp.concatenate([no_bias, bias_heads[1]])).astype(low)
    kv = relay_gather(kv)
    ffn_packs = from_planes(after([ffn_pack], kv[:1])[0])
    (w_enc,) = after([w_enc], kv[:1])
    enc_kv = product(encoder, w_enc) + jnp.concatenate([no_bias, bias_heads[3]])
    enc_kv = enc_kv.astype(low)

    def side_by_side(packs, bounds):
        return jnp.concatenate([pack[:, a:b] for a, b in bounds for pack in packs], axis=1)

    proj_bounds = [(i * head_width, (i + 1) * head_width) for i in range(3)]
    proj_bounds.append((3 * head_width, proj_pack.shape[1]))
    w_proj = side_by_side(proj_packs, proj_bounds)
    w_proj = lax.all_gather(w_proj, SHARD, axis=0, tiled=True)
    (enc_kv,) = after([enc_kv], kv[3:])
    ffn_packs = after(ffn_packs, kv[3:])
    w_one = side_by_side(ffn_packs, [(0, hidden_width)])
    w_one = lax.all_gather(w_one, SHARD, axis=0, tiled=True)
    w_two = side_by_side(ffn_packs, [(hidden_width, 2 * hidden_width)])
    w_two = lax.all_gather(w_two, SHARD, axis=0, tiled=True)
    w_out = w_proj[:, :all_heads], w_proj[:, all_heads : 2 * all_heads]
    w_cross = w_proj[:, 2 * all_heads : 3 * all_heads]
    used = -(-(n_head // 4 + n_up) // 128)
    biases = w_proj.reshape(shards, shard_rows, -1)[:, :used, 3 * all_heads :]
    biases = biases.reshape(shards, used, depth, 128).transpose(0, 2, 1, 3)
    biases = biases.reshape(shards, depth, -1)[:, :, : n_head // 4 + n_up]
    biases = biases.transpose(1, 2, 0).astype(wide)
    bias_cross = biases[:, : n_head // 4].reshape(-1)
    bias_up = biases[:, n_head // 4 :].reshape(-1)

    def heads_to_rows(array):
        return jnp.concatenate(spread(row_blocks(array, depth), T), axis=1)

    def rows_to_heads(array):
        return jnp.concatenate(spread(column_blocks(array, depth), T), axis=0)

    def owned(gradient):
        return lax.psum_scatter(gradient.astype(low), SHARD, scatter_dimension=0, tiled=True)

    def updated(index, gradient, scale=None):
        old = masters[index], gradient, firsts[index], seconds[index]
        master, first, second = adamw_step(*old, RATES[index], DECAYS[index])
        if scale is not None:
            master = master * scale
        return master, first, second, master.astype(low)

    def plane_parts(parts):
        pieces = [column_blocks(part, depth) for part in parts]
        return [jnp.concatenate([p[j] for p in pieces], axis=1) for j in range(depth)]

    self_context, self_lse, peaks = self_fwd(queries, kv, meta)
    self_all = heads_to_rows(self_context)
    enc_kv = relay_gather(enc_kv, [self_all])
    own_tokens = pick_rows(tokens, plane, rows).astype(wide)
    hidden_one = own_tokens + contract_cols(self_all, w_out[0]) + vec_all[0]
    normed_one, unit_one, factor_one = normalize(hidden_one, vec_all[3], vec_all[4])
    low_one = normed_one.astype(low)
    cross_queries = rows_to_heads((product(low_one, w_cross) + bias_cross).astype(low))
    holder = plane * groups // depth
    outgoing = []
    for j in range(groups):
        wanted = lax.dynamic_slice_in_dim(near_bases[j], plane * per_slice, per_slice)
        wanted = jnp.clip(wanted // BLK - member * rounds, 0, rounds - 1)
        picked = [pick_rows(cotangent, wanted[i], BLK) for i in range(per_slice)]
        outgoing.append(jnp.concatenate(picked))
    outgoing = after(outgoing, enc_kv[3:])
    incoming = jnp.where(member == holder, outgoing[0], jnp.zeros_like(outgoing[0]))
    for j in range(1, groups):
        pairs = []
        for level in range(depth):
            source = level * groups // depth
            pairs.append((source * depth + level, (source ^ j) * depth + level))
        incoming = incoming + lax.ppermute(outgoing[j], (C, T), pairs)
    cot_rows = incoming.astype(wide)

    cross_context, cross_lse = cross_fwd(cross_queries, enc_kv, seg)
    cross_all = heads_to_rows(cross_context)
    hidden_two = normed_one + contract_cols(cross_all, w_out[1]) + vec_all[1]
    normed_two, unit_two, factor_two = normalize(hidden_two, vec_all[5], vec_all[6])
    low_two = normed_two.astype(low)
    upward = product(low_two, w_one) + bias_up
    below = 0.5 * (1.0 + lax.erf(upward * 0.5**0.5))
    activated = (upward * below).astype(low)
    slope = below + upward * jnp.exp(-0.5 * upward * upward) * (0.5 / jnp.pi) ** 0.5
    hidden_three = normed_two + contract_cols(activated, w_two) + vec_all[2]
    normed_three, unit_three, factor_three = normalize(hidden_three, vec_all[7], vec_all[8])

    out_rows = from_planes(normed_three.astype(low))

    grad_three, gain_three, shift_three = normalize_back(
        cot_rows, unit_three, factor_three, vec_all[7]
    )
    mlp_grad = grad_three.astype(low)
    grad_w_two = contract_rows(mlp_grad, activated).astype(low)
    act_grad = product(mlp_grad, w_two).astype(low)
    up_grad = (act_grad.astype(wide) * slope).astype(low)
    grad_w_one = contract_rows(low_two, up_grad).astype(low)
    grad_up_bias = jnp.sum(up_grad.astype(wide), axis=0)
    grad_two, gain_two, shift_two = normalize_back(
        grad_three + contract_cols(up_grad, w_one), unit_two, factor_two, vec_all[5]
    )
    low_grad_two = grad_two.astype(low)
    cross_grads = rows_to_heads(product(low_grad_two, w_out[1]).astype(low))
    grad_out_cross = contract_rows(low_grad_two, cross_all).astype(low)
    own_down, own_up = owned(grad_w_two), owned(grad_w_one)
    out_rows = after(out_rows, [cross_grads])
    out_rows = jnp.stack(out_rows)[plane ^ jnp.arange(depth)].reshape(row_count, model_width)
    portion = row_count // groups
    returned = [pick_rows(out_rows, near[j], portion) for j in range(groups)]
    cross_q_grad, *enc_terms = cross_bwd(
        cross_queries,
        enc_kv,
        seg,
        cross_grads,
        cross_context,
        cross_lse,
        [grad_w_two, grad_w_one, grad_out_cross, *returned],
    )
    returned = spread(returned, C)
    enc_passed = relay_start(enc_terms)
    cross_q_all, *returned = after([heads_to_rows(cross_q_grad), *returned], [own_down])
    grad_one, gain_one, shift_one = normalize_back(
        grad_two + contract_cols(cross_q_all, w_cross), unit_one, factor_one, vec_all[3]
    )
    low_grad_one = grad_one.astype(low)
    self_grads = product(low_grad_one, w_out[0]).astype(low)
    enc_passed = after(enc_passed, [self_grads])
    cross_q_late, low_grad_late = after([cross_q_all, low_grad_one], [self_grads])
    self_grads = rows_to_heads(self_grads)
    enc_terms = relay_finish(relay_join(enc_terms, enc_passed))
    grad_in_cross = contract_rows(low_one, cross_q_late).astype(low)
    grad_out_self = contract_rows(low_grad_late, self_all).astype(low)
    grad_vectors = jnp.stack(
        [
            jnp.sum(grad_one, axis=0),
            jnp.sum(grad_two, axis=0),
            jnp.sum(grad_three, axis=0),
            gain_one,
            shift_one,
            gain_two,
            shift_two,
            gain_three,
            shift_three,
        ]
    )
    vec_part = grad_vectors.reshape(9, shards, -1).transpose(1, 0, 2).reshape(shards, -1)
    up_part = grad_up_bias.reshape(depth, -1, shards).transpose(2, 0, 1)
    small_part = jnp.concatenate(
        [
            by_shard(jnp.concatenate([vec_part, up_part[:, j]], axis=1), shard_rows)
            for j in range(depth)
        ],
        axis=1,
    ).astype(low)
    grad_proj = jnp.concatenate([grad_out_self, grad_out_cross, grad_in_cross, small_part], axis=1)
    down_parts = spread(plane_parts(after([own_down], [self_grads])), T)
    q_grad, *kv_terms = self_bwd(
        queries,
        kv,
        meta,
        self_grads,
        self_context,
        self_lse,
        [grad_proj],
    )
    kv_passed = relay_start(kv_terms)

    kv_joined = relay_join(kv_terms, kv_passed)
    (grad_proj,) = after([grad_proj], [own_up, q_grad])
    own_proj = owned(grad_proj)
    up_parts = spread(plane_parts(after([own_up], [q_grad])), T)
    enc_terms = after(enc_terms, kv_joined[1:])
    enc_grad = total(enc_terms).astype(low)
    width_part = model_width // depth
    enc_parts = [
        contract_cols(enc_grad, pick_rows(w_enc, plane ^ j, width_part)).astype(low)
        for j in range(depth)
    ]
    enc_sent = spread(enc_parts, T)
    grad_w_enc = contract_rows(encoder, enc_grad).astype(low)
    result = put_blocks(jnp.concatenate(returned), places, wide)
    top_all = jnp.max(peaks.reshape(-1, heads, BLK), axis=(0, 2))
    for axis in (C, F):
        step = 1
        while step < lax.axis_size(axis):
            top_all = jnp.maximum(top_all, swap(top_all, axis, step))
            step *= 2

    kv_terms = after(relay_finish(kv_joined), [*enc_parts, grad_w_enc, result])
    kv_grad = total(kv_terms).astype(low)
    q_natural = jnp.concatenate([pick_rows(q_grad, plane ^ j, rows) for j in range(depth)])
    qkv_grad = jnp.concatenate([q_natural, kv_grad], axis=1)
    token_terms = []
    for j in range(depth):
        term = contract_cols(qkv_grad, pick_rows(w_self, plane ^ j, width_part))
        piece = lax.dynamic_slice_in_dim(grad_one, (plane ^ j) * width_part, width_part, 1)
        piece = piece + pick_rows(term, plane, rows)
        token_terms.append(
            lax.dynamic_update_slice_in_dim(term, piece, plane * rows, 0).astype(low)
        )
    token_sent = spread(token_terms, T)
    grad_w_self = contract_rows(tokens, qkv_grad)
    grad_head_bias = jnp.stack(
        [
            jnp.sum(q_grad.astype(wide), axis=0),
            jnp.sum(kv_grad[:, head_width:].astype(wide), axis=0),
            jnp.sum(cross_q_grad.astype(wide), axis=0),
            jnp.sum(enc_grad[:, head_width:].astype(wide), axis=0),
        ]
    )
    head_part = grad_head_bias.reshape(4, -1, shards).transpose(2, 0, 1).reshape(shards, -1)
    grad_first = jnp.concatenate([grad_w_self, by_shard(head_part, shard_rows)], axis=1).astype(low)
    own_first = owned(grad_first).astype(wide)
    own_enc = owned(after([grad_w_enc], [grad_first])[0]).astype(wide)
    down_parts = after(down_parts, [grad_first, *token_terms])
    ffn_new = updated(2, total(up_parts)) + updated(3, total(down_parts).T)
    proj_parts = [own_proj[:, i * all_heads : (i + 1) * all_heads] for i in range(3)]
    proj_parts = plane_parts(proj_parts + [own_proj[:, 3 * all_heads :]])
    proj = total(spread(after(proj_parts, [grad_first, *token_terms]), T))
    grad_encoder = total(enc_sent)
    grad_tokens = total(token_sent)

    out_self, out_cross, in_cross = [
        proj[:, i * head_width : (i + 1) * head_width] for i in range(3)
    ]
    small_part = proj[:, 3 * head_width :].reshape(-1)
    gradients = {
        0: jnp.stack(
            column_blocks(own_first[:, : 3 * head_width], 3)
            + [in_cross]
            + column_blocks(own_enc, 2)
        ),
        1: jnp.stack([out_self.T, out_cross.T]),
        4: own_first[:, 3 * head_width :].reshape(-1)[:n_head].reshape(head_bias.shape),
        5: small_part[n_vec : n_vec + n_up].reshape(up_bias.shape),
        6: small_part[:n_vec].reshape(vectors.shape),
    }
    clip_factor = CLIP_LIMIT / jnp.maximum(top_all, CLIP_LIMIT)
    root_factor = jnp.sqrt(clip_factor)
    column_roots = jnp.repeat(root_factor, HEAD)
    in_scale = jnp.concatenate(
        [column_roots[None], column_roots[None], jnp.ones((4, head_width), wide)], axis=0
    )[:, None, :]
    slot_heads = (jnp.arange(head_bias.shape[1]) * shards + shard_index) // HEAD
    picked = jnp.sum(
        jnp.where(slot_heads[:, None] == jnp.arange(heads)[None, :], root_factor[None, :], 0.0),
        axis=1,
    )
    bias_scale = jnp.concatenate([picked[None], jnp.ones((3, picked.shape[0]), wide)], axis=0)
    scales = {0: in_scale, 4: bias_scale[:, :, None]}
    results = [result, grad_tokens, grad_encoder, clip_factor]
    for index in range(7):
        if index in gradients:
            results += updated(index, gradients[index], scales.get(index))
        else:
            results += ffn_new[4 * (index - 2) : 4 * (index - 1)]
    return tuple(results)


def solution(mesh):
    rows, table = P(SHARD, None), P(F, None)
    weights = (
        P(None, SHARD, T),
        P(None, T, SHARD),
        P(SHARD, T),
        P(T, SHARD),
        P(None, T, SHARD),
        P(T, SHARD),
        P(None, SHARD),
    )
    by_columns = P(SHARD, T)
    updates = tuple(spec for spec in weights for _ in range(4))
    return jax.shard_map(
        per_device,
        mesh=mesh,
        in_specs=(rows, rows, rows, table, table) + weights * 3,
        out_specs=(rows, by_columns, by_columns, P(T)) + updates,
        check_vma=False,
    )
```

```python
from functools import partial, reduce

import jax
import jax.numpy as jnp
from jax import lax
from jax.experimental import pallas as pl
from jax.experimental.pallas import tpu as pltpu
from jax.sharding import PartitionSpec as P

HEAD = 64
ENC = 4096
STEP = 10
BLK = 128

NEGATIVE = -1e30
NORM_EPS = 1e-05
ADAM_EPS = 1e-08
BETA = 0.5
CLIP_LIMIT = 10.0
RATES = (0.05, 0.3, 0.05, 0.03, 0.3, 0.3, 0.3)
DECAYS = (0.1, 0.1, 0.1, 0.1, 0.0, 0.0, 0.0)
SCALE = HEAD ** (-0.5)
VMEM_BYTES = 56 * 1024 * 1024
F, C, T = "fsdp", "context", "tensor"
SHARD = (F, C)
NO_COST = pl.CostEstimate(flops=0, bytes_accessed=0, transcendentals=0)
SOME_COST = pl.CostEstimate(flops=2 * 10**10, bytes_accessed=2**25, transcendentals=0)


def product(left_side, right_side):
    return jnp.dot(left_side, right_side, preferred_element_type=jnp.float32)


def contract_rows(left_side, right_side):
    return lax.dot_general(
        left_side, right_side, (((0,), (0,)), ((), ())), preferred_element_type=jnp.float32
    )


def contract_cols(left_side, right_side):
    return lax.dot_general(
        left_side, right_side, (((1,), (1,)), ((), ())), preferred_element_type=jnp.float32
    )


def stack_heads(block, heads):
    lanes = lax.broadcasted_iota(jnp.int32, block.shape, 1) // HEAD
    zero = jnp.zeros_like(block)
    return jnp.concatenate([jnp.where(lanes == h, block, zero) for h in range(heads)], axis=0)


def merge_heads(stacked, heads):
    rows = stacked.shape[0] // heads
    lanes = lax.broadcasted_iota(jnp.int32, (rows, stacked.shape[1]), 1) // HEAD
    merged = stacked[:rows]
    for h in range(1, heads):
        merged = jnp.where(lanes == h, stacked[h * rows : (h + 1) * rows], merged)
    return merged


def col_to_row(column):
    return jnp.transpose(jnp.broadcast_to(column, (column.shape[0], 128)))[0:1]


def fold_lanes(tile, combine):
    return reduce(combine, [tile[:, j : j + 128] for j in range(0, tile.shape[1], 128)])


def whole(shape):
    return pl.BlockSpec(shape, lambda i, s: (0,) * len(shape), pipeline_mode=pl.Buffered(1))


def fetch_kv(sources, places, sems):
    copies = [
        pltpu.make_async_copy(source, place, sems.at[i])
        for i, (source, place) in enumerate(zip(sources, places))
    ]

    @pl.when(pl.program_id(0) == 0)
    def _():
        for copy in copies:
            copy.start()
        for copy in copies:
            copy.wait()


def piece_bounds(pieces):
    full, half = pieces[0].shape[0], pieces[3].shape[0]
    return [(0, 0, full), (1, 0, full), (2, 0, full), (3, 0, half), (3, half, half)]


def member_rows(order_ref, row, bounds, full):
    return [
        pl.ds(pl.multiple_of(order_ref[row, j] * full + start, size), size)
        for j, start, size in bounds
    ]


def gate_body(*refs):
    pass


def after(values, others):
    count, every = len(values), [*values, *others]
    return pl.pallas_call(
        gate_body,
        in_specs=[pl.BlockSpec(memory_space=pl.ANY)] * len(every),
        out_specs=[pl.BlockSpec(memory_space=pl.ANY)] * count,
        out_shape=[jax.ShapeDtypeStruct(value.shape, value.dtype) for value in values],
        input_output_aliases={i: i for i in range(count)},
        cost_estimate=NO_COST,
        name="gate",
    )(*every)


def cross_fwd_body(heads, bounds, seg_ref, q_ref, *refs):
    sources, (o_ref, lse_ref, kv_ref, s_ref, sems) = refs[: len(bounds)], refs[len(bounds) :]
    places = member_rows(seg_ref, 3, bounds, sources[0].shape[0])
    fetch_kv(sources, [kv_ref.at[place] for place in places], sems)
    block = pl.program_id(0)
    low, high, cut = seg_ref[0, block], seg_ref[1, block], seg_ref[2, block]
    queries = stack_heads(q_ref[...] * jnp.bfloat16(SCALE), heads)
    rows, width = queries.shape
    tiles, _, step = s_ref.shape

    def attend(sequence):
        def scores(t, highest):
            at = pl.ds(pl.multiple_of(sequence * ENC + t * step, step), step)
            tile = contract_cols(queries, kv_ref[at, :width])
            s_ref[t] = tile
            return jnp.maximum(highest, fold_lanes(tile, jnp.maximum))

        highest = lax.fori_loop(0, tiles, scores, jnp.full((rows, 128), NEGATIVE, jnp.float32))
        peak = jnp.max(highest, axis=1, keepdims=True)

        def weigh(t, running):
            total, summed = running
            at = pl.ds(pl.multiple_of(sequence * ENC + t * step, step), step)
            weights = jnp.exp(s_ref[t] - peak)
            summed = summed + product(weights.astype(jnp.bfloat16), kv_ref[at, width:])
            return total + fold_lanes(weights, jnp.add), summed

        total, summed = lax.fori_loop(
            0,
            tiles,
            weigh,
            (jnp.zeros((rows, 128), jnp.float32), jnp.zeros((rows, width), jnp.float32)),
        )
        total = jnp.sum(total, axis=1, keepdims=True)
        merged = merge_heads(summed / total, heads)
        lse = col_to_row(peak + jnp.log(total))
        place = lax.broadcasted_iota(jnp.int32, merged.shape, 0)
        own = jnp.where(place >= cut, 1, 0) == sequence
        o_ref[...] = jnp.where(own, merged, o_ref[...].astype(jnp.float32)).astype(o_ref.dtype)
        place = lax.broadcasted_iota(jnp.int32, lse.shape, 1) % BLK
        own = jnp.where(place >= cut, 1, 0) == sequence
        lse_ref[0] = jnp.where(own, lse, lse_ref[0])

    o_ref[...] = jnp.zeros_like(o_ref)
    lse_ref[...] = jnp.zeros_like(lse_ref)
    pl.loop(low, high + 1)(attend)


def cross_fwd(queries, enc_kv, seg):
    count, width = queries.shape
    heads, blocks, step = width // HEAD, count // BLK, 1024
    rows, bounds = heads * BLK, piece_bounds(enc_kv)
    enc_all = sum(piece.shape[0] for piece in enc_kv)
    return pl.pallas_call(
        partial(cross_fwd_body, heads, bounds),
        grid_spec=pltpu.PrefetchScalarGridSpec(
            num_scalar_prefetch=1,
            grid=(blocks,),
            in_specs=[pl.BlockSpec((BLK, width), lambda i, s: (i, 0))]
            + [pl.BlockSpec(memory_space=pl.ANY)] * len(bounds),
            out_specs=[
                pl.BlockSpec((BLK, width), lambda i, s: (i, 0)),
                pl.BlockSpec((1, 1, rows), lambda i, s: (i, 0, 0)),
            ],
            scratch_shapes=[
                pltpu.VMEM((enc_all, 2 * width), jnp.bfloat16),
                pltpu.VMEM((ENC // step, rows, step), jnp.float32),
                pltpu.SemaphoreType.DMA((len(bounds),)),
            ],
        ),
        out_shape=[
            jax.ShapeDtypeStruct((count, width), jnp.bfloat16),
            jax.ShapeDtypeStruct((blocks, 1, rows), jnp.float32),
        ],
        compiler_params=pltpu.CompilerParams(vmem_limit_bytes=VMEM_BYTES),
        cost_estimate=NO_COST,
        name="cross_fwd",
    )(seg, queries, *enc_kv)


def cross_bwd_body(heads, bounds, kind, step, seg_ref, q_ref, g_ref, o_ref, lse_ref, *refs):
    count, outs = len(bounds), refs[-len(bounds) - 4 : -3]
    sources, prior, (dq_ref, *outs) = refs[:count], refs[count], outs
    kv_ref, acc_ref, sems = refs[-3:]
    block = pl.program_id(0)
    sequence, full = seg_ref[4, kind], ENC // 2
    places = [
        pl.ds(pl.multiple_of(seg_ref[3, j] * full + at - sequence * ENC, size), size)
        for j, at, size in bounds
    ]
    fetch_kv(sources, [kv_ref.at[place] for place in places], sems)

    @pl.when(block == 0)
    def _():
        acc_ref[...] = jnp.zeros_like(acc_ref)

    seen = (seg_ref[0, block] <= sequence) & (seg_ref[1, block] >= sequence)
    start = prior[...] if kind == 0 else jnp.zeros_like(dq_ref)
    dq_ref[...] = start

    @pl.when(seen)
    def _():
        queries = stack_heads(q_ref[...] * jnp.bfloat16(SCALE), heads)
        rows, width = queries.shape
        grads = stack_heads(g_ref[...], heads)
        dots = g_ref[...].astype(jnp.float32) * o_ref[...].astype(jnp.float32)
        dot_row = col_to_row(jnp.sum(stack_heads(dots, heads), axis=1, keepdims=True))
        place = lax.broadcasted_iota(jnp.int32, lse_ref[0].shape, 1) % BLK
        own_seq = jnp.where(place >= seg_ref[2, block], 1, 0)
        lse = jnp.where(own_seq == sequence, lse_ref[0], -NEGATIVE)

        def tile_terms(t, q_grad):
            at = pl.ds(pl.multiple_of(t * step, step), step)
            keys, values = kv_ref[at, :width], kv_ref[at, width:]
            probs = jnp.exp(contract_cols(keys, queries) - lse)
            s_grad = (probs * (contract_cols(values, grads) - dot_row)).astype(jnp.bfloat16)
            acc_ref[at, width:] += product(probs.astype(jnp.bfloat16), grads)
            acc_ref[at, :width] += product(s_grad, queries)
            return q_grad + contract_rows(s_grad, keys)

        q_grad = lax.fori_loop(
            0, ENC // step, tile_terms, jnp.zeros((rows, width), jnp.float32)
        )
        q_grad = merge_heads(q_grad, heads) * SCALE + start.astype(jnp.float32)
        dq_ref[...] = q_grad.astype(dq_ref.dtype)

    @pl.when(block == pl.num_programs(0) - 1)
    def _():
        for out, place in zip(outs, places):
            out[...] = acc_ref[place, :].astype(out.dtype)


def cross_bwd(kind, queries, enc_kv, seg, grads, context, lse, prior, others):
    count, width = queries.shape
    heads, blocks, step = width // HEAD, count // BLK, 512
    bounds = piece_bounds(enc_kv)
    picked = [(0, 1), (2, 3, 4)][kind]
    pieces, bounds = [enc_kv[i] for i in picked], [bounds[i] for i in picked]
    row = pl.BlockSpec((BLK, width), lambda i, s: (i, 0))
    return pl.pallas_call(
        partial(cross_bwd_body, heads, bounds, kind, step),
        grid_spec=pltpu.PrefetchScalarGridSpec(
            num_scalar_prefetch=1,
            grid=(blocks,),
            in_specs=[row, row, row, pl.BlockSpec((1, 1, heads * BLK), lambda i, s: (i, 0, 0))]
            + [pl.BlockSpec(memory_space=pl.ANY)] * len(bounds)
            + [row]
            + [pl.BlockSpec(memory_space=pl.ANY)] * len(others),
            out_specs=[row] + [whole(piece.shape) for piece in pieces],
            scratch_shapes=[
                pltpu.VMEM((ENC, 2 * width), jnp.bfloat16),
                pltpu.VMEM((ENC, 2 * width), jnp.float32),
                pltpu.SemaphoreType.DMA((len(bounds),)),
            ],
        ),
        out_shape=[jax.ShapeDtypeStruct((count, width), jnp.bfloat16)]
        + [jax.ShapeDtypeStruct(piece.shape, jnp.bfloat16) for piece in pieces],
        compiler_params=pltpu.CompilerParams(vmem_limit_bytes=VMEM_BYTES),
        cost_estimate=NO_COST,
        name="cross_bwd",
    )(seg, queries, grads, context, lse, *pieces, prior, *others)


def gather_tile(kv_ref, t, columns):
    at = pl.ds(pl.multiple_of(t * BLK, BLK), BLK)
    return jnp.concatenate([kv_ref[j, at, columns] for j in range(kv_ref.shape[0])], axis=0)


def self_fwd_body(heads, bounds, meta_ref, q_ref, *refs):
    sources, (o_ref, lse_ref, top_ref, kv_refs, sems) = refs[: len(bounds)], refs[len(bounds) :]
    fetch_kv(sources, [kv_refs.at[j, pl.ds(at, size)] for j, at, size in bounds], sems)
    groups = kv_refs.shape[0]
    block = pl.program_id(0)
    base, first, last = [meta_ref[groups + k, block] for k in range(3)]
    cut = meta_ref[groups + 3, 0]
    queries = stack_heads(q_ref[...] * jnp.bfloat16(SCALE), heads)
    rows, width = queries.shape
    q_pos = base + lax.broadcasted_iota(jnp.int32, (rows, BLK), 0) % BLK
    q_start = jnp.where(q_pos >= cut, cut, 0)
    lane = lax.broadcasted_iota(jnp.int32, (rows, BLK), 1)

    def visit(t, running):
        peak, total, summed = running
        raw = contract_cols(queries, gather_tile(kv_refs, t, slice(0, width)))
        parts = []
        for d in range(groups):
            k_pos = lane + meta_ref[d, t]
            seen = (k_pos <= q_pos) & (k_pos >= q_start)
            parts.append(jnp.where(seen, raw[:, d * BLK : (d + 1) * BLK], NEGATIVE))
        new_peak = jnp.maximum(peak, jnp.max(reduce(jnp.maximum, parts), axis=1, keepdims=True))
        weights = [jnp.exp(part - new_peak) for part in parts]
        shrink = jnp.exp(peak - new_peak)
        total = total * shrink + jnp.sum(reduce(jnp.add, weights), axis=1, keepdims=True)
        low_weights = jnp.concatenate(weights, axis=1).astype(jnp.bfloat16)
        values = gather_tile(kv_refs, t, slice(width, 2 * width))
        return new_peak, total, summed * shrink + product(low_weights, values)

    peak, total, summed = lax.fori_loop(
        first,
        last + 1,
        visit,
        (
            jnp.full((rows, 1), NEGATIVE, jnp.float32),
            jnp.zeros((rows, 1), jnp.float32),
            jnp.zeros((rows, width), jnp.float32),
        ),
    )
    o_ref[...] = merge_heads(summed / total, heads).astype(o_ref.dtype)
    lse_ref[0] = col_to_row(peak + jnp.log(total))
    top_ref[0] = col_to_row(peak)


def self_fwd(queries, kv, meta):
    count, width = queries.shape
    heads, blocks, bounds = width // HEAD, count // BLK, piece_bounds(kv)
    rows, kept = heads * BLK, (bounds[-1][0] + 1,) + kv[0].shape
    row = pl.BlockSpec((BLK, width), lambda i, s: (i, 0))
    stat = pl.BlockSpec((1, 1, rows), lambda i, s: (i, 0, 0))
    return pl.pallas_call(
        partial(self_fwd_body, heads, bounds),
        grid_spec=pltpu.PrefetchScalarGridSpec(
            num_scalar_prefetch=1,
            grid=(blocks,),
            in_specs=[row] + [pl.BlockSpec(memory_space=pl.ANY)] * len(bounds),
            out_specs=[row, stat, stat],
            scratch_shapes=[
                pltpu.VMEM(kept, jnp.bfloat16),
                pltpu.SemaphoreType.DMA((len(bounds),)),
            ],
        ),
        out_shape=[jax.ShapeDtypeStruct((count, width), jnp.bfloat16)]
        + [jax.ShapeDtypeStruct((blocks, 1, rows), jnp.float32)] * 2,
        compiler_params=pltpu.CompilerParams(vmem_limit_bytes=VMEM_BYTES),
        cost_estimate=NO_COST,
        name="self_fwd",
    )(meta, queries, *kv)


def self_bwd_body(heads, bounds, waits, meta_ref, q_ref, g_ref, o_ref, lse_ref, *refs):
    count = len(bounds)
    sources, (dq_ref, *outs) = refs[:count], refs[count + waits : 2 * count + waits + 1]
    kv_refs, acc_ref, sems = refs[2 * count + waits + 1 :]
    fetch_kv(sources, [kv_refs.at[j, pl.ds(at, size)] for j, at, size in bounds], sems)
    groups = kv_refs.shape[0]
    block = pl.program_id(0)

    @pl.when(block == 0)
    def _():
        acc_ref[...] = jnp.zeros_like(acc_ref)

    base, first, last = [meta_ref[groups + k, block] for k in range(3)]
    cut = meta_ref[groups + 3, 0]
    queries = stack_heads(q_ref[...] * jnp.bfloat16(SCALE), heads)
    rows, width = queries.shape
    grads = stack_heads(g_ref[...], heads)
    dots = g_ref[...].astype(jnp.float32) * o_ref[...].astype(jnp.float32)
    dot_row = col_to_row(jnp.sum(stack_heads(dots, heads), axis=1, keepdims=True))
    lse = lse_ref[0]
    q_pos = base + lax.broadcasted_iota(jnp.int32, lse.shape, 1) % BLK
    q_start = jnp.where(q_pos >= cut, cut, 0)
    sub = lax.broadcasted_iota(jnp.int32, (BLK, rows), 0)

    def tile_terms(t, q_grad):
        at = pl.ds(pl.multiple_of(t * BLK, BLK), BLK)
        keys = gather_tile(kv_refs, t, slice(0, width))
        values = gather_tile(kv_refs, t, slice(width, 2 * width))
        raw = contract_cols(keys, queries)
        parts = []
        for d in range(groups):
            k_base = meta_ref[d, t]
            seen = (sub <= q_pos - k_base) & (sub >= q_start - k_base)
            parts.append(jnp.where(seen, jnp.exp(raw[d * BLK : (d + 1) * BLK] - lse), 0.0))
        probs = jnp.concatenate(parts, axis=0)
        s_grad = (probs * (contract_cols(values, grads) - dot_row)).astype(jnp.bfloat16)
        acc_ref[:, at, width:] += product(probs.astype(jnp.bfloat16), grads).reshape(
            groups, BLK, width
        )
        acc_ref[:, at, :width] += product(s_grad, queries).reshape(groups, BLK, width)
        return q_grad + contract_rows(s_grad, keys)

    q_grad = lax.fori_loop(first, last + 1, tile_terms, jnp.zeros((rows, width), jnp.float32))
    dq_ref[...] = (merge_heads(q_grad, heads) * SCALE).astype(dq_ref.dtype)

    @pl.when(block == pl.num_programs(0) - 1)
    def _():
        for out, (j, at, size) in zip(outs, bounds):
            out[...] = acc_ref[j, at : at + size].astype(out.dtype)


def self_bwd(queries, kv, meta, grads, context, lse, others):
    count, width = queries.shape
    heads, blocks, bounds = width // HEAD, count // BLK, piece_bounds(kv)
    rows, kept = heads * BLK, (bounds[-1][0] + 1,) + kv[0].shape
    row = pl.BlockSpec((BLK, width), lambda i, s: (i, 0))
    stat = pl.BlockSpec((1, 1, rows), lambda i, s: (i, 0, 0))
    return pl.pallas_call(
        partial(self_bwd_body, heads, bounds, len(others)),
        grid_spec=pltpu.PrefetchScalarGridSpec(
            num_scalar_prefetch=1,
            grid=(blocks,),
            in_specs=[row, row, row, stat]
            + [pl.BlockSpec(memory_space=pl.ANY)] * (len(bounds) + len(others)),
            out_specs=[row] + [whole(piece.shape) for piece in kv],
            scratch_shapes=[
                pltpu.VMEM(kept, jnp.bfloat16),
                pltpu.VMEM(kept, jnp.float32),
                pltpu.SemaphoreType.DMA((len(bounds),)),
            ],
        ),
        out_shape=[jax.ShapeDtypeStruct((count, width), jnp.bfloat16)]
        + [jax.ShapeDtypeStruct(piece.shape, jnp.bfloat16) for piece in kv],
        compiler_params=pltpu.CompilerParams(vmem_limit_bytes=VMEM_BYTES),
        cost_estimate=NO_COST,
        name="self_bwd",
    )(meta, queries, grads, context, lse, *kv, *others)


def move_body(index_ref, in_ref, out_ref):
    out_ref[...] = in_ref[...].astype(out_ref.dtype)


def put_blocks(rows, index, dtype):
    count, width = rows.shape
    return pl.pallas_call(
        move_body,
        grid_spec=pltpu.PrefetchScalarGridSpec(
            num_scalar_prefetch=1,
            grid=(count // BLK,),
            in_specs=[pl.BlockSpec((BLK, width), lambda i, s: (i, 0))],
            out_specs=pl.BlockSpec((BLK, width), lambda i, s: (s[i], 0)),
        ),
        out_shape=jax.ShapeDtypeStruct((count, width), dtype),
        cost_estimate=SOME_COST,
        name="put_blocks",
    )(index, rows)


def join_body(whole_ref, passed_ref, *refs):
    total = whole_ref[...].astype(jnp.float32) + passed_ref[...].astype(jnp.float32)
    refs[-1][...] = total.astype(refs[-1].dtype)


def add_half(whole_rows, passed, lower, others):
    half, width = passed.shape
    size = min(half, 256)
    first = half // size if lower else 0
    part = pl.BlockSpec((size, width), lambda i: (first + i, 0))
    return pl.pallas_call(
        join_body,
        grid=(half // size,),
        in_specs=[part, pl.BlockSpec((size, width), lambda i: (i, 0))]
        + [pl.BlockSpec(memory_space=pl.ANY)] * len(others),
        out_specs=part,
        out_shape=jax.ShapeDtypeStruct(whole_rows.shape, whole_rows.dtype),
        input_output_aliases={0: 0},
        cost_estimate=NO_COST,
        name="add_half",
    )(whole_rows, passed, *others)


def grad_body(count, *refs):
    out_ref, start = refs[-1], 0
    for k in range(count):
        terms = contract_rows(refs[2 * k][...], refs[2 * k + 1][...])
        out_ref[:, start : start + terms.shape[1]] = terms.astype(out_ref.dtype)
        start += terms.shape[1]
    for ref in refs[2 * count : -1]:
        out_ref[:, start : start + ref.shape[1]] = ref[...]
        start += ref.shape[1]


def grad_columns(pairs, others, tiles=1):
    flat = [array for pair in pairs for array in pair]
    width = pairs[0][0].shape[1]
    columns = sum(right.shape[1] for _, right in pairs) + sum(array.shape[1] for array in others)
    size = pairs[0][1].shape[0]
    if tiles == 1:
        specs = [pl.BlockSpec(array.shape, lambda i: (0, 0)) for array in flat + others]
    else:
        specs = [
            pl.BlockSpec((size, width), lambda i: (0, 0)),
            pl.BlockSpec((size, columns // tiles), lambda i: (0, i)),
        ]
    return pl.pallas_call(
        partial(grad_body, len(pairs)),
        grid=(tiles,),
        in_specs=specs,
        out_specs=pl.BlockSpec((width, columns // tiles), lambda i: (0, i)),
        out_shape=jax.ShapeDtypeStruct((width, columns), jnp.bfloat16),
        compiler_params=pltpu.CompilerParams(vmem_limit_bytes=VMEM_BYTES),
        cost_estimate=NO_COST,
        name="grad_columns",
    )(*flat, *others)


def plane_body(plane_ref, *refs):
    start = 0
    for ref in refs[:-1]:
        refs[-1][:, start : start + ref.shape[1]] = ref[...]
        start += ref.shape[1]


def by_plane_order(arrays, plane, depth):
    size = arrays[0].shape[0]
    widths = [array.shape[1] // depth for array in arrays]
    return pl.pallas_call(
        plane_body,
        grid_spec=pltpu.PrefetchScalarGridSpec(
            num_scalar_prefetch=1,
            grid=(depth,),
            in_specs=[pl.BlockSpec((size, width), lambda p, s: (0, s[0] ^ p)) for width in widths],
            out_specs=pl.BlockSpec((size, sum(widths)), lambda p, s: (0, p)),
        ),
        out_shape=jax.ShapeDtypeStruct((size, depth * sum(widths)), arrays[0].dtype),
        cost_estimate=NO_COST,
        name="by_plane_order",
    )(plane.reshape(1).astype(jnp.int32), *arrays)


ANYWHERE = pl.BlockSpec(memory_space=pl.ANY)


def sum_body(count, *refs):
    out_ref, column_ref = refs[-2:]
    added = reduce(jnp.add, [ref[...].astype(jnp.float32) for ref in refs[:count]])
    rounded = added.astype(out_ref.dtype)
    out_ref[...] = rounded

    @pl.when(pl.program_id(0) == 0)
    def _():
        column_ref[...] = jnp.zeros_like(column_ref)

    column_ref[...] += jnp.sum(rounded.astype(jnp.float32), axis=0, keepdims=True)


def sum_terms(terms, others, cost=SOME_COST):
    count, width = terms[0].shape
    size = 256
    tile = pl.BlockSpec((size, width), lambda i: (i, 0))
    return pl.pallas_call(
        partial(sum_body, len(terms)),
        grid=(count // size,),
        in_specs=[tile] * len(terms) + [ANYWHERE] * len(others),
        out_specs=[tile, pl.BlockSpec((1, width), lambda i: (0, 0))],
        out_shape=[
            jax.ShapeDtypeStruct((count, width), jnp.bfloat16),
            jax.ShapeDtypeStruct((1, width), jnp.float32),
        ],
        cost_estimate=cost,
        name="sum_terms",
    )(*terms, *others)


def share_body(depth, parts, extra, plane_ref, *refs):
    rows = [ref[...] for ref in refs[:parts]]
    merged = rows[0] if parts == 1 else jnp.concatenate(rows, axis=1)
    own = pl.program_id(0) == plane_ref[0]
    for j in range(depth):
        term = contract_cols(merged, refs[parts + j][...])
        if extra:
            term = term + jnp.where(own, refs[parts + depth + j][...], 0.0)
        refs[len(refs) - depth + j][...] = term.astype(jnp.bfloat16)


def plane_shares(arrays, weight, plane, depth, extra, others, cost=SOME_COST):
    count, size = arrays[-1].shape[0], 256 if extra is None else extra.shape[0]
    part = weight.shape[0] // depth
    last = pl.BlockSpec((size, arrays[-1].shape[1]), lambda i, s: (i, 0))
    specs = [last]
    if len(arrays) == 2:
        specs = [pl.BlockSpec((size, arrays[0].shape[1]), lambda i, s: (s[0] ^ i, 0)), last]
    for j in range(depth):
        specs.append(
            pl.BlockSpec((part, weight.shape[1]), partial(lambda j, i, s: (s[0] ^ j, 0), j))
        )
    inputs = [*arrays, *[weight] * depth]
    if extra is not None:
        for j in range(depth):
            specs.append(pl.BlockSpec((size, part), partial(lambda j, i, s: (0, s[0] ^ j), j)))
        inputs += [extra] * depth
    return pl.pallas_call(
        partial(share_body, depth, len(arrays), extra is not None),
        grid_spec=pltpu.PrefetchScalarGridSpec(
            num_scalar_prefetch=1,
            grid=(count // size,),
            in_specs=specs + [ANYWHERE] * len(others),
            out_specs=[pl.BlockSpec((size, part), lambda i, s: (i, 0))] * depth,
        ),
        out_shape=[jax.ShapeDtypeStruct((count, part), jnp.bfloat16)] * depth,
        compiler_params=pltpu.CompilerParams(vmem_limit_bytes=VMEM_BYTES),
        cost_estimate=cost,
        name="plane_shares",
    )(plane.reshape(1).astype(jnp.int32), *inputs, *others)


def gather_grad_body(parts, adds, plane_ref, left_ref, *refs):
    out_ref, acc_ref = refs[-2:]
    step = pl.program_id(0)

    @pl.when(step == 0)
    def _():
        acc_ref[...] = jnp.zeros_like(acc_ref)

    start = 0
    for ref in refs[:parts]:
        stop = start + ref.shape[1]
        acc_ref[:, start:stop] += contract_rows(left_ref[...], ref[...])
        start = stop

    @pl.when(step == pl.num_programs(0) - 1)
    def _():
        out_ref[:, :start] = acc_ref[...].astype(out_ref.dtype)
        at = start
        for ref in refs[parts : parts + adds]:
            out_ref[:, at : at + ref.shape[1]] = ref[...]
            at += ref.shape[1]


def weight_grad(left, arrays, adds, plane, size, others, cost=SOME_COST):
    count, width = left.shape
    last = pl.BlockSpec((size, arrays[-1].shape[1]), lambda i, s: (i, 0))
    specs = [pl.BlockSpec((size, width), lambda i, s: (i, 0)), last]
    if len(arrays) == 2:
        specs.insert(1, pl.BlockSpec((size, arrays[0].shape[1]), lambda i, s: (s[0] ^ i, 0)))
    made = sum(array.shape[1] for array in arrays)
    columns = made + sum(array.shape[1] for array in adds)
    specs += [whole(array.shape) for array in adds] + [ANYWHERE] * len(others)
    return pl.pallas_call(
        partial(gather_grad_body, len(arrays), len(adds)),
        grid_spec=pltpu.PrefetchScalarGridSpec(
            num_scalar_prefetch=1,
            grid=(count // size,),
            in_specs=specs,
            out_specs=pl.BlockSpec((width, columns), lambda i, s: (0, 0)),
            scratch_shapes=[pltpu.VMEM((width, made), jnp.float32)],
        ),
        out_shape=jax.ShapeDtypeStruct((width, columns), jnp.bfloat16),
        compiler_params=pltpu.CompilerParams(vmem_limit_bytes=VMEM_BYTES),
        cost_estimate=cost,
        name="weight_grad",
    )(plane.reshape(1).astype(jnp.int32), left, *arrays, *adds, *others)


def normalize(hidden, gain_row, shift_row):
    centred = hidden - jnp.mean(hidden, axis=-1, keepdims=True)
    factor = lax.rsqrt(jnp.mean(centred * centred, axis=-1, keepdims=True) + NORM_EPS)
    unit_rows = centred * factor
    return (unit_rows * gain_row + shift_row, unit_rows, factor)


def normalize_back(incoming, unit_rows, factor, gain_row):
    scaled = incoming * gain_row
    centred_grad = (
        scaled
        - jnp.mean(scaled, axis=-1, keepdims=True)
        - unit_rows * jnp.mean(scaled * unit_rows, axis=-1, keepdims=True)
    )
    return (factor * centred_grad, jnp.sum(incoming * unit_rows, axis=0), jnp.sum(incoming, axis=0))


def adamw_step(master, gradient, first_moment, second_moment, step_rate, weight_decay):
    first_moment = BETA * first_moment + (1.0 - BETA) * gradient
    second_moment = BETA * second_moment + (1.0 - BETA) * gradient * gradient
    correction = 1.0 - BETA**STEP
    update = first_moment / correction / (jnp.sqrt(second_moment / correction) + ADAM_EPS)
    return (master - step_rate * (update + weight_decay * master), first_moment, second_moment)
def swap(value, axis, j):
    return lax.ppermute(value, axis, [(i, i ^ j) for i in range(lax.axis_size(axis))])


def spread(blocks, axis):
    return [blocks[0]] + [swap(blocks[j], axis, j) for j in range(1, len(blocks))]


def total(blocks):
    return reduce(jnp.add, [block.astype(jnp.float32) for block in blocks])


def column_blocks(array, count):
    size = array.shape[1] // count
    return [array[:, j * size : (j + 1) * size] for j in range(count)]


def row_blocks(array, count):
    size = array.shape[0] // count
    return [array[j * size : (j + 1) * size] for j in range(count)]


def pick_rows(array, index, size):
    return lax.dynamic_slice_in_dim(array, index * size, size, 0)


def by_shard(flat, shard_rows):
    shards, used = flat.shape
    flat = jnp.pad(flat, ((0, 0), (0, -used % 128))).reshape(shards, -1, 128)
    return jnp.pad(flat, ((0, 0), (0, shard_rows - flat.shape[1]), (0, 0))).reshape(-1, 128)


def relay_gather(block, others=()):
    near, far = swap(block, C, 1), swap(block, C, 2)
    if others:
        near, far = after([near, far], others)
    half = block.shape[0] // 2
    return [block, near, far, swap(far[:half], C, 1), swap(near[half:], C, 2)]


def relay_start(upper, lower):
    return swap(upper, C, 1), swap(lower, C, 2)


def relay_join(terms, passed, others=()):
    own, near, far = terms[:3]
    return own, add_half(near, passed[1], True, others), add_half(far, passed[0], False, others)


def relay_finish(joined):
    own, near, far = joined
    return [own, swap(near, C, 1), swap(far, C, 2)]


def per_device(tokens, encoder, cotangent, lengths, order, *params):
    masters, firsts, seconds = params[:7], params[7:14], params[14:]
    in_proj, out_proj, w_up, w_down, head_bias, up_bias, vectors = masters
    low, wide = jnp.bfloat16, jnp.float32
    groups, member = lax.axis_size(C), lax.axis_index(C)
    depth, plane = lax.axis_size(T), lax.axis_index(T)
    shards, shard_index = lax.axis_size(SHARD), lax.axis_index(SHARD)
    row_count, model_width = tokens.shape
    head_width, hidden_width = in_proj.shape[2], w_up.shape[1]
    heads = head_width // HEAD
    shard_rows = in_proj.shape[1]
    rounds = row_count // BLK
    rows = row_count // depth
    per_slice, per_member = rows // BLK, rounds // groups
    all_heads, all_hidden = depth * head_width, depth * hidden_width

    n_vec, n_head, n_up = vectors.size, head_bias.size, up_bias.size
    small = jnp.concatenate([vectors.reshape(-1), head_bias.reshape(-1)])
    first_part = jnp.concatenate(
        [in_proj[0], in_proj[1], in_proj[2], by_shard(small[None], shard_rows)], axis=1
    )
    first_part = lax.all_gather(first_part.astype(low), SHARD, axis=0, tiled=True)
    biases = jnp.concatenate([head_bias[2].reshape(-1), up_bias.reshape(-1)])
    proj_pack = jnp.concatenate(
        [out_proj[0].T, out_proj[1].T, in_proj[3], by_shard(biases[None], shard_rows)], axis=1
    ).astype(low)
    ffn_pack = jnp.concatenate([w_up, w_down.T], axis=1).astype(low)

    def from_planes(array):
        return [array] + [swap(array, T, j) for j in range(1, depth)]

    proj_packs = from_planes(proj_pack)
    w_enc = jnp.concatenate([in_proj[4], in_proj[5]], axis=1).astype(low)
    (w_enc,) = after([w_enc], proj_packs[1:])
    w_enc = lax.all_gather(w_enc, SHARD, axis=0, tiled=True)
    w_self = first_part[:, : 3 * head_width]
    used = -(-(n_vec + n_head) // 128)
    small = first_part.reshape(shards, shard_rows, -1)[:, :used, 3 * head_width :]
    small = small.reshape(shards, -1)
    vec_all = small[:, :n_vec].reshape(shards, 9, -1).transpose(1, 0, 2).reshape(9, -1)
    vec_all = vec_all.astype(wide)

    def by_columns(flat, count):
        return flat.reshape(shards, count, -1).transpose(1, 2, 0).reshape(count, -1).astype(wide)

    bias_heads = by_columns(small[:, n_vec : n_vec + n_head], 4)

    bases = order[0].reshape(groups, rounds, BLK)[:, :, 0]
    cut = lengths[0, 0]
    near = member ^ jnp.arange(groups)
    spot = jnp.arange(rounds)
    q_rounds = (plane ^ (spot // per_slice)) * per_slice + spot % per_slice
    q_bases = jnp.take(lax.dynamic_index_in_dim(bases, member, 0, keepdims=False), q_rounds)
    seg = jnp.stack(
        [
            (q_bases >= cut).astype(jnp.int32),
            (q_bases + BLK - 1 >= cut).astype(jnp.int32),
            jnp.clip(cut - q_bases, 0, BLK),
            jnp.pad(near, (0, rounds - groups)),
            (member * encoder.shape[0] // ENC) ^ jnp.minimum(spot, 1),
        ]
    ).astype(jnp.int32)
    near_bases = jnp.take(bases, near, axis=0)
    meta = jnp.concatenate(
        [
            near_bases,
            q_bases[None],
            jnp.where(q_bases >= cut, cut // (groups * BLK), 0)[None],
            q_rounds[None],
            jnp.full((1, rounds), cut),
        ],
        axis=0,
    ).astype(jnp.int32)
    places = (
        lax.dynamic_slice_in_dim(near_bases, member * per_member, per_member, 1) // BLK
        - member * rounds
    ).reshape(-1)

    qkv = product(tokens, w_self)
    queries = (qkv[:, :head_width] + bias_heads[0]).astype(low)
    queries = jnp.concatenate([pick_rows(queries, plane ^ j, rows) for j in range(depth)])
    no_bias = jnp.zeros((head_width,), wide)
    kv = (qkv[:, head_width:] + jnp.concatenate([no_bias, bias_heads[1]])).astype(low)
    kv = relay_gather(kv)
    ffn_packs = from_planes(after([ffn_pack], kv[:1])[0])
    (w_enc,) = after([w_enc], kv[:1])
    enc_kv = product(encoder, w_enc) + jnp.concatenate([no_bias, bias_heads[3]])
    enc_kv = enc_kv.astype(low)
    *kv[3:], w_kept = after([*kv[3:], w_self], [enc_kv])

    def side_by_side(packs, bounds):
        return jnp.concatenate([pack[:, a:b] for a, b in bounds for pack in packs], axis=1)

    proj_bounds = [(i * head_width, (i + 1) * head_width) for i in range(3)]
    proj_bounds.append((3 * head_width, proj_pack.shape[1]))
    w_proj = side_by_side(proj_packs, proj_bounds)
    w_proj = lax.all_gather(w_proj, SHARD, axis=0, tiled=True)
    (enc_kv,) = after([enc_kv], kv[3:])
    ffn_packs = after(ffn_packs, kv[3:])
    w_one = side_by_side(ffn_packs, [(0, hidden_width)])
    w_one = lax.all_gather(w_one, SHARD, axis=0, tiled=True)
    w_two = side_by_side(ffn_packs, [(hidden_width, 2 * hidden_width)])
    w_two = lax.all_gather(w_two, SHARD, axis=0, tiled=True)
    w_out = w_proj[:, :all_heads], w_proj[:, all_heads : 2 * all_heads]
    w_cross = w_proj[:, 2 * all_heads : 3 * all_heads]
    used = -(-(n_head // 4 + n_up) // 128)
    biases = w_proj.reshape(shards, shard_rows, -1)[:, :used, 3 * all_heads :]
    biases = biases.reshape(shards, used, depth, 128).transpose(0, 2, 1, 3)
    biases = biases.reshape(shards, depth, -1)[:, :, : n_head // 4 + n_up]
    biases = biases.transpose(1, 2, 0).astype(wide)
    bias_cross = biases[:, : n_head // 4].reshape(-1)
    bias_up = biases[:, n_head // 4 :].reshape(-1)

    def heads_to_rows(array):
        return jnp.concatenate(spread(row_blocks(array, depth), T), axis=1)

    def to_heads(array):
        return spread(column_blocks(array, depth), T)

    def rows_to_heads(array):
        return jnp.concatenate(to_heads(array), axis=0)

    def owned(gradient):
        return lax.psum_scatter(gradient.astype(low), SHARD, scatter_dimension=0, tiled=True)

    def updated(index, gradient, scale=None):
        old = masters[index], gradient, firsts[index], seconds[index]
        master, first, second = adamw_step(*old, RATES[index], DECAYS[index])
        if scale is not None:
            master = master * scale
        return master, first, second, master.astype(low)

    self_context, self_lse, peaks = self_fwd(queries, kv, meta)
    self_all = heads_to_rows(self_context)
    enc_kv = relay_gather(enc_kv, [self_all])
    own_tokens = pick_rows(tokens, plane, rows).astype(wide)
    hidden_one = own_tokens + contract_cols(self_all, w_out[0]) + vec_all[0]
    normed_one, unit_one, factor_one = normalize(hidden_one, vec_all[3], vec_all[4])
    low_one = normed_one.astype(low)
    cross_queries = rows_to_heads((product(low_one, w_cross) + bias_cross).astype(low))
    holder = plane * groups // depth
    outgoing = []
    for j in range(groups):
        wanted = lax.dynamic_slice_in_dim(near_bases[j], plane * per_slice, per_slice)
        wanted = jnp.clip(wanted // BLK - member * rounds, 0, rounds - 1)
        picked = [pick_rows(cotangent, wanted[i], BLK) for i in range(per_slice)]
        outgoing.append(jnp.concatenate(picked))
    (peaks,) = after([peaks], [cross_queries])
    top_all = jnp.max(peaks.reshape(-1, heads, BLK), axis=(0, 2))
    for axis in (C, F):
        step = 1
        while step < lax.axis_size(axis):
            top_all = jnp.maximum(top_all, swap(top_all, axis, step))
            step *= 2
    enc_kv[3:] = after(enc_kv[3:], [cross_queries, top_all])
    outgoing = after(outgoing, enc_kv[3:])
    incoming = jnp.where(member == holder, outgoing[0], jnp.zeros_like(outgoing[0]))
    for j in range(1, groups):
        pairs = []
        for level in range(depth):
            source = level * groups // depth
            pairs.append((source * depth + level, (source ^ j) * depth + level))
        incoming = incoming + lax.ppermute(outgoing[j], (C, T), pairs)
    cross_context, cross_lse = cross_fwd(cross_queries, enc_kv, seg)
    cross_all = heads_to_rows(cross_context)
    hidden_two = normed_one + contract_cols(cross_all, w_out[1]) + vec_all[1]
    normed_two, unit_two, factor_two = normalize(hidden_two, vec_all[5], vec_all[6])
    low_two = normed_two.astype(low)
    upward = product(low_two, w_one) + bias_up
    below = 0.5 * (1.0 + lax.erf(upward * 0.5**0.5))
    activated = (upward * below).astype(low)
    slope = below + upward * jnp.exp(-0.5 * upward * upward) * (0.5 / jnp.pi) ** 0.5
    hidden_three = normed_two + contract_cols(activated, w_two) + vec_all[2]
    normed_three, unit_three, factor_three = normalize(hidden_three, vec_all[7], vec_all[8])

    grad_three, gain_three, shift_three = normalize_back(
        incoming.astype(wide), unit_three, factor_three, vec_all[7]
    )
    mlp_grad = grad_three.astype(low)
    grad_w_two = contract_rows(mlp_grad, activated).astype(low)
    act_grad = product(after([mlp_grad], [grad_w_two])[0], w_two).astype(low)
    up_grad = (act_grad.astype(wide) * slope).astype(low)
    grad_up_bias = jnp.sum(up_grad.astype(wide), axis=0)
    grad_two, gain_two, shift_two = normalize_back(
        grad_three + contract_cols(up_grad, w_one), unit_two, factor_two, vec_all[5]
    )
    low_grad_two = grad_two.astype(low)
    cross_grads = product(low_grad_two, w_out[1]).astype(low)
    (up_late,) = after([up_grad], [cross_grads])
    grad_w_one = grad_columns([(low_two, up_late)], [], depth)
    cross_grads = rows_to_heads(cross_grads)
    own_down, own_up = owned(grad_w_two), owned(grad_w_one)
    out_rows = from_planes(after([normed_three.astype(low)], [cross_grads])[0])
    saved = seg, cross_grads, cross_context, cross_lse
    cross_q_grad, far, *halves = cross_bwd(
        1, cross_queries, enc_kv, *saved, cross_queries, [grad_w_two, grad_w_one]
    )
    enc_passed = relay_start(*halves)
    cross_q_grad, *enc_terms = cross_bwd(0, cross_queries, enc_kv, *saved, cross_q_grad, [])
    (cross_q_grad,) = after([cross_q_grad], [*out_rows[1:], *enc_passed, own_down])
    (cross_q_all,) = after([heads_to_rows(cross_q_grad)], [own_up])
    grad_one, gain_one, shift_one = normalize_back(
        grad_two + contract_cols(cross_q_all, w_cross), unit_one, factor_one, vec_all[3]
    )
    low_grad_one = grad_one.astype(low)
    self_grads = product(low_grad_one, w_out[0]).astype(low)
    grad_vectors = jnp.stack(
        [
            jnp.sum(grad_one, axis=0),
            jnp.sum(grad_two, axis=0),
            jnp.sum(grad_three, axis=0),
            gain_one,
            shift_one,
            gain_two,
            shift_two,
            gain_three,
            shift_three,
        ]
    )
    vec_part = grad_vectors.reshape(9, shards, -1).transpose(1, 0, 2).reshape(shards, -1)
    up_part = grad_up_bias.reshape(depth, -1, shards).transpose(2, 0, 1)
    small_part = [jnp.concatenate([vec_part, up_part[:, j]], axis=1) for j in range(depth)]
    small_part = jnp.concatenate([by_shard(part, shard_rows) for part in small_part], axis=1)
    self_grads = rows_to_heads(self_grads)
    own_down, own_up = after([own_down, own_up], [self_grads])
    by_plane = by_plane_order([own_up, own_down], plane, depth)
    ffn = lax.psum_scatter(by_plane, T, scatter_dimension=1, tiled=True)
    enc_joined = relay_join([*enc_terms, far], enc_passed, [cross_q_all])
    enc_terms = relay_finish(enc_joined)
    q_grad, *kv_terms = self_bwd(
        queries, kv, meta, self_grads, self_context, self_lse, [*enc_joined[1:], by_plane]
    )
    kv_passed = relay_start(*kv_terms[3:])
    (cross_late,) = after([cross_q_all], [q_grad])
    grad_proj = grad_columns(
        [(low_grad_two, cross_all), (low_grad_one, self_all), (low_one, cross_late)],
        [small_part.astype(low)],
    )
    own_proj = owned(grad_proj)
    enc_grad, enc_columns = sum_terms(enc_terms, [q_grad])

    enc_parts = plane_shares([enc_grad], w_enc, plane, depth, None, [])
    enc_sent = spread(enc_parts, T)
    grad_w_enc = weight_grad(encoder, [enc_grad], [], plane, 512, enc_parts)
    kv_joined = relay_join(kv_terms, kv_passed, [ffn, grad_w_enc])

    out_rows = after(out_rows, kv_joined[1:])
    out_rows = jnp.stack(out_rows)[plane ^ jnp.arange(depth)].reshape(row_count, model_width)
    portion = row_count // groups
    returned = [pick_rows(out_rows, near[j], portion) for j in range(groups)]
    ffn = after([ffn], kv_joined[1:])[0].astype(wide)
    ffn_new = updated(2, ffn[:, :hidden_width]) + updated(3, ffn[:, hidden_width:].T)

    kv_grad, kv_columns = sum_terms(relay_finish(kv_joined), [grad_w_enc, *enc_sent[1:3], *ffn_new, *returned], SOME_COST)
    returned = spread(after(returned, [kv_grad]), C)
    grad_head_bias = jnp.stack(
        [
            jnp.sum(q_grad.astype(wide), axis=0),
            kv_columns[0, head_width:],
            jnp.sum(cross_q_grad.astype(wide), axis=0),
            enc_columns[0, head_width:],
        ]
    )
    head_part = grad_head_bias.reshape(4, -1, shards).transpose(2, 0, 1).reshape(shards, -1)
    head_part = by_shard(head_part, shard_rows).astype(low)
    adds = [head_part, grad_w_enc]
    grad_first = weight_grad(tokens, [q_grad, kv_grad], adds, plane, rows, [], SOME_COST)
    (grad_first,) = after([grad_first], [own_proj])
    token_terms = plane_shares(
        [q_grad, kv_grad], w_kept, plane, depth, grad_one, [grad_first, *enc_sent[3:]], SOME_COST
    )
    token_sent = spread(token_terms, T)
    own_first = owned(grad_first)
    cuts = [0, all_heads, 2 * all_heads, 3 * all_heads, own_proj.shape[1]]
    own_proj = [own_proj[:, a:b] for a, b in zip(cuts, cuts[1:])]
    proj_parts = [column_blocks(part, depth) for part in own_proj]
    proj_parts = [jnp.concatenate([p[j] for p in proj_parts], axis=1) for j in range(depth)]
    own_first, *proj_parts = after([own_first, *proj_parts], token_sent[1:])
    own_first = own_first.astype(wide)
    proj = total(spread(proj_parts, T))
    result = put_blocks(jnp.concatenate(returned), places, wide)
    (token_sent[0],) = after(token_sent[:1], [result])
    grad_tokens = total(token_sent)
    grad_encoder = total(after(enc_sent, [result]))

    out_cross, out_self, in_cross = [
        proj[:, i * head_width : (i + 1) * head_width] for i in range(3)
    ]
    small_part = proj[:, 3 * head_width :].reshape(-1)
    gradients = {
        0: jnp.stack(
            column_blocks(own_first[:, : 3 * head_width], 3)
            + [in_cross]
            + column_blocks(own_first[:, 3 * head_width + 128 :], 2)
        ),
        1: jnp.stack([out_self.T, out_cross.T]),
        4: own_first[:, 3 * head_width : 3 * head_width + 128].reshape(-1)[:n_head].reshape(head_bias.shape),
        5: small_part[n_vec : n_vec + n_up].reshape(up_bias.shape),
        6: small_part[:n_vec].reshape(vectors.shape),
    }
    clip_factor = CLIP_LIMIT / jnp.maximum(top_all, CLIP_LIMIT)
    root_factor = jnp.sqrt(clip_factor)
    column_roots = jnp.repeat(root_factor, HEAD)
    in_scale = jnp.concatenate(
        [column_roots[None], column_roots[None], jnp.ones((4, head_width), wide)], axis=0
    )[:, None, :]
    slot_heads = (jnp.arange(head_bias.shape[1]) * shards + shard_index) // HEAD
    picked = jnp.sum(
        jnp.where(slot_heads[:, None] == jnp.arange(heads)[None, :], root_factor[None, :], 0.0),
        axis=1,
    )
    bias_scale = jnp.concatenate([picked[None], jnp.ones((3, picked.shape[0]), wide)], axis=0)
    scales = {0: in_scale, 4: bias_scale[:, :, None]}
    results = [result, grad_tokens, grad_encoder, clip_factor]
    for index in range(7):
        if index in gradients:
            results += updated(index, gradients[index], scales.get(index))
        else:
            results += ffn_new[4 * (index - 2) : 4 * (index - 1)]
    return tuple(results)


def solution(mesh):
    rows, table = P(SHARD, None), P(F, None)
    weights = (
        P(None, SHARD, T),
        P(None, T, SHARD),
        P(SHARD, T),
        P(T, SHARD),
        P(None, T, SHARD),
        P(T, SHARD),
        P(None, SHARD),
    )
    by_columns = P(SHARD, T)
    updates = tuple(spec for spec in weights for _ in range(4))
    return jax.shard_map(
        per_device,
        mesh=mesh,
        in_specs=(rows, rows, rows, table, table) + weights * 3,
        out_specs=(rows, by_columns, by_columns, P(T)) + updates,
        check_vma=False,
    )
```

```python
from functools import partial, reduce

import jax
import jax.numpy as jnp
from jax import lax
from jax.experimental import pallas as pl
from jax.experimental.pallas import tpu as pltpu
from jax.sharding import PartitionSpec as P

HEAD = 64
ENC = 4096
STEP = 10
BLK = 128

NEGATIVE = -1e30
NORM_EPS = 1e-05
ADAM_EPS = 1e-08
BETA = 0.5
CLIP_LIMIT = 10.0
RATES = (0.05, 0.3, 0.05, 0.03, 0.3, 0.3, 0.3)
DECAYS = (0.1, 0.1, 0.1, 0.1, 0.0, 0.0, 0.0)
SCALE = HEAD ** (-0.5)
VMEM_BYTES = 56 * 1024 * 1024
F, C, T = "fsdp", "context", "tensor"
SHARD = (F, C)
NO_COST = pl.CostEstimate(flops=0, bytes_accessed=0, transcendentals=0)
SOME_COST = pl.CostEstimate(flops=2 * 10**10, bytes_accessed=2**25, transcendentals=0)


def product(left_side, right_side):
    return jnp.dot(left_side, right_side, preferred_element_type=jnp.float32)


def contract_rows(left_side, right_side):
    return lax.dot_general(
        left_side, right_side, (((0,), (0,)), ((), ())), preferred_element_type=jnp.float32
    )


def contract_cols(left_side, right_side):
    return lax.dot_general(
        left_side, right_side, (((1,), (1,)), ((), ())), preferred_element_type=jnp.float32
    )


def stack_heads(block, heads):
    lanes = lax.broadcasted_iota(jnp.int32, block.shape, 1) // HEAD
    zero = jnp.zeros_like(block)
    return jnp.concatenate([jnp.where(lanes == h, block, zero) for h in range(heads)], axis=0)


def merge_heads(stacked, heads):
    rows = stacked.shape[0] // heads
    lanes = lax.broadcasted_iota(jnp.int32, (rows, stacked.shape[1]), 1) // HEAD
    merged = stacked[:rows]
    for h in range(1, heads):
        merged = jnp.where(lanes == h, stacked[h * rows : (h + 1) * rows], merged)
    return merged


def col_to_row(column):
    return jnp.transpose(jnp.broadcast_to(column, (column.shape[0], 128)))[0:1]


def fold_lanes(tile, combine):
    return reduce(combine, [tile[:, j : j + 128] for j in range(0, tile.shape[1], 128)])


def whole(shape):
    return pl.BlockSpec(shape, lambda i, s: (0,) * len(shape), pipeline_mode=pl.Buffered(1))


def fetch_kv(sources, places, sems):
    copies = [
        pltpu.make_async_copy(source, place, sems.at[i])
        for i, (source, place) in enumerate(zip(sources, places))
    ]

    @pl.when(pl.program_id(0) == 0)
    def _():
        for copy in copies:
            copy.start()
        for copy in copies:
            copy.wait()


def piece_bounds(pieces):
    full, half = pieces[0].shape[0], pieces[3].shape[0]
    return [(0, 0, full), (1, 0, full), (2, 0, full), (3, 0, half), (3, half, half)]


def member_rows(order_ref, row, bounds, full):
    return [
        pl.ds(pl.multiple_of(order_ref[row, j] * full + start, size), size)
        for j, start, size in bounds
    ]


def gate_body(*refs):
    pass


def after(values, others):
    count, every = len(values), [*values, *others]
    return pl.pallas_call(
        gate_body,
        in_specs=[pl.BlockSpec(memory_space=pl.ANY)] * len(every),
        out_specs=[pl.BlockSpec(memory_space=pl.ANY)] * count,
        out_shape=[jax.ShapeDtypeStruct(value.shape, value.dtype) for value in values],
        input_output_aliases={i: i for i in range(count)},
        cost_estimate=NO_COST,
        name="gate",
    )(*every)


def cross_fwd_body(heads, bounds, seg_ref, q_ref, *refs):
    sources, (o_ref, lse_ref, kv_ref, s_ref, sems) = refs[: len(bounds)], refs[len(bounds) :]
    places = member_rows(seg_ref, 3, bounds, sources[0].shape[0])
    fetch_kv(sources, [kv_ref.at[place] for place in places], sems)
    block = pl.program_id(0)
    low, high, cut = seg_ref[0, block], seg_ref[1, block], seg_ref[2, block]
    queries = stack_heads(q_ref[...] * jnp.bfloat16(SCALE), heads)
    rows, width = queries.shape
    tiles, _, step = s_ref.shape

    def attend(sequence):
        def scores(t, highest):
            at = pl.ds(pl.multiple_of(sequence * ENC + t * step, step), step)
            tile = contract_cols(queries, kv_ref[at, :width])
            s_ref[t] = tile
            return jnp.maximum(highest, fold_lanes(tile, jnp.maximum))

        highest = lax.fori_loop(0, tiles, scores, jnp.full((rows, 128), NEGATIVE, jnp.float32))
        peak = jnp.max(highest, axis=1, keepdims=True)

        def weigh(t, running):
            total, summed = running
            at = pl.ds(pl.multiple_of(sequence * ENC + t * step, step), step)
            weights = jnp.exp(s_ref[t] - peak)
            summed = summed + product(weights.astype(jnp.bfloat16), kv_ref[at, width:])
            return total + fold_lanes(weights, jnp.add), summed

        total, summed = lax.fori_loop(
            0,
            tiles,
            weigh,
            (jnp.zeros((rows, 128), jnp.float32), jnp.zeros((rows, width), jnp.float32)),
        )
        total = jnp.sum(total, axis=1, keepdims=True)
        merged = merge_heads(summed / total, heads)
        lse = col_to_row(peak + jnp.log(total))
        place = lax.broadcasted_iota(jnp.int32, merged.shape, 0)
        own = jnp.where(place >= cut, 1, 0) == sequence
        o_ref[...] = jnp.where(own, merged, o_ref[...].astype(jnp.float32)).astype(o_ref.dtype)
        place = lax.broadcasted_iota(jnp.int32, lse.shape, 1) % BLK
        own = jnp.where(place >= cut, 1, 0) == sequence
        lse_ref[0] = jnp.where(own, lse, lse_ref[0])

    o_ref[...] = jnp.zeros_like(o_ref)
    lse_ref[...] = jnp.zeros_like(lse_ref)
    pl.loop(low, high + 1)(attend)


def cross_fwd(queries, enc_kv, seg):
    count, width = queries.shape
    heads, blocks, step = width // HEAD, count // BLK, 1024
    rows, bounds = heads * BLK, piece_bounds(enc_kv)
    enc_all = sum(piece.shape[0] for piece in enc_kv)
    return pl.pallas_call(
        partial(cross_fwd_body, heads, bounds),
        grid_spec=pltpu.PrefetchScalarGridSpec(
            num_scalar_prefetch=1,
            grid=(blocks,),
            in_specs=[pl.BlockSpec((BLK, width), lambda i, s: (i, 0))]
            + [pl.BlockSpec(memory_space=pl.ANY)] * len(bounds),
            out_specs=[
                pl.BlockSpec((BLK, width), lambda i, s: (i, 0)),
                pl.BlockSpec((1, 1, rows), lambda i, s: (i, 0, 0)),
            ],
            scratch_shapes=[
                pltpu.VMEM((enc_all, 2 * width), jnp.bfloat16),
                pltpu.VMEM((ENC // step, rows, step), jnp.float32),
                pltpu.SemaphoreType.DMA((len(bounds),)),
            ],
        ),
        out_shape=[
            jax.ShapeDtypeStruct((count, width), jnp.bfloat16),
            jax.ShapeDtypeStruct((blocks, 1, rows), jnp.float32),
        ],
        compiler_params=pltpu.CompilerParams(vmem_limit_bytes=VMEM_BYTES),
        cost_estimate=NO_COST,
        name="cross_fwd",
    )(seg, queries, *enc_kv)


def cross_bwd_body(heads, bounds, kind, step, seg_ref, q_ref, g_ref, o_ref, lse_ref, *refs):
    count, outs = len(bounds), refs[-len(bounds) - 4 : -3]
    sources, prior, (dq_ref, *outs) = refs[:count], refs[count], outs
    kv_ref, acc_ref, sems = refs[-3:]
    block = pl.program_id(0)
    sequence, full = seg_ref[4, kind], ENC // 2
    places = [
        pl.ds(pl.multiple_of(seg_ref[3, j] * full + at - sequence * ENC, size), size)
        for j, at, size in bounds
    ]
    fetch_kv(sources, [kv_ref.at[place] for place in places], sems)

    @pl.when(block == 0)
    def _():
        acc_ref[...] = jnp.zeros_like(acc_ref)

    seen = (seg_ref[0, block] <= sequence) & (seg_ref[1, block] >= sequence)
    start = prior[...] if kind == 0 else jnp.zeros_like(dq_ref)
    dq_ref[...] = start

    @pl.when(seen)
    def _():
        queries = stack_heads(q_ref[...] * jnp.bfloat16(SCALE), heads)
        rows, width = queries.shape
        grads = stack_heads(g_ref[...], heads)
        dots = g_ref[...].astype(jnp.float32) * o_ref[...].astype(jnp.float32)
        dot_row = col_to_row(jnp.sum(stack_heads(dots, heads), axis=1, keepdims=True))
        place = lax.broadcasted_iota(jnp.int32, lse_ref[0].shape, 1) % BLK
        own_seq = jnp.where(place >= seg_ref[2, block], 1, 0)
        lse = jnp.where(own_seq == sequence, lse_ref[0], -NEGATIVE)

        def tile_terms(t, q_grad):
            at = pl.ds(pl.multiple_of(t * step, step), step)
            keys, values = kv_ref[at, :width], kv_ref[at, width:]
            probs = jnp.exp(contract_cols(keys, queries) - lse)
            s_grad = (probs * (contract_cols(values, grads) - dot_row)).astype(jnp.bfloat16)
            acc_ref[at, width:] += product(probs.astype(jnp.bfloat16), grads)
            acc_ref[at, :width] += product(s_grad, queries)
            return q_grad + contract_rows(s_grad, keys)

        q_grad = lax.fori_loop(
            0, ENC // step, tile_terms, jnp.zeros((rows, width), jnp.float32)
        )
        q_grad = merge_heads(q_grad, heads) * SCALE + start.astype(jnp.float32)
        dq_ref[...] = q_grad.astype(dq_ref.dtype)

    @pl.when(block == pl.num_programs(0) - 1)
    def _():
        for out, place in zip(outs, places):
            out[...] = acc_ref[place, :].astype(out.dtype)


def cross_bwd(kind, queries, enc_kv, seg, grads, context, lse, prior, others):
    count, width = queries.shape
    heads, blocks, step = width // HEAD, count // BLK, 2048
    bounds = piece_bounds(enc_kv)
    picked = [(0, 1), (2, 3, 4)][kind]
    pieces, bounds = [enc_kv[i] for i in picked], [bounds[i] for i in picked]
    row = pl.BlockSpec((BLK, width), lambda i, s: (i, 0))
    return pl.pallas_call(
        partial(cross_bwd_body, heads, bounds, kind, step),
        grid_spec=pltpu.PrefetchScalarGridSpec(
            num_scalar_prefetch=1,
            grid=(blocks,),
            in_specs=[row, row, row, pl.BlockSpec((1, 1, heads * BLK), lambda i, s: (i, 0, 0))]
            + [pl.BlockSpec(memory_space=pl.ANY)] * len(bounds)
            + [row]
            + [pl.BlockSpec(memory_space=pl.ANY)] * len(others),
            out_specs=[row] + [whole(piece.shape) for piece in pieces],
            scratch_shapes=[
                pltpu.VMEM((ENC, 2 * width), jnp.bfloat16),
                pltpu.VMEM((ENC, 2 * width), jnp.float32),
                pltpu.SemaphoreType.DMA((len(bounds),)),
            ],
        ),
        out_shape=[jax.ShapeDtypeStruct((count, width), jnp.bfloat16)]
        + [jax.ShapeDtypeStruct(piece.shape, jnp.bfloat16) for piece in pieces],
        compiler_params=pltpu.CompilerParams(vmem_limit_bytes=VMEM_BYTES),
        cost_estimate=NO_COST,
        name="cross_bwd",
    )(seg, queries, grads, context, lse, *pieces, prior, *others)


def gather_tile(kv_ref, t, columns):
    at = pl.ds(pl.multiple_of(t * BLK, BLK), BLK)
    return jnp.concatenate([kv_ref[j, at, columns] for j in range(kv_ref.shape[0])], axis=0)


def self_fwd_body(heads, bounds, meta_ref, q_ref, *refs):
    sources, (o_ref, lse_ref, top_ref, kv_refs, sems) = refs[: len(bounds)], refs[len(bounds) :]
    fetch_kv(sources, [kv_refs.at[j, pl.ds(at, size)] for j, at, size in bounds], sems)
    groups = kv_refs.shape[0]
    block = pl.program_id(0)
    base, first, last = [meta_ref[groups + k, block] for k in range(3)]
    cut = meta_ref[groups + 3, 0]
    queries = stack_heads(q_ref[...] * jnp.bfloat16(SCALE), heads)
    rows, width = queries.shape
    q_pos = base + lax.broadcasted_iota(jnp.int32, (rows, BLK), 0) % BLK
    q_start = jnp.where(q_pos >= cut, cut, 0)
    lane = lax.broadcasted_iota(jnp.int32, (rows, BLK), 1)

    def visit(t, running):
        peak, total, summed = running
        raw = contract_cols(queries, gather_tile(kv_refs, t, slice(0, width)))
        parts = []
        for d in range(groups):
            k_pos = lane + meta_ref[d, t]
            seen = (k_pos <= q_pos) & (k_pos >= q_start)
            parts.append(jnp.where(seen, raw[:, d * BLK : (d + 1) * BLK], NEGATIVE))
        new_peak = jnp.maximum(peak, jnp.max(reduce(jnp.maximum, parts), axis=1, keepdims=True))
        weights = [jnp.exp(part - new_peak) for part in parts]
        shrink = jnp.exp(peak - new_peak)
        total = total * shrink + jnp.sum(reduce(jnp.add, weights), axis=1, keepdims=True)
        low_weights = jnp.concatenate(weights, axis=1).astype(jnp.bfloat16)
        values = gather_tile(kv_refs, t, slice(width, 2 * width))
        return new_peak, total, summed * shrink + product(low_weights, values)

    peak, total, summed = lax.fori_loop(
        first,
        last + 1,
        visit,
        (
            jnp.full((rows, 1), NEGATIVE, jnp.float32),
            jnp.zeros((rows, 1), jnp.float32),
            jnp.zeros((rows, width), jnp.float32),
        ),
    )
    o_ref[...] = merge_heads(summed / total, heads).astype(o_ref.dtype)
    lse_ref[0] = col_to_row(peak + jnp.log(total))
    top_ref[0] = col_to_row(peak)


def self_fwd(queries, kv, meta):
    count, width = queries.shape
    heads, blocks, bounds = width // HEAD, count // BLK, piece_bounds(kv)
    rows, kept = heads * BLK, (bounds[-1][0] + 1,) + kv[0].shape
    row = pl.BlockSpec((BLK, width), lambda i, s: (i, 0))
    stat = pl.BlockSpec((1, 1, rows), lambda i, s: (i, 0, 0))
    return pl.pallas_call(
        partial(self_fwd_body, heads, bounds),
        grid_spec=pltpu.PrefetchScalarGridSpec(
            num_scalar_prefetch=1,
            grid=(blocks,),
            in_specs=[row] + [pl.BlockSpec(memory_space=pl.ANY)] * len(bounds),
            out_specs=[row, stat, stat],
            scratch_shapes=[
                pltpu.VMEM(kept, jnp.bfloat16),
                pltpu.SemaphoreType.DMA((len(bounds),)),
            ],
        ),
        out_shape=[jax.ShapeDtypeStruct((count, width), jnp.bfloat16)]
        + [jax.ShapeDtypeStruct((blocks, 1, rows), jnp.float32)] * 2,
        compiler_params=pltpu.CompilerParams(vmem_limit_bytes=VMEM_BYTES),
        cost_estimate=NO_COST,
        name="self_fwd",
    )(meta, queries, *kv)


def self_bwd_body(heads, bounds, waits, meta_ref, q_ref, g_ref, o_ref, lse_ref, *refs):
    count = len(bounds)
    sources, (dq_ref, *outs) = refs[:count], refs[count + waits : 2 * count + waits + 1]
    kv_refs, acc_ref, sems = refs[2 * count + waits + 1 :]
    fetch_kv(sources, [kv_refs.at[j, pl.ds(at, size)] for j, at, size in bounds], sems)
    groups = kv_refs.shape[0]
    block = pl.program_id(0)

    @pl.when(block == 0)
    def _():
        acc_ref[...] = jnp.zeros_like(acc_ref)

    base, first, last = [meta_ref[groups + k, block] for k in range(3)]
    cut = meta_ref[groups + 3, 0]
    queries = stack_heads(q_ref[...] * jnp.bfloat16(SCALE), heads)
    rows, width = queries.shape
    grads = stack_heads(g_ref[...], heads)
    dots = g_ref[...].astype(jnp.float32) * o_ref[...].astype(jnp.float32)
    dot_row = col_to_row(jnp.sum(stack_heads(dots, heads), axis=1, keepdims=True))
    lse = lse_ref[0]
    q_pos = base + lax.broadcasted_iota(jnp.int32, lse.shape, 1) % BLK
    q_start = jnp.where(q_pos >= cut, cut, 0)
    sub = lax.broadcasted_iota(jnp.int32, (BLK, rows), 0)

    def tile_terms(t, q_grad):
        at = pl.ds(pl.multiple_of(t * BLK, BLK), BLK)
        keys = gather_tile(kv_refs, t, slice(0, width))
        values = gather_tile(kv_refs, t, slice(width, 2 * width))
        raw = contract_cols(keys, queries)
        parts = []
        for d in range(groups):
            k_base = meta_ref[d, t]
            seen = (sub <= q_pos - k_base) & (sub >= q_start - k_base)
            parts.append(jnp.where(seen, jnp.exp(raw[d * BLK : (d + 1) * BLK] - lse), 0.0))
        probs = jnp.concatenate(parts, axis=0)
        s_grad = (probs * (contract_cols(values, grads) - dot_row)).astype(jnp.bfloat16)
        acc_ref[:, at, width:] += product(probs.astype(jnp.bfloat16), grads).reshape(
            groups, BLK, width
        )
        acc_ref[:, at, :width] += product(s_grad, queries).reshape(groups, BLK, width)
        return q_grad + contract_rows(s_grad, keys)

    q_grad = lax.fori_loop(first, last + 1, tile_terms, jnp.zeros((rows, width), jnp.float32))
    dq_ref[...] = (merge_heads(q_grad, heads) * SCALE).astype(dq_ref.dtype)

    @pl.when(block == pl.num_programs(0) - 1)
    def _():
        for out, (j, at, size) in zip(outs, bounds):
            out[...] = acc_ref[j, at : at + size].astype(out.dtype)


def self_bwd(queries, kv, meta, grads, context, lse, others):
    count, width = queries.shape
    heads, blocks, bounds = width // HEAD, count // BLK, piece_bounds(kv)
    rows, kept = heads * BLK, (bounds[-1][0] + 1,) + kv[0].shape
    row = pl.BlockSpec((BLK, width), lambda i, s: (i, 0))
    stat = pl.BlockSpec((1, 1, rows), lambda i, s: (i, 0, 0))
    return pl.pallas_call(
        partial(self_bwd_body, heads, bounds, len(others)),
        grid_spec=pltpu.PrefetchScalarGridSpec(
            num_scalar_prefetch=1,
            grid=(blocks,),
            in_specs=[row, row, row, stat]
            + [pl.BlockSpec(memory_space=pl.ANY)] * (len(bounds) + len(others)),
            out_specs=[row] + [whole(piece.shape) for piece in kv],
            scratch_shapes=[
                pltpu.VMEM(kept, jnp.bfloat16),
                pltpu.VMEM(kept, jnp.float32),
                pltpu.SemaphoreType.DMA((len(bounds),)),
            ],
        ),
        out_shape=[jax.ShapeDtypeStruct((count, width), jnp.bfloat16)]
        + [jax.ShapeDtypeStruct(piece.shape, jnp.bfloat16) for piece in kv],
        compiler_params=pltpu.CompilerParams(vmem_limit_bytes=VMEM_BYTES),
        cost_estimate=NO_COST,
        name="self_bwd",
    )(meta, queries, grads, context, lse, *kv, *others)


def move_body(index_ref, in_ref, out_ref):
    out_ref[...] = in_ref[...].astype(out_ref.dtype)


def put_blocks(rows, index, dtype):
    count, width = rows.shape
    return pl.pallas_call(
        move_body,
        grid_spec=pltpu.PrefetchScalarGridSpec(
            num_scalar_prefetch=1,
            grid=(count // BLK,),
            in_specs=[pl.BlockSpec((BLK, width), lambda i, s: (i, 0))],
            out_specs=pl.BlockSpec((BLK, width), lambda i, s: (s[i], 0)),
        ),
        out_shape=jax.ShapeDtypeStruct((count, width), dtype),
        cost_estimate=SOME_COST,
        name="put_blocks",
    )(index, rows)


def join_body(whole_ref, passed_ref, *refs):
    total = whole_ref[...].astype(jnp.float32) + passed_ref[...].astype(jnp.float32)
    refs[-1][...] = total.astype(refs[-1].dtype)


def add_half(whole_rows, passed, lower, others):
    half, width = passed.shape
    size = min(half, 256)
    first = half // size if lower else 0
    part = pl.BlockSpec((size, width), lambda i: (first + i, 0))
    return pl.pallas_call(
        join_body,
        grid=(half // size,),
        in_specs=[part, pl.BlockSpec((size, width), lambda i: (i, 0))]
        + [pl.BlockSpec(memory_space=pl.ANY)] * len(others),
        out_specs=part,
        out_shape=jax.ShapeDtypeStruct(whole_rows.shape, whole_rows.dtype),
        input_output_aliases={0: 0},
        cost_estimate=NO_COST,
        name="add_half",
    )(whole_rows, passed, *others)


def grad_body(count, *refs):
    out_ref, start = refs[-1], 0
    for k in range(count):
        terms = contract_rows(refs[2 * k][...], refs[2 * k + 1][...])
        out_ref[:, start : start + terms.shape[1]] = terms.astype(out_ref.dtype)
        start += terms.shape[1]
    for ref in refs[2 * count : -1]:
        out_ref[:, start : start + ref.shape[1]] = ref[...]
        start += ref.shape[1]


def grad_columns(pairs, others, tiles=1):
    flat = [array for pair in pairs for array in pair]
    width = pairs[0][0].shape[1]
    columns = sum(right.shape[1] for _, right in pairs) + sum(array.shape[1] for array in others)
    size = pairs[0][1].shape[0]
    if tiles == 1:
        specs = [pl.BlockSpec(array.shape, lambda i: (0, 0)) for array in flat + others]
    else:
        specs = [
            pl.BlockSpec((size, width), lambda i: (0, 0)),
            pl.BlockSpec((size, columns // tiles), lambda i: (0, i)),
        ]
    return pl.pallas_call(
        partial(grad_body, len(pairs)),
        grid=(tiles,),
        in_specs=specs,
        out_specs=pl.BlockSpec((width, columns // tiles), lambda i: (0, i)),
        out_shape=jax.ShapeDtypeStruct((width, columns), jnp.bfloat16),
        compiler_params=pltpu.CompilerParams(vmem_limit_bytes=VMEM_BYTES),
        cost_estimate=NO_COST,
        name="grad_columns",
    )(*flat, *others)


def plane_body(plane_ref, *refs):
    start = 0
    for ref in refs[:-1]:
        refs[-1][:, start : start + ref.shape[1]] = ref[...]
        start += ref.shape[1]


def by_plane_order(arrays, plane, depth):
    size = arrays[0].shape[0]
    widths = [array.shape[1] // depth for array in arrays]
    return pl.pallas_call(
        plane_body,
        grid_spec=pltpu.PrefetchScalarGridSpec(
            num_scalar_prefetch=1,
            grid=(depth,),
            in_specs=[pl.BlockSpec((size, width), lambda p, s: (0, s[0] ^ p)) for width in widths],
            out_specs=pl.BlockSpec((size, sum(widths)), lambda p, s: (0, p)),
        ),
        out_shape=jax.ShapeDtypeStruct((size, depth * sum(widths)), arrays[0].dtype),
        cost_estimate=NO_COST,
        name="by_plane_order",
    )(plane.reshape(1).astype(jnp.int32), *arrays)


ANYWHERE = pl.BlockSpec(memory_space=pl.ANY)


def sum_body(count, *refs):
    out_ref, column_ref = refs[-2:]
    added = reduce(jnp.add, [ref[...].astype(jnp.float32) for ref in refs[:count]])
    rounded = added.astype(out_ref.dtype)
    out_ref[...] = rounded

    @pl.when(pl.program_id(0) == 0)
    def _():
        column_ref[...] = jnp.zeros_like(column_ref)

    column_ref[...] += jnp.sum(rounded.astype(jnp.float32), axis=0, keepdims=True)


def sum_terms(terms, others, cost=SOME_COST):
    count, width = terms[0].shape
    size = 256
    tile = pl.BlockSpec((size, width), lambda i: (i, 0))
    return pl.pallas_call(
        partial(sum_body, len(terms)),
        grid=(count // size,),
        in_specs=[tile] * len(terms) + [ANYWHERE] * len(others),
        out_specs=[tile, pl.BlockSpec((1, width), lambda i: (0, 0))],
        out_shape=[
            jax.ShapeDtypeStruct((count, width), jnp.bfloat16),
            jax.ShapeDtypeStruct((1, width), jnp.float32),
        ],
        cost_estimate=cost,
        name="sum_terms",
    )(*terms, *others)


def share_body(depth, parts, extra, plane_ref, *refs):
    rows = [ref[...] for ref in refs[:parts]]
    merged = rows[0] if parts == 1 else jnp.concatenate(rows, axis=1)
    own = pl.program_id(0) == plane_ref[0]
    for j in range(depth):
        term = contract_cols(merged, refs[parts + j][...])
        if extra:
            term = term + jnp.where(own, refs[parts + depth + j][...], 0.0)
        refs[len(refs) - depth + j][...] = term.astype(jnp.bfloat16)


def plane_shares(arrays, weight, plane, depth, extra, others, cost=SOME_COST):
    count, size = arrays[-1].shape[0], 256 if extra is None else extra.shape[0]
    part = weight.shape[0] // depth
    last = pl.BlockSpec((size, arrays[-1].shape[1]), lambda i, s: (i, 0))
    specs = [last]
    if len(arrays) == 2:
        specs = [pl.BlockSpec((size, arrays[0].shape[1]), lambda i, s: (s[0] ^ i, 0)), last]
    for j in range(depth):
        specs.append(
            pl.BlockSpec((part, weight.shape[1]), partial(lambda j, i, s: (s[0] ^ j, 0), j))
        )
    inputs = [*arrays, *[weight] * depth]
    if extra is not None:
        for j in range(depth):
            specs.append(pl.BlockSpec((size, part), partial(lambda j, i, s: (0, s[0] ^ j), j)))
        inputs += [extra] * depth
    return pl.pallas_call(
        partial(share_body, depth, len(arrays), extra is not None),
        grid_spec=pltpu.PrefetchScalarGridSpec(
            num_scalar_prefetch=1,
            grid=(count // size,),
            in_specs=specs + [ANYWHERE] * len(others),
            out_specs=[pl.BlockSpec((size, part), lambda i, s: (i, 0))] * depth,
        ),
        out_shape=[jax.ShapeDtypeStruct((count, part), jnp.bfloat16)] * depth,
        compiler_params=pltpu.CompilerParams(vmem_limit_bytes=VMEM_BYTES),
        cost_estimate=cost,
        name="plane_shares",
    )(plane.reshape(1).astype(jnp.int32), *inputs, *others)


def gather_grad_body(parts, adds, plane_ref, left_ref, *refs):
    out_ref, acc_ref = refs[-2:]
    step = pl.program_id(0)

    @pl.when(step == 0)
    def _():
        acc_ref[...] = jnp.zeros_like(acc_ref)

    start = 0
    for ref in refs[:parts]:
        stop = start + ref.shape[1]
        acc_ref[:, start:stop] += contract_rows(left_ref[...], ref[...])
        start = stop

    @pl.when(step == pl.num_programs(0) - 1)
    def _():
        out_ref[:, :start] = acc_ref[...].astype(out_ref.dtype)
        at = start
        for ref in refs[parts : parts + adds]:
            out_ref[:, at : at + ref.shape[1]] = ref[...]
            at += ref.shape[1]


def weight_grad(left, arrays, adds, plane, size, others, cost=SOME_COST):
    count, width = left.shape
    last = pl.BlockSpec((size, arrays[-1].shape[1]), lambda i, s: (i, 0))
    specs = [pl.BlockSpec((size, width), lambda i, s: (i, 0)), last]
    if len(arrays) == 2:
        specs.insert(1, pl.BlockSpec((size, arrays[0].shape[1]), lambda i, s: (s[0] ^ i, 0)))
    made = sum(array.shape[1] for array in arrays)
    columns = made + sum(array.shape[1] for array in adds)
    specs += [whole(array.shape) for array in adds] + [ANYWHERE] * len(others)
    return pl.pallas_call(
        partial(gather_grad_body, len(arrays), len(adds)),
        grid_spec=pltpu.PrefetchScalarGridSpec(
            num_scalar_prefetch=1,
            grid=(count // size,),
            in_specs=specs,
            out_specs=pl.BlockSpec((width, columns), lambda i, s: (0, 0)),
            scratch_shapes=[pltpu.VMEM((width, made), jnp.float32)],
        ),
        out_shape=jax.ShapeDtypeStruct((width, columns), jnp.bfloat16),
        compiler_params=pltpu.CompilerParams(vmem_limit_bytes=VMEM_BYTES),
        cost_estimate=cost,
        name="weight_grad",
    )(plane.reshape(1).astype(jnp.int32), left, *arrays, *adds, *others)


def normalize(hidden, gain_row, shift_row):
    centred = hidden - jnp.mean(hidden, axis=-1, keepdims=True)
    factor = lax.rsqrt(jnp.mean(centred * centred, axis=-1, keepdims=True) + NORM_EPS)
    unit_rows = centred * factor
    return (unit_rows * gain_row + shift_row, unit_rows, factor)


def normalize_back(incoming, unit_rows, factor, gain_row):
    scaled = incoming * gain_row
    centred_grad = (
        scaled
        - jnp.mean(scaled, axis=-1, keepdims=True)
        - unit_rows * jnp.mean(scaled * unit_rows, axis=-1, keepdims=True)
    )
    return (factor * centred_grad, jnp.sum(incoming * unit_rows, axis=0), jnp.sum(incoming, axis=0))


def adamw_step(master, gradient, first_moment, second_moment, step_rate, weight_decay):
    first_moment = BETA * first_moment + (1.0 - BETA) * gradient
    second_moment = BETA * second_moment + (1.0 - BETA) * gradient * gradient
    correction = 1.0 - BETA**STEP
    update = first_moment / correction / (jnp.sqrt(second_moment / correction) + ADAM_EPS)
    return (master - step_rate * (update + weight_decay * master), first_moment, second_moment)
def swap(value, axis, j):
    return lax.ppermute(value, axis, [(i, i ^ j) for i in range(lax.axis_size(axis))])


def spread(blocks, axis):
    return [blocks[0]] + [swap(blocks[j], axis, j) for j in range(1, len(blocks))]


def total(blocks):
    return reduce(jnp.add, [block.astype(jnp.float32) for block in blocks])


def column_blocks(array, count):
    size = array.shape[1] // count
    return [array[:, j * size : (j + 1) * size] for j in range(count)]


def row_blocks(array, count):
    size = array.shape[0] // count
    return [array[j * size : (j + 1) * size] for j in range(count)]


def pick_rows(array, index, size):
    return lax.dynamic_slice_in_dim(array, index * size, size, 0)


def by_shard(flat, shard_rows):
    shards, used = flat.shape
    flat = jnp.pad(flat, ((0, 0), (0, -used % 128))).reshape(shards, -1, 128)
    return jnp.pad(flat, ((0, 0), (0, shard_rows - flat.shape[1]), (0, 0))).reshape(-1, 128)


def relay_gather(block, others=()):
    near, far = swap(block, C, 1), swap(block, C, 2)
    if others:
        near, far = after([near, far], others)
    half = block.shape[0] // 2
    return [block, near, far, swap(far[:half], C, 1), swap(near[half:], C, 2)]


def relay_start(upper, lower):
    return swap(upper, C, 1), swap(lower, C, 2)


def relay_join(terms, passed, others=()):
    own, near, far = terms[:3]
    return own, add_half(near, passed[1], True, others), add_half(far, passed[0], False, others)


def relay_finish(joined):
    own, near, far = joined
    return [own, swap(near, C, 1), swap(far, C, 2)]


def per_device(tokens, encoder, cotangent, lengths, order, *params):
    masters, firsts, seconds = params[:7], params[7:14], params[14:]
    in_proj, out_proj, w_up, w_down, head_bias, up_bias, vectors = masters
    low, wide = jnp.bfloat16, jnp.float32
    groups, member = lax.axis_size(C), lax.axis_index(C)
    depth, plane = lax.axis_size(T), lax.axis_index(T)
    shards, shard_index = lax.axis_size(SHARD), lax.axis_index(SHARD)
    row_count, model_width = tokens.shape
    head_width, hidden_width = in_proj.shape[2], w_up.shape[1]
    heads = head_width // HEAD
    shard_rows = in_proj.shape[1]
    rounds = row_count // BLK
    rows = row_count // depth
    per_slice, per_member = rows // BLK, rounds // groups
    all_heads, all_hidden = depth * head_width, depth * hidden_width

    n_vec, n_head, n_up = vectors.size, head_bias.size, up_bias.size
    small = jnp.concatenate([vectors.reshape(-1), head_bias.reshape(-1)])
    first_part = jnp.concatenate(
        [in_proj[0], in_proj[1], in_proj[2], by_shard(small[None], shard_rows)], axis=1
    )
    first_part = lax.all_gather(first_part.astype(low), SHARD, axis=0, tiled=True)
    biases = jnp.concatenate([head_bias[2].reshape(-1), up_bias.reshape(-1)])
    proj_pack = jnp.concatenate(
        [out_proj[0].T, out_proj[1].T, in_proj[3], by_shard(biases[None], shard_rows)], axis=1
    ).astype(low)
    ffn_pack = jnp.concatenate([w_up, w_down.T], axis=1).astype(low)

    def from_planes(array):
        return [array] + [swap(array, T, j) for j in range(1, depth)]

    proj_packs = from_planes(proj_pack)
    w_enc = jnp.concatenate([in_proj[4], in_proj[5]], axis=1).astype(low)
    (w_enc,) = after([w_enc], proj_packs[1:])
    w_enc = lax.all_gather(w_enc, SHARD, axis=0, tiled=True)
    w_self = first_part[:, : 3 * head_width]
    used = -(-(n_vec + n_head) // 128)
    small = first_part.reshape(shards, shard_rows, -1)[:, :used, 3 * head_width :]
    small = small.reshape(shards, -1)
    vec_all = small[:, :n_vec].reshape(shards, 9, -1).transpose(1, 0, 2).reshape(9, -1)
    vec_all = vec_all.astype(wide)

    def by_columns(flat, count):
        return flat.reshape(shards, count, -1).transpose(1, 2, 0).reshape(count, -1).astype(wide)

    bias_heads = by_columns(small[:, n_vec : n_vec + n_head], 4)

    bases = order[0].reshape(groups, rounds, BLK)[:, :, 0]
    cut = lengths[0, 0]
    near = member ^ jnp.arange(groups)
    spot = jnp.arange(rounds)
    q_rounds = (plane ^ (spot // per_slice)) * per_slice + spot % per_slice
    q_bases = jnp.take(lax.dynamic_index_in_dim(bases, member, 0, keepdims=False), q_rounds)
    seg = jnp.stack(
        [
            (q_bases >= cut).astype(jnp.int32),
            (q_bases + BLK - 1 >= cut).astype(jnp.int32),
            jnp.clip(cut - q_bases, 0, BLK),
            jnp.pad(near, (0, rounds - groups)),
            (member * encoder.shape[0] // ENC) ^ jnp.minimum(spot, 1),
        ]
    ).astype(jnp.int32)
    near_bases = jnp.take(bases, near, axis=0)
    meta = jnp.concatenate(
        [
            near_bases,
            q_bases[None],
            jnp.where(q_bases >= cut, cut // (groups * BLK), 0)[None],
            q_rounds[None],
            jnp.full((1, rounds), cut),
        ],
        axis=0,
    ).astype(jnp.int32)
    places = (
        lax.dynamic_slice_in_dim(near_bases, member * per_member, per_member, 1) // BLK
        - member * rounds
    ).reshape(-1)

    qkv = product(tokens, w_self)
    queries = (qkv[:, :head_width] + bias_heads[0]).astype(low)
    queries = jnp.concatenate([pick_rows(queries, plane ^ j, rows) for j in range(depth)])
    no_bias = jnp.zeros((head_width,), wide)
    kv = (qkv[:, head_width:] + jnp.concatenate([no_bias, bias_heads[1]])).astype(low)
    kv = relay_gather(kv)
    ffn_packs = from_planes(after([ffn_pack], kv[:1])[0])
    (w_enc,) = after([w_enc], kv[:1])
    enc_kv = product(encoder, w_enc) + jnp.concatenate([no_bias, bias_heads[3]])
    enc_kv = enc_kv.astype(low)
    *kv[3:], w_kept = after([*kv[3:], w_self], [enc_kv])

    def side_by_side(packs, bounds):
        return jnp.concatenate([pack[:, a:b] for a, b in bounds for pack in packs], axis=1)

    proj_bounds = [(i * head_width, (i + 1) * head_width) for i in range(3)]
    proj_bounds.append((3 * head_width, proj_pack.shape[1]))
    w_proj = side_by_side(proj_packs, proj_bounds)
    w_proj = lax.all_gather(w_proj, SHARD, axis=0, tiled=True)
    (enc_kv,) = after([enc_kv], kv[3:])
    ffn_packs = after(ffn_packs, kv[3:])
    w_one = side_by_side(ffn_packs, [(0, hidden_width)])
    w_one = lax.all_gather(w_one, SHARD, axis=0, tiled=True)
    w_two = side_by_side(ffn_packs, [(hidden_width, 2 * hidden_width)])
    w_two = lax.all_gather(w_two, SHARD, axis=0, tiled=True)
    w_out = w_proj[:, :all_heads], w_proj[:, all_heads : 2 * all_heads]
    w_cross = w_proj[:, 2 * all_heads : 3 * all_heads]
    used = -(-(n_head // 4 + n_up) // 128)
    biases = w_proj.reshape(shards, shard_rows, -1)[:, :used, 3 * all_heads :]
    biases = biases.reshape(shards, used, depth, 128).transpose(0, 2, 1, 3)
    biases = biases.reshape(shards, depth, -1)[:, :, : n_head // 4 + n_up]
    biases = biases.transpose(1, 2, 0).astype(wide)
    bias_cross = biases[:, : n_head // 4].reshape(-1)
    bias_up = biases[:, n_head // 4 :].reshape(-1)

    def heads_to_rows(array):
        return jnp.concatenate(spread(row_blocks(array, depth), T), axis=1)

    def to_heads(array):
        return spread(column_blocks(array, depth), T)

    def rows_to_heads(array):
        return jnp.concatenate(to_heads(array), axis=0)

    def owned(gradient):
        return lax.psum_scatter(gradient.astype(low), SHARD, scatter_dimension=0, tiled=True)

    def updated(index, gradient, scale=None):
        old = masters[index], gradient, firsts[index], seconds[index]
        master, first, second = adamw_step(*old, RATES[index], DECAYS[index])
        if scale is not None:
            master = master * scale
        return master, first, second, master.astype(low)

    self_context, self_lse, peaks = self_fwd(queries, kv, meta)
    self_all = heads_to_rows(self_context)
    enc_kv = relay_gather(enc_kv, [self_all])
    own_tokens = pick_rows(tokens, plane, rows).astype(wide)
    hidden_one = own_tokens + contract_cols(self_all, w_out[0]) + vec_all[0]
    normed_one, unit_one, factor_one = normalize(hidden_one, vec_all[3], vec_all[4])
    low_one = normed_one.astype(low)
    cross_queries = rows_to_heads((product(low_one, w_cross) + bias_cross).astype(low))
    holder = plane * groups // depth
    outgoing = []
    for j in range(groups):
        wanted = lax.dynamic_slice_in_dim(near_bases[j], plane * per_slice, per_slice)
        wanted = jnp.clip(wanted // BLK - member * rounds, 0, rounds - 1)
        picked = [pick_rows(cotangent, wanted[i], BLK) for i in range(per_slice)]
        outgoing.append(jnp.concatenate(picked))
    (peaks,) = after([peaks], [cross_queries])
    top_all = jnp.max(peaks.reshape(-1, heads, BLK), axis=(0, 2))
    for axis in (C, F):
        step = 1
        while step < lax.axis_size(axis):
            top_all = jnp.maximum(top_all, swap(top_all, axis, step))
            step *= 2
    enc_kv[3:] = after(enc_kv[3:], [cross_queries, top_all])
    outgoing = after(outgoing, enc_kv[3:])
    incoming = jnp.where(member == holder, outgoing[0], jnp.zeros_like(outgoing[0]))
    for j in range(1, groups):
        pairs = []
        for level in range(depth):
            source = level * groups // depth
            pairs.append((source * depth + level, (source ^ j) * depth + level))
        incoming = incoming + lax.ppermute(outgoing[j], (C, T), pairs)
    cross_context, cross_lse = cross_fwd(cross_queries, enc_kv, seg)
    cross_all = heads_to_rows(cross_context)
    hidden_two = normed_one + contract_cols(cross_all, w_out[1]) + vec_all[1]
    normed_two, unit_two, factor_two = normalize(hidden_two, vec_all[5], vec_all[6])
    low_two = normed_two.astype(low)
    upward = product(low_two, w_one) + bias_up
    below = 0.5 * (1.0 + lax.erf(upward * 0.5**0.5))
    activated = (upward * below).astype(low)
    slope = below + upward * jnp.exp(-0.5 * upward * upward) * (0.5 / jnp.pi) ** 0.5
    hidden_three = normed_two + contract_cols(activated, w_two) + vec_all[2]
    normed_three, unit_three, factor_three = normalize(hidden_three, vec_all[7], vec_all[8])

    grad_three, gain_three, shift_three = normalize_back(
        incoming.astype(wide), unit_three, factor_three, vec_all[7]
    )
    mlp_grad = grad_three.astype(low)
    grad_w_two = contract_rows(mlp_grad, activated).astype(low)
    act_grad = product(after([mlp_grad], [grad_w_two])[0], w_two).astype(low)
    up_grad = (act_grad.astype(wide) * slope).astype(low)
    grad_up_bias = jnp.sum(up_grad.astype(wide), axis=0)
    grad_two, gain_two, shift_two = normalize_back(
        grad_three + contract_cols(up_grad, w_one), unit_two, factor_two, vec_all[5]
    )
    low_grad_two = grad_two.astype(low)
    cross_grads = product(low_grad_two, w_out[1]).astype(low)
    (up_late,) = after([up_grad], [cross_grads])
    grad_w_one = grad_columns([(low_two, up_late)], [], depth)
    cross_grads = rows_to_heads(cross_grads)
    own_down, own_up = owned(grad_w_two), owned(grad_w_one)
    out_rows = from_planes(after([normed_three.astype(low)], [cross_grads])[0])
    saved = seg, cross_grads, cross_context, cross_lse
    cross_q_grad, far, *halves = cross_bwd(
        1, cross_queries, enc_kv, *saved, cross_queries, [grad_w_two, grad_w_one]
    )
    enc_passed = relay_start(*halves)
    cross_q_grad, *enc_terms = cross_bwd(0, cross_queries, enc_kv, *saved, cross_q_grad, [])
    (cross_q_grad,) = after([cross_q_grad], [*out_rows[1:], *enc_passed, own_down])
    (cross_q_all,) = after([heads_to_rows(cross_q_grad)], [own_up])
    grad_one, gain_one, shift_one = normalize_back(
        grad_two + contract_cols(cross_q_all, w_cross), unit_one, factor_one, vec_all[3]
    )
    low_grad_one = grad_one.astype(low)
    self_grads = product(low_grad_one, w_out[0]).astype(low)
    grad_vectors = jnp.stack(
        [
            jnp.sum(grad_one, axis=0),
            jnp.sum(grad_two, axis=0),
            jnp.sum(grad_three, axis=0),
            gain_one,
            shift_one,
            gain_two,
            shift_two,
            gain_three,
            shift_three,
        ]
    )
    vec_part = grad_vectors.reshape(9, shards, -1).transpose(1, 0, 2).reshape(shards, -1)
    up_part = grad_up_bias.reshape(depth, -1, shards).transpose(2, 0, 1)
    small_part = [jnp.concatenate([vec_part, up_part[:, j]], axis=1) for j in range(depth)]
    small_part = jnp.concatenate([by_shard(part, shard_rows) for part in small_part], axis=1)
    self_grads = rows_to_heads(self_grads)
    own_down, own_up = after([own_down, own_up], [self_grads])
    by_plane = by_plane_order([own_up, own_down], plane, depth)
    ffn = lax.psum_scatter(by_plane, T, scatter_dimension=1, tiled=True)
    enc_joined = relay_join([*enc_terms, far], enc_passed, [cross_q_all])
    enc_terms = relay_finish(enc_joined)
    q_grad, *kv_terms = self_bwd(
        queries, kv, meta, self_grads, self_context, self_lse, [*enc_joined[1:], by_plane]
    )
    kv_passed = relay_start(*kv_terms[3:])
    (cross_late,) = after([cross_q_all], [q_grad])
    grad_proj = grad_columns(
        [(low_grad_two, cross_all), (low_grad_one, self_all), (low_one, cross_late)],
        [small_part.astype(low)],
    )
    own_proj = owned(grad_proj)
    enc_grad, enc_columns = sum_terms(enc_terms, [q_grad])

    enc_parts = plane_shares([enc_grad], w_enc, plane, depth, None, [])
    enc_sent = spread(enc_parts, T)
    grad_w_enc = weight_grad(encoder, [enc_grad], [], plane, 512, enc_parts)
    kv_joined = relay_join(kv_terms, kv_passed, [ffn, grad_w_enc])

    out_rows = after(out_rows, kv_joined[1:])
    out_rows = jnp.stack(out_rows)[plane ^ jnp.arange(depth)].reshape(row_count, model_width)
    portion = row_count // groups
    returned = [pick_rows(out_rows, near[j], portion) for j in range(groups)]
    ffn = after([ffn], kv_joined[1:])[0].astype(wide)
    ffn_new = updated(2, ffn[:, :hidden_width]) + updated(3, ffn[:, hidden_width:].T)

    kv_grad, kv_columns = sum_terms(relay_finish(kv_joined), [grad_w_enc, enc_sent[1], *ffn_new, *returned], SOME_COST)
    returned = spread(after(returned, [kv_grad]), C)
    grad_head_bias = jnp.stack(
        [
            jnp.sum(q_grad.astype(wide), axis=0),
            kv_columns[0, head_width:],
            jnp.sum(cross_q_grad.astype(wide), axis=0),
            enc_columns[0, head_width:],
        ]
    )
    head_part = grad_head_bias.reshape(4, -1, shards).transpose(2, 0, 1).reshape(shards, -1)
    head_part = by_shard(head_part, shard_rows).astype(low)
    adds = [head_part, grad_w_enc]
    grad_first = weight_grad(tokens, [q_grad, kv_grad], adds, plane, rows, [], SOME_COST)
    (grad_first,) = after([grad_first], [own_proj])
    token_terms = plane_shares(
        [q_grad, kv_grad], w_kept, plane, depth, grad_one, [grad_first, *enc_sent[2:]], SOME_COST
    )
    token_sent = spread(token_terms, T)
    own_first = owned(grad_first)
    cuts = [0, all_heads, 2 * all_heads, 3 * all_heads, own_proj.shape[1]]
    own_proj = [own_proj[:, a:b] for a, b in zip(cuts, cuts[1:])]
    proj_parts = [column_blocks(part, depth) for part in own_proj]
    proj_parts = [jnp.concatenate([p[j] for p in proj_parts], axis=1) for j in range(depth)]
    own_first, *proj_parts = after([own_first, *proj_parts], token_sent[1:])
    own_first = own_first.astype(wide)
    proj = total(spread(proj_parts, T))
    result = put_blocks(jnp.concatenate(returned), places, wide)
    (token_sent[0],) = after(token_sent[:1], [result])
    grad_tokens = total(token_sent)
    grad_encoder = total(after(enc_sent, [result]))

    out_cross, out_self, in_cross = [
        proj[:, i * head_width : (i + 1) * head_width] for i in range(3)
    ]
    small_part = proj[:, 3 * head_width :].reshape(-1)
    gradients = {
        0: jnp.stack(
            column_blocks(own_first[:, : 3 * head_width], 3)
            + [in_cross]
            + column_blocks(own_first[:, 3 * head_width + 128 :], 2)
        ),
        1: jnp.stack([out_self.T, out_cross.T]),
        4: own_first[:, 3 * head_width : 3 * head_width + 128].reshape(-1)[:n_head].reshape(head_bias.shape),
        5: small_part[n_vec : n_vec + n_up].reshape(up_bias.shape),
        6: small_part[:n_vec].reshape(vectors.shape),
    }
    clip_factor = CLIP_LIMIT / jnp.maximum(top_all, CLIP_LIMIT)
    root_factor = jnp.sqrt(clip_factor)
    column_roots = jnp.repeat(root_factor, HEAD)
    in_scale = jnp.concatenate(
        [column_roots[None], column_roots[None], jnp.ones((4, head_width), wide)], axis=0
    )[:, None, :]
    slot_heads = (jnp.arange(head_bias.shape[1]) * shards + shard_index) // HEAD
    picked = jnp.sum(
        jnp.where(slot_heads[:, None] == jnp.arange(heads)[None, :], root_factor[None, :], 0.0),
        axis=1,
    )
    bias_scale = jnp.concatenate([picked[None], jnp.ones((3, picked.shape[0]), wide)], axis=0)
    scales = {0: in_scale, 4: bias_scale[:, :, None]}
    results = [result, grad_tokens, grad_encoder, clip_factor]
    for index in range(7):
        if index in gradients:
            results += updated(index, gradients[index], scales.get(index))
        else:
            results += ffn_new[4 * (index - 2) : 4 * (index - 1)]
    return tuple(results)


def solution(mesh):
    rows, table = P(SHARD, None), P(F, None)
    weights = (
        P(None, SHARD, T),
        P(None, T, SHARD),
        P(SHARD, T),
        P(T, SHARD),
        P(None, T, SHARD),
        P(T, SHARD),
        P(None, SHARD),
    )
    by_columns = P(SHARD, T)
    updates = tuple(spec for spec in weights for _ in range(4))
    return jax.shard_map(
        per_device,
        mesh=mesh,
        in_specs=(rows, rows, rows, table, table) + weights * 3,
        out_specs=(rows, by_columns, by_columns, P(T)) + updates,
        check_vma=False,
    )
```

```python
from functools import partial, reduce

import jax
import jax.numpy as jnp
from jax import lax
from jax.experimental import pallas as pl
from jax.experimental.pallas import tpu as pltpu
from jax.sharding import PartitionSpec as P

HEAD = 64
ENC = 4096
STEP = 10
BLK = 128

NEGATIVE = -1e30
NORM_EPS = 1e-05
ADAM_EPS = 1e-08
BETA = 0.5
CLIP_LIMIT = 10.0
RATES = (0.05, 0.3, 0.05, 0.03, 0.3, 0.3, 0.3)
DECAYS = (0.1, 0.1, 0.1, 0.1, 0.0, 0.0, 0.0)
SCALE = HEAD ** (-0.5)
VMEM_BYTES = 56 * 1024 * 1024
F, C, T = "fsdp", "context", "tensor"
SHARD = (F, C)
NO_COST = pl.CostEstimate(flops=0, bytes_accessed=0, transcendentals=0)
SOME_COST = pl.CostEstimate(flops=2 * 10**10, bytes_accessed=2**25, transcendentals=0)


def product(left_side, right_side):
    return jnp.dot(left_side, right_side, preferred_element_type=jnp.float32)


def contract_rows(left_side, right_side):
    return lax.dot_general(
        left_side, right_side, (((0,), (0,)), ((), ())), preferred_element_type=jnp.float32
    )


def contract_cols(left_side, right_side):
    return lax.dot_general(
        left_side, right_side, (((1,), (1,)), ((), ())), preferred_element_type=jnp.float32
    )


def stack_heads(block, heads):
    lanes = lax.broadcasted_iota(jnp.int32, block.shape, 1) // HEAD
    zero = jnp.zeros_like(block)
    return jnp.concatenate([jnp.where(lanes == h, block, zero) for h in range(heads)], axis=0)


def merge_heads(stacked, heads):
    rows = stacked.shape[0] // heads
    lanes = lax.broadcasted_iota(jnp.int32, (rows, stacked.shape[1]), 1) // HEAD
    merged = stacked[:rows]
    for h in range(1, heads):
        merged = jnp.where(lanes == h, stacked[h * rows : (h + 1) * rows], merged)
    return merged


def col_to_row(column):
    return jnp.transpose(jnp.broadcast_to(column, (column.shape[0], 128)))[0:1]


def fold_lanes(tile, combine):
    return reduce(combine, [tile[:, j : j + 128] for j in range(0, tile.shape[1], 128)])


def whole(shape):
    return pl.BlockSpec(shape, lambda i, s: (0,) * len(shape), pipeline_mode=pl.Buffered(1))


def fetch_kv(sources, places, sems):
    copies = [
        pltpu.make_async_copy(source, place, sems.at[i])
        for i, (source, place) in enumerate(zip(sources, places))
    ]

    @pl.when(pl.program_id(0) == 0)
    def _():
        for copy in copies:
            copy.start()
        for copy in copies:
            copy.wait()


def piece_bounds(pieces):
    full, half = pieces[0].shape[0], pieces[3].shape[0]
    return [(0, 0, full), (1, 0, full), (2, 0, full), (3, 0, half), (3, half, half)]


def member_rows(order_ref, row, bounds, full):
    return [
        pl.ds(pl.multiple_of(order_ref[row, j] * full + start, size), size)
        for j, start, size in bounds
    ]


def gate_body(*refs):
    pass


def after(values, others):
    count, every = len(values), [*values, *others]
    return pl.pallas_call(
        gate_body,
        in_specs=[pl.BlockSpec(memory_space=pl.ANY)] * len(every),
        out_specs=[pl.BlockSpec(memory_space=pl.ANY)] * count,
        out_shape=[jax.ShapeDtypeStruct(value.shape, value.dtype) for value in values],
        input_output_aliases={i: i for i in range(count)},
        cost_estimate=NO_COST,
        name="gate",
    )(*every)


def cross_fwd_body(heads, bounds, seg_ref, q_ref, *refs):
    sources, (o_ref, lse_ref, kv_ref, s_ref, sems) = refs[: len(bounds)], refs[len(bounds) :]
    places = member_rows(seg_ref, 3, bounds, sources[0].shape[0])
    fetch_kv(sources, [kv_ref.at[place] for place in places], sems)
    block = pl.program_id(0)
    low, high, cut = seg_ref[0, block], seg_ref[1, block], seg_ref[2, block]
    queries = stack_heads(q_ref[...] * jnp.bfloat16(SCALE), heads)
    rows, width = queries.shape
    tiles, _, step = s_ref.shape

    def attend(sequence):
        def scores(t, highest):
            at = pl.ds(pl.multiple_of(sequence * ENC + t * step, step), step)
            tile = contract_cols(queries, kv_ref[at, :width])
            s_ref[t] = tile
            return jnp.maximum(highest, fold_lanes(tile, jnp.maximum))

        highest = lax.fori_loop(0, tiles, scores, jnp.full((rows, 128), NEGATIVE, jnp.float32))
        peak = jnp.max(highest, axis=1, keepdims=True)

        def weigh(t, running):
            total, summed = running
            at = pl.ds(pl.multiple_of(sequence * ENC + t * step, step), step)
            weights = jnp.exp(s_ref[t] - peak)
            summed = summed + product(weights.astype(jnp.bfloat16), kv_ref[at, width:])
            return total + fold_lanes(weights, jnp.add), summed

        total, summed = lax.fori_loop(
            0,
            tiles,
            weigh,
            (jnp.zeros((rows, 128), jnp.float32), jnp.zeros((rows, width), jnp.float32)),
        )
        total = jnp.sum(total, axis=1, keepdims=True)
        merged = merge_heads(summed / total, heads)
        lse = col_to_row(peak + jnp.log(total))
        place = lax.broadcasted_iota(jnp.int32, merged.shape, 0)
        own = jnp.where(place >= cut, 1, 0) == sequence
        o_ref[...] = jnp.where(own, merged, o_ref[...].astype(jnp.float32)).astype(o_ref.dtype)
        place = lax.broadcasted_iota(jnp.int32, lse.shape, 1) % BLK
        own = jnp.where(place >= cut, 1, 0) == sequence
        lse_ref[0] = jnp.where(own, lse, lse_ref[0])

    o_ref[...] = jnp.zeros_like(o_ref)
    lse_ref[...] = jnp.zeros_like(lse_ref)
    pl.loop(low, high + 1)(attend)


def cross_fwd(queries, enc_kv, seg):
    count, width = queries.shape
    heads, blocks, step = width // HEAD, count // BLK, 1024
    rows, bounds = heads * BLK, piece_bounds(enc_kv)
    enc_all = sum(piece.shape[0] for piece in enc_kv)
    return pl.pallas_call(
        partial(cross_fwd_body, heads, bounds),
        grid_spec=pltpu.PrefetchScalarGridSpec(
            num_scalar_prefetch=1,
            grid=(blocks,),
            in_specs=[pl.BlockSpec((BLK, width), lambda i, s: (i, 0))]
            + [pl.BlockSpec(memory_space=pl.ANY)] * len(bounds),
            out_specs=[
                pl.BlockSpec((BLK, width), lambda i, s: (i, 0)),
                pl.BlockSpec((1, 1, rows), lambda i, s: (i, 0, 0)),
            ],
            scratch_shapes=[
                pltpu.VMEM((enc_all, 2 * width), jnp.bfloat16),
                pltpu.VMEM((ENC // step, rows, step), jnp.float32),
                pltpu.SemaphoreType.DMA((len(bounds),)),
            ],
        ),
        out_shape=[
            jax.ShapeDtypeStruct((count, width), jnp.bfloat16),
            jax.ShapeDtypeStruct((blocks, 1, rows), jnp.float32),
        ],
        compiler_params=pltpu.CompilerParams(vmem_limit_bytes=VMEM_BYTES),
        cost_estimate=NO_COST,
        name="cross_fwd",
    )(seg, queries, *enc_kv)


def cross_bwd_body(heads, bounds, kind, step, seg_ref, q_ref, g_ref, o_ref, lse_ref, *refs):
    count, outs = len(bounds), refs[-len(bounds) - 4 : -3]
    sources, prior, (dq_ref, *outs) = refs[:count], refs[count], outs
    kv_ref, acc_ref, sems = refs[-3:]
    block = pl.program_id(0)
    sequence, full = seg_ref[4, kind], ENC // 2
    places = [
        pl.ds(pl.multiple_of(seg_ref[3, j] * full + at - sequence * ENC, size), size)
        for j, at, size in bounds
    ]
    fetch_kv(sources, [kv_ref.at[place] for place in places], sems)

    @pl.when(block == 0)
    def _():
        acc_ref[...] = jnp.zeros_like(acc_ref)

    seen = (seg_ref[0, block] <= sequence) & (seg_ref[1, block] >= sequence)
    start = prior[...] if kind == 0 else jnp.zeros_like(dq_ref)
    dq_ref[...] = start

    @pl.when(seen)
    def _():
        queries = stack_heads(q_ref[...] * jnp.bfloat16(SCALE), heads)
        rows, width = queries.shape
        grads = stack_heads(g_ref[...], heads)
        dots = g_ref[...].astype(jnp.float32) * o_ref[...].astype(jnp.float32)
        dot_row = col_to_row(jnp.sum(stack_heads(dots, heads), axis=1, keepdims=True))
        place = lax.broadcasted_iota(jnp.int32, lse_ref[0].shape, 1) % BLK
        own_seq = jnp.where(place >= seg_ref[2, block], 1, 0)
        lse = jnp.where(own_seq == sequence, lse_ref[0], -NEGATIVE)

        def tile_terms(t, q_grad):
            at = pl.ds(pl.multiple_of(t * step, step), step)
            keys, values = kv_ref[at, :width], kv_ref[at, width:]
            probs = jnp.exp(contract_cols(keys, queries) - lse)
            s_grad = (probs * (contract_cols(values, grads) - dot_row)).astype(jnp.bfloat16)
            acc_ref[at, width:] += product(probs.astype(jnp.bfloat16), grads)
            acc_ref[at, :width] += product(s_grad, queries)
            return q_grad + contract_rows(s_grad, keys)

        q_grad = lax.fori_loop(
            0, ENC // step, tile_terms, jnp.zeros((rows, width), jnp.float32)
        )
        q_grad = merge_heads(q_grad, heads) * SCALE + start.astype(jnp.float32)
        dq_ref[...] = q_grad.astype(dq_ref.dtype)

    @pl.when(block == pl.num_programs(0) - 1)
    def _():
        for out, place in zip(outs, places):
            out[...] = acc_ref[place, :].astype(out.dtype)


def cross_bwd(kind, queries, enc_kv, seg, grads, context, lse, prior, others):
    count, width = queries.shape
    heads, blocks, step = width // HEAD, count // BLK, 2048
    bounds = piece_bounds(enc_kv)
    picked = [(0, 1), (2, 3, 4)][kind]
    pieces, bounds = [enc_kv[i] for i in picked], [bounds[i] for i in picked]
    row = pl.BlockSpec((BLK, width), lambda i, s: (i, 0))
    return pl.pallas_call(
        partial(cross_bwd_body, heads, bounds, kind, step),
        grid_spec=pltpu.PrefetchScalarGridSpec(
            num_scalar_prefetch=1,
            grid=(blocks,),
            in_specs=[row, row, row, pl.BlockSpec((1, 1, heads * BLK), lambda i, s: (i, 0, 0))]
            + [pl.BlockSpec(memory_space=pl.ANY)] * len(bounds)
            + [row]
            + [pl.BlockSpec(memory_space=pl.ANY)] * len(others),
            out_specs=[row] + [whole(piece.shape) for piece in pieces],
            scratch_shapes=[
                pltpu.VMEM((ENC, 2 * width), jnp.bfloat16),
                pltpu.VMEM((ENC, 2 * width), jnp.float32),
                pltpu.SemaphoreType.DMA((len(bounds),)),
            ],
        ),
        out_shape=[jax.ShapeDtypeStruct((count, width), jnp.bfloat16)]
        + [jax.ShapeDtypeStruct(piece.shape, jnp.bfloat16) for piece in pieces],
        compiler_params=pltpu.CompilerParams(vmem_limit_bytes=VMEM_BYTES),
        cost_estimate=NO_COST,
        name="cross_bwd",
    )(seg, queries, grads, context, lse, *pieces, prior, *others)


def gather_tile(kv_ref, t, columns):
    at = pl.ds(pl.multiple_of(t * BLK, BLK), BLK)
    return jnp.concatenate([kv_ref[j, at, columns] for j in range(kv_ref.shape[0])], axis=0)


def self_fwd_body(heads, bounds, meta_ref, q_ref, *refs):
    sources, (o_ref, lse_ref, top_ref, kv_refs, sems) = refs[: len(bounds)], refs[len(bounds) :]
    fetch_kv(sources, [kv_refs.at[j, pl.ds(at, size)] for j, at, size in bounds], sems)
    groups = kv_refs.shape[0]
    block = pl.program_id(0)
    base, first, last = [meta_ref[groups + k, block] for k in range(3)]
    cut = meta_ref[groups + 3, 0]
    queries = stack_heads(q_ref[...] * jnp.bfloat16(SCALE), heads)
    rows, width = queries.shape
    q_pos = base + lax.broadcasted_iota(jnp.int32, (rows, BLK), 0) % BLK
    q_start = jnp.where(q_pos >= cut, cut, 0)
    lane = lax.broadcasted_iota(jnp.int32, (rows, BLK), 1)

    def visit(t, running):
        peak, total, summed = running
        raw = contract_cols(queries, gather_tile(kv_refs, t, slice(0, width)))
        parts = []
        for d in range(groups):
            k_pos = lane + meta_ref[d, t]
            seen = (k_pos <= q_pos) & (k_pos >= q_start)
            parts.append(jnp.where(seen, raw[:, d * BLK : (d + 1) * BLK], NEGATIVE))
        new_peak = jnp.maximum(peak, jnp.max(reduce(jnp.maximum, parts), axis=1, keepdims=True))
        weights = [jnp.exp(part - new_peak) for part in parts]
        shrink = jnp.exp(peak - new_peak)
        total = total * shrink + jnp.sum(reduce(jnp.add, weights), axis=1, keepdims=True)
        low_weights = jnp.concatenate(weights, axis=1).astype(jnp.bfloat16)
        values = gather_tile(kv_refs, t, slice(width, 2 * width))
        return new_peak, total, summed * shrink + product(low_weights, values)

    peak, total, summed = lax.fori_loop(
        first,
        last + 1,
        visit,
        (
            jnp.full((rows, 1), NEGATIVE, jnp.float32),
            jnp.zeros((rows, 1), jnp.float32),
            jnp.zeros((rows, width), jnp.float32),
        ),
    )
    o_ref[...] = merge_heads(summed / total, heads).astype(o_ref.dtype)
    lse_ref[0] = col_to_row(peak + jnp.log(total))
    top_ref[0] = col_to_row(peak)


def self_fwd(queries, kv, meta):
    count, width = queries.shape
    heads, blocks, bounds = width // HEAD, count // BLK, piece_bounds(kv)
    rows, kept = heads * BLK, (bounds[-1][0] + 1,) + kv[0].shape
    row = pl.BlockSpec((BLK, width), lambda i, s: (i, 0))
    stat = pl.BlockSpec((1, 1, rows), lambda i, s: (i, 0, 0))
    return pl.pallas_call(
        partial(self_fwd_body, heads, bounds),
        grid_spec=pltpu.PrefetchScalarGridSpec(
            num_scalar_prefetch=1,
            grid=(blocks,),
            in_specs=[row] + [pl.BlockSpec(memory_space=pl.ANY)] * len(bounds),
            out_specs=[row, stat, stat],
            scratch_shapes=[
                pltpu.VMEM(kept, jnp.bfloat16),
                pltpu.SemaphoreType.DMA((len(bounds),)),
            ],
        ),
        out_shape=[jax.ShapeDtypeStruct((count, width), jnp.bfloat16)]
        + [jax.ShapeDtypeStruct((blocks, 1, rows), jnp.float32)] * 2,
        compiler_params=pltpu.CompilerParams(vmem_limit_bytes=VMEM_BYTES),
        cost_estimate=NO_COST,
        name="self_fwd",
    )(meta, queries, *kv)


def self_bwd_body(heads, bounds, waits, meta_ref, q_ref, g_ref, o_ref, lse_ref, *refs):
    count = len(bounds)
    sources, (dq_ref, *outs) = refs[:count], refs[count + waits : 2 * count + waits + 1]
    kv_refs, acc_ref, sems = refs[2 * count + waits + 1 :]
    fetch_kv(sources, [kv_refs.at[j, pl.ds(at, size)] for j, at, size in bounds], sems)
    groups = kv_refs.shape[0]
    block = pl.program_id(0)

    @pl.when(block == 0)
    def _():
        acc_ref[...] = jnp.zeros_like(acc_ref)

    base, first, last = [meta_ref[groups + k, block] for k in range(3)]
    cut = meta_ref[groups + 3, 0]
    queries = stack_heads(q_ref[...] * jnp.bfloat16(SCALE), heads)
    rows, width = queries.shape
    grads = stack_heads(g_ref[...], heads)
    dots = g_ref[...].astype(jnp.float32) * o_ref[...].astype(jnp.float32)
    dot_row = col_to_row(jnp.sum(stack_heads(dots, heads), axis=1, keepdims=True))
    lse = lse_ref[0]
    q_pos = base + lax.broadcasted_iota(jnp.int32, lse.shape, 1) % BLK
    q_start = jnp.where(q_pos >= cut, cut, 0)
    sub = lax.broadcasted_iota(jnp.int32, (BLK, rows), 0)

    def tile_terms(t, q_grad):
        at = pl.ds(pl.multiple_of(t * BLK, BLK), BLK)
        keys = gather_tile(kv_refs, t, slice(0, width))
        values = gather_tile(kv_refs, t, slice(width, 2 * width))
        raw = contract_cols(keys, queries)
        parts = []
        for d in range(groups):
            k_base = meta_ref[d, t]
            seen = (sub <= q_pos - k_base) & (sub >= q_start - k_base)
            parts.append(jnp.where(seen, jnp.exp(raw[d * BLK : (d + 1) * BLK] - lse), 0.0))
        probs = jnp.concatenate(parts, axis=0)
        s_grad = (probs * (contract_cols(values, grads) - dot_row)).astype(jnp.bfloat16)
        acc_ref[:, at, width:] += product(probs.astype(jnp.bfloat16), grads).reshape(
            groups, BLK, width
        )
        acc_ref[:, at, :width] += product(s_grad, queries).reshape(groups, BLK, width)
        return q_grad + contract_rows(s_grad, keys)

    q_grad = lax.fori_loop(first, last + 1, tile_terms, jnp.zeros((rows, width), jnp.float32))
    dq_ref[...] = (merge_heads(q_grad, heads) * SCALE).astype(dq_ref.dtype)

    @pl.when(block == pl.num_programs(0) - 1)
    def _():
        for out, (j, at, size) in zip(outs, bounds):
            out[...] = acc_ref[j, at : at + size].astype(out.dtype)


def self_bwd(queries, kv, meta, grads, context, lse, others):
    count, width = queries.shape
    heads, blocks, bounds = width // HEAD, count // BLK, piece_bounds(kv)
    rows, kept = heads * BLK, (bounds[-1][0] + 1,) + kv[0].shape
    row = pl.BlockSpec((BLK, width), lambda i, s: (i, 0))
    stat = pl.BlockSpec((1, 1, rows), lambda i, s: (i, 0, 0))
    return pl.pallas_call(
        partial(self_bwd_body, heads, bounds, len(others)),
        grid_spec=pltpu.PrefetchScalarGridSpec(
            num_scalar_prefetch=1,
            grid=(blocks,),
            in_specs=[row, row, row, stat]
            + [pl.BlockSpec(memory_space=pl.ANY)] * (len(bounds) + len(others)),
            out_specs=[row] + [whole(piece.shape) for piece in kv],
            scratch_shapes=[
                pltpu.VMEM(kept, jnp.bfloat16),
                pltpu.VMEM(kept, jnp.float32),
                pltpu.SemaphoreType.DMA((len(bounds),)),
            ],
        ),
        out_shape=[jax.ShapeDtypeStruct((count, width), jnp.bfloat16)]
        + [jax.ShapeDtypeStruct(piece.shape, jnp.bfloat16) for piece in kv],
        compiler_params=pltpu.CompilerParams(vmem_limit_bytes=VMEM_BYTES),
        cost_estimate=NO_COST,
        name="self_bwd",
    )(meta, queries, grads, context, lse, *kv, *others)


def move_body(index_ref, in_ref, out_ref):
    out_ref[...] = in_ref[...].astype(out_ref.dtype)


def put_blocks(rows, index, dtype):
    count, width = rows.shape
    return pl.pallas_call(
        move_body,
        grid_spec=pltpu.PrefetchScalarGridSpec(
            num_scalar_prefetch=1,
            grid=(count // BLK,),
            in_specs=[pl.BlockSpec((BLK, width), lambda i, s: (i, 0))],
            out_specs=pl.BlockSpec((BLK, width), lambda i, s: (s[i], 0)),
        ),
        out_shape=jax.ShapeDtypeStruct((count, width), dtype),
        cost_estimate=SOME_COST,
        name="put_blocks",
    )(index, rows)


def join_body(whole_ref, passed_ref, *refs):
    total = whole_ref[...].astype(jnp.float32) + passed_ref[...].astype(jnp.float32)
    refs[-1][...] = total.astype(refs[-1].dtype)


def add_half(whole_rows, passed, lower, others):
    half, width = passed.shape
    size = min(half, 256)
    first = half // size if lower else 0
    part = pl.BlockSpec((size, width), lambda i: (first + i, 0))
    return pl.pallas_call(
        join_body,
        grid=(half // size,),
        in_specs=[part, pl.BlockSpec((size, width), lambda i: (i, 0))]
        + [pl.BlockSpec(memory_space=pl.ANY)] * len(others),
        out_specs=part,
        out_shape=jax.ShapeDtypeStruct(whole_rows.shape, whole_rows.dtype),
        input_output_aliases={0: 0},
        cost_estimate=NO_COST,
        name="add_half",
    )(whole_rows, passed, *others)


def grad_body(count, *refs):
    out_ref, start = refs[-1], 0
    for k in range(count):
        terms = contract_rows(refs[2 * k][...], refs[2 * k + 1][...])
        out_ref[:, start : start + terms.shape[1]] = terms.astype(out_ref.dtype)
        start += terms.shape[1]
    for ref in refs[2 * count : -1]:
        out_ref[:, start : start + ref.shape[1]] = ref[...]
        start += ref.shape[1]


def grad_columns(pairs, others, tiles=1):
    flat = [array for pair in pairs for array in pair]
    width = pairs[0][0].shape[1]
    columns = sum(right.shape[1] for _, right in pairs) + sum(array.shape[1] for array in others)
    size = pairs[0][1].shape[0]
    if tiles == 1:
        specs = [pl.BlockSpec(array.shape, lambda i: (0, 0)) for array in flat + others]
    else:
        specs = [
            pl.BlockSpec((size, width), lambda i: (0, 0)),
            pl.BlockSpec((size, columns // tiles), lambda i: (0, i)),
        ]
    return pl.pallas_call(
        partial(grad_body, len(pairs)),
        grid=(tiles,),
        in_specs=specs,
        out_specs=pl.BlockSpec((width, columns // tiles), lambda i: (0, i)),
        out_shape=jax.ShapeDtypeStruct((width, columns), jnp.bfloat16),
        compiler_params=pltpu.CompilerParams(vmem_limit_bytes=VMEM_BYTES),
        cost_estimate=NO_COST,
        name="grad_columns",
    )(*flat, *others)


def plane_body(plane_ref, *refs):
    start = 0
    for ref in refs[:-1]:
        refs[-1][:, start : start + ref.shape[1]] = ref[...]
        start += ref.shape[1]


def by_plane_order(arrays, plane, depth):
    size = arrays[0].shape[0]
    widths = [array.shape[1] // depth for array in arrays]
    return pl.pallas_call(
        plane_body,
        grid_spec=pltpu.PrefetchScalarGridSpec(
            num_scalar_prefetch=1,
            grid=(depth,),
            in_specs=[pl.BlockSpec((size, width), lambda p, s: (0, s[0] ^ p)) for width in widths],
            out_specs=pl.BlockSpec((size, sum(widths)), lambda p, s: (0, p)),
        ),
        out_shape=jax.ShapeDtypeStruct((size, depth * sum(widths)), arrays[0].dtype),
        cost_estimate=NO_COST,
        name="by_plane_order",
    )(plane.reshape(1).astype(jnp.int32), *arrays)


ANYWHERE = pl.BlockSpec(memory_space=pl.ANY)


def sum_body(count, *refs):
    out_ref, column_ref = refs[-2:]
    added = reduce(jnp.add, [ref[...].astype(jnp.float32) for ref in refs[:count]])
    rounded = added.astype(out_ref.dtype)
    out_ref[...] = rounded

    @pl.when(pl.program_id(0) == 0)
    def _():
        column_ref[...] = jnp.zeros_like(column_ref)

    column_ref[...] += jnp.sum(rounded.astype(jnp.float32), axis=0, keepdims=True)


def sum_terms(terms, others, cost=SOME_COST):
    count, width = terms[0].shape
    size = 256
    tile = pl.BlockSpec((size, width), lambda i: (i, 0))
    return pl.pallas_call(
        partial(sum_body, len(terms)),
        grid=(count // size,),
        in_specs=[tile] * len(terms) + [ANYWHERE] * len(others),
        out_specs=[tile, pl.BlockSpec((1, width), lambda i: (0, 0))],
        out_shape=[
            jax.ShapeDtypeStruct((count, width), jnp.bfloat16),
            jax.ShapeDtypeStruct((1, width), jnp.float32),
        ],
        cost_estimate=cost,
        name="sum_terms",
    )(*terms, *others)


def share_body(depth, parts, extra, plane_ref, *refs):
    rows = [ref[...] for ref in refs[:parts]]
    merged = rows[0] if parts == 1 else jnp.concatenate(rows, axis=1)
    own = pl.program_id(0) == plane_ref[0]
    for j in range(depth):
        term = contract_cols(merged, refs[parts + j][...])
        if extra:
            term = term + jnp.where(own, refs[parts + depth + j][...], 0.0)
        refs[len(refs) - depth + j][...] = term.astype(jnp.bfloat16)


def plane_shares(arrays, weight, plane, depth, extra, others, cost=SOME_COST):
    count, size = arrays[-1].shape[0], 256 if extra is None else extra.shape[0]
    part = weight.shape[0] // depth
    last = pl.BlockSpec((size, arrays[-1].shape[1]), lambda i, s: (i, 0))
    specs = [last]
    if len(arrays) == 2:
        specs = [pl.BlockSpec((size, arrays[0].shape[1]), lambda i, s: (s[0] ^ i, 0)), last]
    for j in range(depth):
        specs.append(
            pl.BlockSpec((part, weight.shape[1]), partial(lambda j, i, s: (s[0] ^ j, 0), j))
        )
    inputs = [*arrays, *[weight] * depth]
    if extra is not None:
        for j in range(depth):
            specs.append(pl.BlockSpec((size, part), partial(lambda j, i, s: (0, s[0] ^ j), j)))
        inputs += [extra] * depth
    return pl.pallas_call(
        partial(share_body, depth, len(arrays), extra is not None),
        grid_spec=pltpu.PrefetchScalarGridSpec(
            num_scalar_prefetch=1,
            grid=(count // size,),
            in_specs=specs + [ANYWHERE] * len(others),
            out_specs=[pl.BlockSpec((size, part), lambda i, s: (i, 0))] * depth,
        ),
        out_shape=[jax.ShapeDtypeStruct((count, part), jnp.bfloat16)] * depth,
        compiler_params=pltpu.CompilerParams(vmem_limit_bytes=VMEM_BYTES),
        cost_estimate=cost,
        name="plane_shares",
    )(plane.reshape(1).astype(jnp.int32), *inputs, *others)


def gather_grad_body(parts, adds, plane_ref, left_ref, *refs):
    out_ref, acc_ref = refs[-2:]
    step = pl.program_id(0)

    @pl.when(step == 0)
    def _():
        acc_ref[...] = jnp.zeros_like(acc_ref)

    start = 0
    for ref in refs[:parts]:
        stop = start + ref.shape[1]
        acc_ref[:, start:stop] += contract_rows(left_ref[...], ref[...])
        start = stop

    @pl.when(step == pl.num_programs(0) - 1)
    def _():
        out_ref[:, :start] = acc_ref[...].astype(out_ref.dtype)
        at = start
        for ref in refs[parts : parts + adds]:
            out_ref[:, at : at + ref.shape[1]] = ref[...]
            at += ref.shape[1]


def weight_grad(left, arrays, adds, plane, size, others, cost=SOME_COST):
    count, width = left.shape
    last = pl.BlockSpec((size, arrays[-1].shape[1]), lambda i, s: (i, 0))
    specs = [pl.BlockSpec((size, width), lambda i, s: (i, 0)), last]
    if len(arrays) == 2:
        specs.insert(1, pl.BlockSpec((size, arrays[0].shape[1]), lambda i, s: (s[0] ^ i, 0)))
    made = sum(array.shape[1] for array in arrays)
    columns = made + sum(array.shape[1] for array in adds)
    specs += [whole(array.shape) for array in adds] + [ANYWHERE] * len(others)
    return pl.pallas_call(
        partial(gather_grad_body, len(arrays), len(adds)),
        grid_spec=pltpu.PrefetchScalarGridSpec(
            num_scalar_prefetch=1,
            grid=(count // size,),
            in_specs=specs,
            out_specs=pl.BlockSpec((width, columns), lambda i, s: (0, 0)),
            scratch_shapes=[pltpu.VMEM((width, made), jnp.float32)],
        ),
        out_shape=jax.ShapeDtypeStruct((width, columns), jnp.bfloat16),
        compiler_params=pltpu.CompilerParams(vmem_limit_bytes=VMEM_BYTES),
        cost_estimate=cost,
        name="weight_grad",
    )(plane.reshape(1).astype(jnp.int32), left, *arrays, *adds, *others)


def normalize(hidden, gain_row, shift_row):
    centred = hidden - jnp.mean(hidden, axis=-1, keepdims=True)
    factor = lax.rsqrt(jnp.mean(centred * centred, axis=-1, keepdims=True) + NORM_EPS)
    unit_rows = centred * factor
    return (unit_rows * gain_row + shift_row, unit_rows, factor)


def normalize_back(incoming, unit_rows, factor, gain_row):
    scaled = incoming * gain_row
    centred_grad = (
        scaled
        - jnp.mean(scaled, axis=-1, keepdims=True)
        - unit_rows * jnp.mean(scaled * unit_rows, axis=-1, keepdims=True)
    )
    return (factor * centred_grad, jnp.sum(incoming * unit_rows, axis=0), jnp.sum(incoming, axis=0))


def adamw_step(master, gradient, first_moment, second_moment, step_rate, weight_decay):
    first_moment = BETA * first_moment + (1.0 - BETA) * gradient
    second_moment = BETA * second_moment + (1.0 - BETA) * gradient * gradient
    correction = 1.0 - BETA**STEP
    update = first_moment / correction / (jnp.sqrt(second_moment / correction) + ADAM_EPS)
    return (master - step_rate * (update + weight_decay * master), first_moment, second_moment)
def swap(value, axis, j):
    return lax.ppermute(value, axis, [(i, i ^ j) for i in range(lax.axis_size(axis))])


def spread(blocks, axis):
    return [blocks[0]] + [swap(blocks[j], axis, j) for j in range(1, len(blocks))]


def total(blocks):
    return reduce(jnp.add, [block.astype(jnp.float32) for block in blocks])


def column_blocks(array, count):
    size = array.shape[1] // count
    return [array[:, j * size : (j + 1) * size] for j in range(count)]


def row_blocks(array, count):
    size = array.shape[0] // count
    return [array[j * size : (j + 1) * size] for j in range(count)]


def pick_rows(array, index, size):
    return lax.dynamic_slice_in_dim(array, index * size, size, 0)


def by_shard(flat, shard_rows):
    shards, used = flat.shape
    flat = jnp.pad(flat, ((0, 0), (0, -used % 128))).reshape(shards, -1, 128)
    return jnp.pad(flat, ((0, 0), (0, shard_rows - flat.shape[1]), (0, 0))).reshape(-1, 128)


def relay_gather(block, others=()):
    near, far = swap(block, C, 1), swap(block, C, 2)
    if others:
        near, far = after([near, far], others)
    half = block.shape[0] // 2
    return [block, near, far, swap(far[:half], C, 1), swap(near[half:], C, 2)]


def relay_start(upper, lower):
    return swap(upper, C, 1), swap(lower, C, 2)


def relay_join(terms, passed, others=()):
    own, near, far = terms[:3]
    return own, add_half(near, passed[1], True, others), add_half(far, passed[0], False, others)


def relay_finish(joined):
    own, near, far = joined
    return [own, swap(near, C, 1), swap(far, C, 2)]


def per_device(tokens, encoder, cotangent, lengths, order, *params):
    masters, firsts, seconds = params[:7], params[7:14], params[14:]
    in_proj, out_proj, w_up, w_down, head_bias, up_bias, vectors = masters
    low, wide = jnp.bfloat16, jnp.float32
    groups, member = lax.axis_size(C), lax.axis_index(C)
    depth, plane = lax.axis_size(T), lax.axis_index(T)
    shards, shard_index = lax.axis_size(SHARD), lax.axis_index(SHARD)
    row_count, model_width = tokens.shape
    head_width, hidden_width = in_proj.shape[2], w_up.shape[1]
    heads = head_width // HEAD
    shard_rows = in_proj.shape[1]
    rounds = row_count // BLK
    rows = row_count // depth
    per_slice, per_member = rows // BLK, rounds // groups
    all_heads, all_hidden = depth * head_width, depth * hidden_width

    n_vec, n_head, n_up = vectors.size, head_bias.size, up_bias.size
    small = jnp.concatenate([vectors.reshape(-1), head_bias.reshape(-1)])
    first_part = jnp.concatenate(
        [in_proj[0], in_proj[1], in_proj[2], by_shard(small[None], shard_rows)], axis=1
    )
    first_part = lax.all_gather(first_part.astype(low), SHARD, axis=0, tiled=True)
    biases = jnp.concatenate([head_bias[2].reshape(-1), up_bias.reshape(-1)])
    proj_pack = jnp.concatenate(
        [out_proj[0].T, out_proj[1].T, in_proj[3], by_shard(biases[None], shard_rows)], axis=1
    ).astype(low)
    ffn_pack = jnp.concatenate([w_up, w_down.T], axis=1).astype(low)

    def from_planes(array):
        return [array] + [swap(array, T, j) for j in range(1, depth)]

    proj_packs = from_planes(proj_pack)
    w_enc = jnp.concatenate([in_proj[4], in_proj[5]], axis=1).astype(low)
    (w_enc,) = after([w_enc], proj_packs[1:])
    w_enc = lax.all_gather(w_enc, SHARD, axis=0, tiled=True)
    w_self = first_part[:, : 3 * head_width]
    used = -(-(n_vec + n_head) // 128)
    small = first_part.reshape(shards, shard_rows, -1)[:, :used, 3 * head_width :]
    small = small.reshape(shards, -1)
    vec_all = small[:, :n_vec].reshape(shards, 9, -1).transpose(1, 0, 2).reshape(9, -1)
    vec_all = vec_all.astype(wide)

    def by_columns(flat, count):
        return flat.reshape(shards, count, -1).transpose(1, 2, 0).reshape(count, -1).astype(wide)

    bias_heads = by_columns(small[:, n_vec : n_vec + n_head], 4)

    bases = order[0].reshape(groups, rounds, BLK)[:, :, 0]
    cut = lengths[0, 0]
    near = member ^ jnp.arange(groups)
    spot = jnp.arange(rounds)
    q_rounds = (plane ^ (spot // per_slice)) * per_slice + spot % per_slice
    q_bases = jnp.take(lax.dynamic_index_in_dim(bases, member, 0, keepdims=False), q_rounds)
    seg = jnp.stack(
        [
            (q_bases >= cut).astype(jnp.int32),
            (q_bases + BLK - 1 >= cut).astype(jnp.int32),
            jnp.clip(cut - q_bases, 0, BLK),
            jnp.pad(near, (0, rounds - groups)),
            (member * encoder.shape[0] // ENC) ^ jnp.minimum(spot, 1),
        ]
    ).astype(jnp.int32)
    near_bases = jnp.take(bases, near, axis=0)
    meta = jnp.concatenate(
        [
            near_bases,
            q_bases[None],
            jnp.where(q_bases >= cut, cut // (groups * BLK), 0)[None],
            q_rounds[None],
            jnp.full((1, rounds), cut),
        ],
        axis=0,
    ).astype(jnp.int32)
    places = (
        lax.dynamic_slice_in_dim(near_bases, member * per_member, per_member, 1) // BLK
        - member * rounds
    ).reshape(-1)

    qkv = product(tokens, w_self)
    queries = (qkv[:, :head_width] + bias_heads[0]).astype(low)
    queries = jnp.concatenate([pick_rows(queries, plane ^ j, rows) for j in range(depth)])
    no_bias = jnp.zeros((head_width,), wide)
    kv = (qkv[:, head_width:] + jnp.concatenate([no_bias, bias_heads[1]])).astype(low)
    kv = relay_gather(kv)
    ffn_packs = from_planes(after([ffn_pack], kv[:1])[0])
    (w_enc,) = after([w_enc], kv[:1])
    enc_kv = product(encoder, w_enc) + jnp.concatenate([no_bias, bias_heads[3]])
    enc_kv = enc_kv.astype(low)
    *kv[3:], w_kept = after([*kv[3:], w_self], [enc_kv])

    def side_by_side(packs, bounds):
        return jnp.concatenate([pack[:, a:b] for a, b in bounds for pack in packs], axis=1)

    proj_bounds = [(i * head_width, (i + 1) * head_width) for i in range(3)]
    proj_bounds.append((3 * head_width, proj_pack.shape[1]))
    w_proj = side_by_side(proj_packs, proj_bounds)
    w_proj = lax.all_gather(w_proj, SHARD, axis=0, tiled=True)
    (enc_kv,) = after([enc_kv], kv[3:])
    ffn_packs = after(ffn_packs, kv[3:])
    w_one = side_by_side(ffn_packs, [(0, hidden_width)])
    w_one = lax.all_gather(w_one, SHARD, axis=0, tiled=True)
    w_two = side_by_side(ffn_packs, [(hidden_width, 2 * hidden_width)])
    w_two = lax.all_gather(w_two, SHARD, axis=0, tiled=True)
    w_out = w_proj[:, :all_heads], w_proj[:, all_heads : 2 * all_heads]
    w_cross = w_proj[:, 2 * all_heads : 3 * all_heads]
    used = -(-(n_head // 4 + n_up) // 128)
    biases = w_proj.reshape(shards, shard_rows, -1)[:, :used, 3 * all_heads :]
    biases = biases.reshape(shards, used, depth, 128).transpose(0, 2, 1, 3)
    biases = biases.reshape(shards, depth, -1)[:, :, : n_head // 4 + n_up]
    biases = biases.transpose(1, 2, 0).astype(wide)
    bias_cross = biases[:, : n_head // 4].reshape(-1)
    bias_up = biases[:, n_head // 4 :].reshape(-1)

    def heads_to_rows(array):
        return jnp.concatenate(spread(row_blocks(array, depth), T), axis=1)

    def to_heads(array):
        return spread(column_blocks(array, depth), T)

    def rows_to_heads(array):
        return jnp.concatenate(to_heads(array), axis=0)

    def owned(gradient):
        return lax.psum_scatter(gradient.astype(low), SHARD, scatter_dimension=0, tiled=True)

    def updated(index, gradient, scale=None):
        old = masters[index], gradient, firsts[index], seconds[index]
        master, first, second = adamw_step(*old, RATES[index], DECAYS[index])
        if scale is not None:
            master = master * scale
        return master, first, second, master.astype(low)

    self_context, self_lse, peaks = self_fwd(queries, kv, meta)
    self_all = heads_to_rows(self_context)
    enc_kv = relay_gather(enc_kv, [self_all])
    own_tokens = pick_rows(tokens, plane, rows).astype(wide)
    hidden_one = own_tokens + contract_cols(self_all, w_out[0]) + vec_all[0]
    normed_one, unit_one, factor_one = normalize(hidden_one, vec_all[3], vec_all[4])
    low_one = normed_one.astype(low)
    cross_queries = rows_to_heads((product(low_one, w_cross) + bias_cross).astype(low))
    holder = plane * groups // depth
    outgoing = []
    for j in range(groups):
        wanted = lax.dynamic_slice_in_dim(near_bases[j], plane * per_slice, per_slice)
        wanted = jnp.clip(wanted // BLK - member * rounds, 0, rounds - 1)
        picked = [pick_rows(cotangent, wanted[i], BLK) for i in range(per_slice)]
        outgoing.append(jnp.concatenate(picked))
    (peaks,) = after([peaks], [cross_queries])
    top_all = jnp.max(peaks.reshape(-1, heads, BLK), axis=(0, 2))
    for axis in (C, F):
        step = 1
        while step < lax.axis_size(axis):
            top_all = jnp.maximum(top_all, swap(top_all, axis, step))
            step *= 2
    enc_kv[3:] = after(enc_kv[3:], [cross_queries, top_all])
    outgoing = after(outgoing, enc_kv[3:])
    incoming = jnp.where(member == holder, outgoing[0], jnp.zeros_like(outgoing[0]))
    for j in range(1, groups):
        pairs = []
        for level in range(depth):
            source = level * groups // depth
            pairs.append((source * depth + level, (source ^ j) * depth + level))
        incoming = incoming + lax.ppermute(outgoing[j], (C, T), pairs)
    cross_context, cross_lse = cross_fwd(cross_queries, enc_kv, seg)
    cross_all = heads_to_rows(cross_context)
    hidden_two = normed_one + contract_cols(cross_all, w_out[1]) + vec_all[1]
    normed_two, unit_two, factor_two = normalize(hidden_two, vec_all[5], vec_all[6])
    low_two = normed_two.astype(low)
    upward = product(low_two, w_one) + bias_up
    below = 0.5 * (1.0 + lax.erf(upward * 0.5**0.5))
    activated = (upward * below).astype(low)
    slope = below + upward * jnp.exp(-0.5 * upward * upward) * (0.5 / jnp.pi) ** 0.5
    hidden_three = normed_two + contract_cols(activated, w_two) + vec_all[2]
    normed_three, unit_three, factor_three = normalize(hidden_three, vec_all[7], vec_all[8])

    grad_three, gain_three, shift_three = normalize_back(
        incoming.astype(wide), unit_three, factor_three, vec_all[7]
    )
    mlp_grad = grad_three.astype(low)
    grad_w_two = contract_rows(mlp_grad, activated).astype(low)
    act_grad = product(after([mlp_grad], [grad_w_two])[0], w_two).astype(low)
    up_grad = (act_grad.astype(wide) * slope).astype(low)
    grad_up_bias = jnp.sum(up_grad.astype(wide), axis=0)
    grad_two, gain_two, shift_two = normalize_back(
        grad_three + contract_cols(up_grad, w_one), unit_two, factor_two, vec_all[5]
    )
    low_grad_two = grad_two.astype(low)
    cross_grads = product(low_grad_two, w_out[1]).astype(low)
    (up_late,) = after([up_grad], [cross_grads])
    grad_w_one = grad_columns([(low_two, up_late)], [], depth)
    cross_grads = rows_to_heads(cross_grads)
    own_down, own_up = owned(grad_w_two), owned(grad_w_one)
    out_rows = from_planes(after([normed_three.astype(low)], [cross_grads])[0])
    saved = seg, cross_grads, cross_context, cross_lse
    cross_q_grad, far, *halves = cross_bwd(
        1, cross_queries, enc_kv, *saved, cross_queries, [grad_w_two, grad_w_one]
    )
    enc_passed = relay_start(*halves)
    cross_q_grad, *enc_terms = cross_bwd(0, cross_queries, enc_kv, *saved, cross_q_grad, [])
    (cross_q_grad,) = after([cross_q_grad], [*out_rows[1:], *enc_passed, own_down])
    cross_q_all = heads_to_rows(cross_q_grad)
    grad_one, gain_one, shift_one = normalize_back(
        grad_two + contract_cols(cross_q_all, w_cross), unit_one, factor_one, vec_all[3]
    )
    low_grad_one = grad_one.astype(low)
    self_grads = product(low_grad_one, w_out[0]).astype(low)
    grad_vectors = jnp.stack(
        [
            jnp.sum(grad_one, axis=0),
            jnp.sum(grad_two, axis=0),
            jnp.sum(grad_three, axis=0),
            gain_one,
            shift_one,
            gain_two,
            shift_two,
            gain_three,
            shift_three,
        ]
    )
    vec_part = grad_vectors.reshape(9, shards, -1).transpose(1, 0, 2).reshape(shards, -1)
    up_part = grad_up_bias.reshape(depth, -1, shards).transpose(2, 0, 1)
    small_part = [jnp.concatenate([vec_part, up_part[:, j]], axis=1) for j in range(depth)]
    small_part = jnp.concatenate([by_shard(part, shard_rows) for part in small_part], axis=1)
    self_grads = rows_to_heads(self_grads)
    enc_joined = relay_join([*enc_terms, far], enc_passed, [cross_q_all])
    own_down, own_up = after([own_down, own_up], [self_grads, *enc_joined[1:]])
    by_plane = by_plane_order([own_up, own_down], plane, depth)
    ffn = lax.psum_scatter(by_plane, T, scatter_dimension=1, tiled=True)
    enc_terms = relay_finish(enc_joined)
    q_grad, *kv_terms = self_bwd(
        queries, kv, meta, self_grads, self_context, self_lse, [*enc_joined[1:], by_plane]
    )
    kv_passed = relay_start(*kv_terms[3:])
    (cross_late,) = after([cross_q_all], [q_grad])
    grad_proj = grad_columns(
        [(low_grad_two, cross_all), (low_grad_one, self_all), (low_one, cross_late)],
        [small_part.astype(low)],
    )
    own_proj = owned(grad_proj)
    enc_grad, enc_columns = sum_terms(enc_terms, [q_grad])

    enc_parts = plane_shares([enc_grad], w_enc, plane, depth, None, [])
    enc_sent = spread(enc_parts, T)
    grad_w_enc = weight_grad(encoder, [enc_grad], [], plane, 512, enc_parts)
    kv_joined = relay_join(kv_terms, kv_passed, [ffn, grad_w_enc])

    out_rows = after(out_rows, kv_joined[1:])
    out_rows = jnp.stack(out_rows)[plane ^ jnp.arange(depth)].reshape(row_count, model_width)
    portion = row_count // groups
    returned = [pick_rows(out_rows, near[j], portion) for j in range(groups)]
    ffn = after([ffn], kv_joined[1:])[0].astype(wide)
    (down_grad,) = after([ffn[:, hidden_width:].T], kv_joined[1:])
    ffn_new = updated(2, ffn[:, :hidden_width]) + updated(3, down_grad)

    kv_grad, kv_columns = sum_terms(relay_finish(kv_joined), [grad_w_enc, enc_sent[1], *ffn_new, *returned], SOME_COST)
    returned = spread(after(returned, [kv_grad]), C)
    grad_head_bias = jnp.stack(
        [
            jnp.sum(q_grad.astype(wide), axis=0),
            kv_columns[0, head_width:],
            jnp.sum(cross_q_grad.astype(wide), axis=0),
            enc_columns[0, head_width:],
        ]
    )
    head_part = grad_head_bias.reshape(4, -1, shards).transpose(2, 0, 1).reshape(shards, -1)
    head_part = by_shard(head_part, shard_rows).astype(low)
    adds = [head_part, grad_w_enc]
    grad_first = weight_grad(tokens, [q_grad, kv_grad], adds, plane, rows, [], SOME_COST)
    (grad_first,) = after([grad_first], [own_proj])
    token_terms = plane_shares(
        [q_grad, kv_grad], w_kept, plane, depth, grad_one, [grad_first, *enc_sent[2:]], SOME_COST
    )
    token_sent = spread(token_terms, T)
    own_first = owned(grad_first)
    cuts = [0, all_heads, 2 * all_heads, 3 * all_heads, own_proj.shape[1]]
    own_proj = [own_proj[:, a:b] for a, b in zip(cuts, cuts[1:])]
    proj_parts = [column_blocks(part, depth) for part in own_proj]
    proj_parts = [jnp.concatenate([p[j] for p in proj_parts], axis=1) for j in range(depth)]
    own_first, *proj_parts = after([own_first, *proj_parts], token_sent[1:])
    own_first = own_first.astype(wide)
    proj = total(spread(proj_parts, T))
    result = put_blocks(jnp.concatenate(returned), places, wide)
    (token_sent[0],) = after(token_sent[:1], [result])
    grad_tokens = total(token_sent)
    grad_encoder = total(after(enc_sent, [result]))

    out_cross, out_self, in_cross = [
        proj[:, i * head_width : (i + 1) * head_width] for i in range(3)
    ]
    small_part = proj[:, 3 * head_width :].reshape(-1)
    gradients = {
        0: jnp.stack(
            column_blocks(own_first[:, : 3 * head_width], 3)
            + [in_cross]
            + column_blocks(own_first[:, 3 * head_width + 128 :], 2)
        ),
        1: after([jnp.stack([out_self.T, out_cross.T])], token_sent[1:])[0],
        4: own_first[:, 3 * head_width : 3 * head_width + 128].reshape(-1)[:n_head].reshape(head_bias.shape),
        5: small_part[n_vec : n_vec + n_up].reshape(up_bias.shape),
        6: small_part[:n_vec].reshape(vectors.shape),
    }
    clip_factor = CLIP_LIMIT / jnp.maximum(top_all, CLIP_LIMIT)
    root_factor = jnp.sqrt(clip_factor)
    column_roots = jnp.repeat(root_factor, HEAD)
    in_scale = jnp.concatenate(
        [column_roots[None], column_roots[None], jnp.ones((4, head_width), wide)], axis=0
    )[:, None, :]
    slot_heads = (jnp.arange(head_bias.shape[1]) * shards + shard_index) // HEAD
    picked = jnp.sum(
        jnp.where(slot_heads[:, None] == jnp.arange(heads)[None, :], root_factor[None, :], 0.0),
        axis=1,
    )
    bias_scale = jnp.concatenate([picked[None], jnp.ones((3, picked.shape[0]), wide)], axis=0)
    scales = {0: in_scale, 4: bias_scale[:, :, None]}
    results = [result, grad_tokens, grad_encoder, clip_factor]
    for index in range(7):
        if index in gradients:
            results += updated(index, gradients[index], scales.get(index))
        else:
            results += ffn_new[4 * (index - 2) : 4 * (index - 1)]
    return tuple(results)


def solution(mesh):
    rows, table = P(SHARD, None), P(F, None)
    weights = (
        P(None, SHARD, T),
        P(None, T, SHARD),
        P(SHARD, T),
        P(T, SHARD),
        P(None, T, SHARD),
        P(T, SHARD),
        P(None, SHARD),
    )
    by_columns = P(SHARD, T)
    updates = tuple(spec for spec in weights for _ in range(4))
    return jax.shard_map(
        per_device,
        mesh=mesh,
        in_specs=(rows, rows, rows, table, table) + weights * 3,
        out_specs=(rows, by_columns, by_columns, P(T)) + updates,
        check_vma=False,
    )
```

```python
from functools import partial, reduce

import jax
import jax.numpy as jnp
from jax import lax
from jax.experimental import pallas as pl
from jax.experimental.pallas import tpu as pltpu
from jax.sharding import PartitionSpec as P

HEAD = 64
ENC = 4096
STEP = 10
BLK = 128

NEGATIVE = -1e30
NORM_EPS = 1e-05
ADAM_EPS = 1e-08
BETA = 0.5
CLIP_LIMIT = 10.0
RATES = (0.05, 0.3, 0.05, 0.03, 0.3, 0.3, 0.3)
DECAYS = (0.1, 0.1, 0.1, 0.1, 0.0, 0.0, 0.0)
SCALE = HEAD ** (-0.5)
VMEM_BYTES = 56 * 1024 * 1024
F, C, T = "fsdp", "context", "tensor"
SHARD = (F, C)
NO_COST = pl.CostEstimate(flops=0, bytes_accessed=0, transcendentals=0)
SOME_COST = pl.CostEstimate(flops=2 * 10**10, bytes_accessed=2**25, transcendentals=0)


def product(left_side, right_side):
    return jnp.dot(left_side, right_side, preferred_element_type=jnp.float32)


def contract_rows(left_side, right_side):
    return lax.dot_general(
        left_side, right_side, (((0,), (0,)), ((), ())), preferred_element_type=jnp.float32
    )


def contract_cols(left_side, right_side):
    return lax.dot_general(
        left_side, right_side, (((1,), (1,)), ((), ())), preferred_element_type=jnp.float32
    )


def stack_heads(block, heads):
    lanes = lax.broadcasted_iota(jnp.int32, block.shape, 1) // HEAD
    zero = jnp.zeros_like(block)
    return jnp.concatenate([jnp.where(lanes == h, block, zero) for h in range(heads)], axis=0)


def merge_heads(stacked, heads):
    rows = stacked.shape[0] // heads
    lanes = lax.broadcasted_iota(jnp.int32, (rows, stacked.shape[1]), 1) // HEAD
    merged = stacked[:rows]
    for h in range(1, heads):
        merged = jnp.where(lanes == h, stacked[h * rows : (h + 1) * rows], merged)
    return merged


def col_to_row(column):
    return jnp.transpose(jnp.broadcast_to(column, (column.shape[0], 128)))[0:1]


def fold_lanes(tile, combine):
    return reduce(combine, [tile[:, j : j + 128] for j in range(0, tile.shape[1], 128)])


def whole(shape):
    return pl.BlockSpec(shape, lambda i, s: (0,) * len(shape), pipeline_mode=pl.Buffered(1))


def fetch_kv(sources, places, sems):
    copies = [
        pltpu.make_async_copy(source, place, sems.at[i])
        for i, (source, place) in enumerate(zip(sources, places))
    ]

    @pl.when(pl.program_id(0) == 0)
    def _():
        for copy in copies:
            copy.start()
        for copy in copies:
            copy.wait()


def piece_bounds(pieces):
    full, half = pieces[0].shape[0], pieces[3].shape[0]
    return [(0, 0, full), (1, 0, full), (2, 0, full), (3, 0, half), (3, half, half)]


def member_rows(order_ref, row, bounds, full):
    return [
        pl.ds(pl.multiple_of(order_ref[row, j] * full + start, size), size)
        for j, start, size in bounds
    ]


def gate_body(*refs):
    pass


def after(values, others):
    count, every = len(values), [*values, *others]
    return pl.pallas_call(
        gate_body,
        in_specs=[pl.BlockSpec(memory_space=pl.ANY)] * len(every),
        out_specs=[pl.BlockSpec(memory_space=pl.ANY)] * count,
        out_shape=[jax.ShapeDtypeStruct(value.shape, value.dtype) for value in values],
        input_output_aliases={i: i for i in range(count)},
        cost_estimate=NO_COST,
        name="gate",
    )(*every)


def cross_fwd_body(heads, bounds, seg_ref, q_ref, *refs):
    sources, (o_ref, lse_ref, kv_ref, s_ref, sems) = refs[: len(bounds)], refs[len(bounds) :]
    places = member_rows(seg_ref, 3, bounds, sources[0].shape[0])
    fetch_kv(sources, [kv_ref.at[place] for place in places], sems)
    block = pl.program_id(0)
    low, high, cut = seg_ref[0, block], seg_ref[1, block], seg_ref[2, block]
    queries = stack_heads(q_ref[...] * jnp.bfloat16(SCALE), heads)
    rows, width = queries.shape
    tiles, _, step = s_ref.shape

    def attend(sequence):
        def scores(t, highest):
            at = pl.ds(pl.multiple_of(sequence * ENC + t * step, step), step)
            tile = contract_cols(queries, kv_ref[at, :width])
            s_ref[t] = tile
            return jnp.maximum(highest, fold_lanes(tile, jnp.maximum))

        highest = lax.fori_loop(0, tiles, scores, jnp.full((rows, 128), NEGATIVE, jnp.float32))
        peak = jnp.max(highest, axis=1, keepdims=True)

        def weigh(t, running):
            total, summed = running
            at = pl.ds(pl.multiple_of(sequence * ENC + t * step, step), step)
            weights = jnp.exp(s_ref[t] - peak)
            summed = summed + product(weights.astype(jnp.bfloat16), kv_ref[at, width:])
            return total + fold_lanes(weights, jnp.add), summed

        total, summed = lax.fori_loop(
            0,
            tiles,
            weigh,
            (jnp.zeros((rows, 128), jnp.float32), jnp.zeros((rows, width), jnp.float32)),
        )
        total = jnp.sum(total, axis=1, keepdims=True)
        merged = merge_heads(summed / total, heads)
        lse = col_to_row(peak + jnp.log(total))
        place = lax.broadcasted_iota(jnp.int32, merged.shape, 0)
        own = jnp.where(place >= cut, 1, 0) == sequence
        o_ref[...] = jnp.where(own, merged, o_ref[...].astype(jnp.float32)).astype(o_ref.dtype)
        place = lax.broadcasted_iota(jnp.int32, lse.shape, 1) % BLK
        own = jnp.where(place >= cut, 1, 0) == sequence
        lse_ref[0] = jnp.where(own, lse, lse_ref[0])

    o_ref[...] = jnp.zeros_like(o_ref)
    lse_ref[...] = jnp.zeros_like(lse_ref)
    pl.loop(low, high + 1)(attend)


def cross_fwd(queries, enc_kv, seg):
    count, width = queries.shape
    heads, blocks, step = width // HEAD, count // BLK, 1024
    rows, bounds = heads * BLK, piece_bounds(enc_kv)
    enc_all = sum(piece.shape[0] for piece in enc_kv)
    return pl.pallas_call(
        partial(cross_fwd_body, heads, bounds),
        grid_spec=pltpu.PrefetchScalarGridSpec(
            num_scalar_prefetch=1,
            grid=(blocks,),
            in_specs=[pl.BlockSpec((BLK, width), lambda i, s: (i, 0))]
            + [pl.BlockSpec(memory_space=pl.ANY)] * len(bounds),
            out_specs=[
                pl.BlockSpec((BLK, width), lambda i, s: (i, 0)),
                pl.BlockSpec((1, 1, rows), lambda i, s: (i, 0, 0)),
            ],
            scratch_shapes=[
                pltpu.VMEM((enc_all, 2 * width), jnp.bfloat16),
                pltpu.VMEM((ENC // step, rows, step), jnp.float32),
                pltpu.SemaphoreType.DMA((len(bounds),)),
            ],
        ),
        out_shape=[
            jax.ShapeDtypeStruct((count, width), jnp.bfloat16),
            jax.ShapeDtypeStruct((blocks, 1, rows), jnp.float32),
        ],
        compiler_params=pltpu.CompilerParams(vmem_limit_bytes=VMEM_BYTES),
        cost_estimate=NO_COST,
        name="cross_fwd",
    )(seg, queries, *enc_kv)


def cross_bwd_body(heads, bounds, kind, step, seg_ref, q_ref, g_ref, o_ref, lse_ref, *refs):
    count, outs = len(bounds), refs[-len(bounds) - 4 : -3]
    sources, prior, (dq_ref, *outs) = refs[:count], refs[count], outs
    kv_ref, acc_ref, sems = refs[-3:]
    block = pl.program_id(0)
    sequence, full = seg_ref[4, kind], ENC // 2
    places = [
        pl.ds(pl.multiple_of(seg_ref[3, j] * full + at - sequence * ENC, size), size)
        for j, at, size in bounds
    ]
    fetch_kv(sources, [kv_ref.at[place] for place in places], sems)

    @pl.when(block == 0)
    def _():
        acc_ref[...] = jnp.zeros_like(acc_ref)

    seen = (seg_ref[0, block] <= sequence) & (seg_ref[1, block] >= sequence)
    start = prior[...] if kind == 0 else jnp.zeros_like(dq_ref)
    dq_ref[...] = start

    @pl.when(seen)
    def _():
        queries = stack_heads(q_ref[...] * jnp.bfloat16(SCALE), heads)
        rows, width = queries.shape
        grads = stack_heads(g_ref[...], heads)
        dots = g_ref[...].astype(jnp.float32) * o_ref[...].astype(jnp.float32)
        dot_row = col_to_row(jnp.sum(stack_heads(dots, heads), axis=1, keepdims=True))
        place = lax.broadcasted_iota(jnp.int32, lse_ref[0].shape, 1) % BLK
        own_seq = jnp.where(place >= seg_ref[2, block], 1, 0)
        lse = jnp.where(own_seq == sequence, lse_ref[0], -NEGATIVE)

        def tile_terms(t, q_grad):
            at = pl.ds(pl.multiple_of(t * step, step), step)
            keys, values = kv_ref[at, :width], kv_ref[at, width:]
            probs = jnp.exp(contract_cols(keys, queries) - lse)
            s_grad = (probs * (contract_cols(values, grads) - dot_row)).astype(jnp.bfloat16)
            acc_ref[at, width:] += product(probs.astype(jnp.bfloat16), grads)
            acc_ref[at, :width] += product(s_grad, queries)
            return q_grad + contract_rows(s_grad, keys)

        q_grad = lax.fori_loop(
            0, ENC // step, tile_terms, jnp.zeros((rows, width), jnp.float32)
        )
        q_grad = merge_heads(q_grad, heads) * SCALE + start.astype(jnp.float32)
        dq_ref[...] = q_grad.astype(dq_ref.dtype)

    @pl.when(block == pl.num_programs(0) - 1)
    def _():
        for out, place in zip(outs, places):
            out[...] = acc_ref[place, :].astype(out.dtype)


def cross_bwd(kind, queries, enc_kv, seg, grads, context, lse, prior, others):
    count, width = queries.shape
    heads, blocks, step = width // HEAD, count // BLK, 2048
    bounds = piece_bounds(enc_kv)
    picked = [(0, 1), (2, 3, 4)][kind]
    pieces, bounds = [enc_kv[i] for i in picked], [bounds[i] for i in picked]
    row = pl.BlockSpec((BLK, width), lambda i, s: (i, 0))
    return pl.pallas_call(
        partial(cross_bwd_body, heads, bounds, kind, step),
        grid_spec=pltpu.PrefetchScalarGridSpec(
            num_scalar_prefetch=1,
            grid=(blocks,),
            in_specs=[row, row, row, pl.BlockSpec((1, 1, heads * BLK), lambda i, s: (i, 0, 0))]
            + [pl.BlockSpec(memory_space=pl.ANY)] * len(bounds)
            + [row]
            + [pl.BlockSpec(memory_space=pl.ANY)] * len(others),
            out_specs=[row] + [whole(piece.shape) for piece in pieces],
            scratch_shapes=[
                pltpu.VMEM((ENC, 2 * width), jnp.bfloat16),
                pltpu.VMEM((ENC, 2 * width), jnp.float32),
                pltpu.SemaphoreType.DMA((len(bounds),)),
            ],
        ),
        out_shape=[jax.ShapeDtypeStruct((count, width), jnp.bfloat16)]
        + [jax.ShapeDtypeStruct(piece.shape, jnp.bfloat16) for piece in pieces],
        compiler_params=pltpu.CompilerParams(vmem_limit_bytes=VMEM_BYTES),
        cost_estimate=NO_COST,
        name="cross_bwd",
    )(seg, queries, grads, context, lse, *pieces, prior, *others)


def gather_tile(kv_ref, t, columns):
    at = pl.ds(pl.multiple_of(t * BLK, BLK), BLK)
    return jnp.concatenate([kv_ref[j, at, columns] for j in range(kv_ref.shape[0])], axis=0)


def self_fwd_body(heads, bounds, meta_ref, q_ref, *refs):
    sources, (o_ref, lse_ref, top_ref, kv_refs, sems) = refs[: len(bounds)], refs[len(bounds) :]
    fetch_kv(sources, [kv_refs.at[j, pl.ds(at, size)] for j, at, size in bounds], sems)
    groups = kv_refs.shape[0]
    block = pl.program_id(0)
    base, first, last = [meta_ref[groups + k, block] for k in range(3)]
    cut = meta_ref[groups + 3, 0]
    queries = stack_heads(q_ref[...] * jnp.bfloat16(SCALE), heads)
    rows, width = queries.shape
    q_pos = base + lax.broadcasted_iota(jnp.int32, (rows, BLK), 0) % BLK
    q_start = jnp.where(q_pos >= cut, cut, 0)
    lane = lax.broadcasted_iota(jnp.int32, (rows, BLK), 1)

    def visit(t, running):
        peak, total, summed = running
        raw = contract_cols(queries, gather_tile(kv_refs, t, slice(0, width)))
        parts = []
        for d in range(groups):
            k_pos = lane + meta_ref[d, t]
            seen = (k_pos <= q_pos) & (k_pos >= q_start)
            parts.append(jnp.where(seen, raw[:, d * BLK : (d + 1) * BLK], NEGATIVE))
        new_peak = jnp.maximum(peak, jnp.max(reduce(jnp.maximum, parts), axis=1, keepdims=True))
        weights = [jnp.exp(part - new_peak) for part in parts]
        shrink = jnp.exp(peak - new_peak)
        total = total * shrink + jnp.sum(reduce(jnp.add, weights), axis=1, keepdims=True)
        low_weights = jnp.concatenate(weights, axis=1).astype(jnp.bfloat16)
        values = gather_tile(kv_refs, t, slice(width, 2 * width))
        return new_peak, total, summed * shrink + product(low_weights, values)

    peak, total, summed = lax.fori_loop(
        first,
        last + 1,
        visit,
        (
            jnp.full((rows, 1), NEGATIVE, jnp.float32),
            jnp.zeros((rows, 1), jnp.float32),
            jnp.zeros((rows, width), jnp.float32),
        ),
    )
    o_ref[...] = merge_heads(summed / total, heads).astype(o_ref.dtype)
    lse_ref[0] = col_to_row(peak + jnp.log(total))
    top_ref[0] = col_to_row(peak)


def self_fwd(queries, kv, meta):
    count, width = queries.shape
    heads, blocks, bounds = width // HEAD, count // BLK, piece_bounds(kv)
    rows, kept = heads * BLK, (bounds[-1][0] + 1,) + kv[0].shape
    row = pl.BlockSpec((BLK, width), lambda i, s: (i, 0))
    stat = pl.BlockSpec((1, 1, rows), lambda i, s: (i, 0, 0))
    return pl.pallas_call(
        partial(self_fwd_body, heads, bounds),
        grid_spec=pltpu.PrefetchScalarGridSpec(
            num_scalar_prefetch=1,
            grid=(blocks,),
            in_specs=[row] + [pl.BlockSpec(memory_space=pl.ANY)] * len(bounds),
            out_specs=[row, stat, stat],
            scratch_shapes=[
                pltpu.VMEM(kept, jnp.bfloat16),
                pltpu.SemaphoreType.DMA((len(bounds),)),
            ],
        ),
        out_shape=[jax.ShapeDtypeStruct((count, width), jnp.bfloat16)]
        + [jax.ShapeDtypeStruct((blocks, 1, rows), jnp.float32)] * 2,
        compiler_params=pltpu.CompilerParams(vmem_limit_bytes=VMEM_BYTES),
        cost_estimate=NO_COST,
        name="self_fwd",
    )(meta, queries, *kv)


def self_bwd_body(heads, bounds, waits, meta_ref, q_ref, g_ref, o_ref, lse_ref, *refs):
    count = len(bounds)
    sources, (dq_ref, *outs) = refs[:count], refs[count + waits : 2 * count + waits + 1]
    kv_refs, acc_ref, sems = refs[2 * count + waits + 1 :]
    fetch_kv(sources, [kv_refs.at[j, pl.ds(at, size)] for j, at, size in bounds], sems)
    groups = kv_refs.shape[0]
    block = pl.program_id(0)

    @pl.when(block == 0)
    def _():
        acc_ref[...] = jnp.zeros_like(acc_ref)

    base, first, last = [meta_ref[groups + k, block] for k in range(3)]
    cut = meta_ref[groups + 3, 0]
    queries = stack_heads(q_ref[...] * jnp.bfloat16(SCALE), heads)
    rows, width = queries.shape
    grads = stack_heads(g_ref[...], heads)
    dots = g_ref[...].astype(jnp.float32) * o_ref[...].astype(jnp.float32)
    dot_row = col_to_row(jnp.sum(stack_heads(dots, heads), axis=1, keepdims=True))
    lse = lse_ref[0]
    q_pos = base + lax.broadcasted_iota(jnp.int32, lse.shape, 1) % BLK
    q_start = jnp.where(q_pos >= cut, cut, 0)
    sub = lax.broadcasted_iota(jnp.int32, (BLK, rows), 0)

    def tile_terms(t, q_grad):
        at = pl.ds(pl.multiple_of(t * BLK, BLK), BLK)
        keys = gather_tile(kv_refs, t, slice(0, width))
        values = gather_tile(kv_refs, t, slice(width, 2 * width))
        raw = contract_cols(keys, queries)
        parts = []
        for d in range(groups):
            k_base = meta_ref[d, t]
            seen = (sub <= q_pos - k_base) & (sub >= q_start - k_base)
            parts.append(jnp.where(seen, jnp.exp(raw[d * BLK : (d + 1) * BLK] - lse), 0.0))
        probs = jnp.concatenate(parts, axis=0)
        s_grad = (probs * (contract_cols(values, grads) - dot_row)).astype(jnp.bfloat16)
        acc_ref[:, at, width:] += product(probs.astype(jnp.bfloat16), grads).reshape(
            groups, BLK, width
        )
        acc_ref[:, at, :width] += product(s_grad, queries).reshape(groups, BLK, width)
        return q_grad + contract_rows(s_grad, keys)

    q_grad = lax.fori_loop(first, last + 1, tile_terms, jnp.zeros((rows, width), jnp.float32))
    dq_ref[...] = (merge_heads(q_grad, heads) * SCALE).astype(dq_ref.dtype)

    @pl.when(block == pl.num_programs(0) - 1)
    def _():
        for out, (j, at, size) in zip(outs, bounds):
            out[...] = acc_ref[j, at : at + size].astype(out.dtype)


def self_bwd(queries, kv, meta, grads, context, lse, others):
    count, width = queries.shape
    heads, blocks, bounds = width // HEAD, count // BLK, piece_bounds(kv)
    rows, kept = heads * BLK, (bounds[-1][0] + 1,) + kv[0].shape
    row = pl.BlockSpec((BLK, width), lambda i, s: (i, 0))
    stat = pl.BlockSpec((1, 1, rows), lambda i, s: (i, 0, 0))
    return pl.pallas_call(
        partial(self_bwd_body, heads, bounds, len(others)),
        grid_spec=pltpu.PrefetchScalarGridSpec(
            num_scalar_prefetch=1,
            grid=(blocks,),
            in_specs=[row, row, row, stat]
            + [pl.BlockSpec(memory_space=pl.ANY)] * (len(bounds) + len(others)),
            out_specs=[row] + [whole(piece.shape) for piece in kv],
            scratch_shapes=[
                pltpu.VMEM(kept, jnp.bfloat16),
                pltpu.VMEM(kept, jnp.float32),
                pltpu.SemaphoreType.DMA((len(bounds),)),
            ],
        ),
        out_shape=[jax.ShapeDtypeStruct((count, width), jnp.bfloat16)]
        + [jax.ShapeDtypeStruct(piece.shape, jnp.bfloat16) for piece in kv],
        compiler_params=pltpu.CompilerParams(vmem_limit_bytes=VMEM_BYTES),
        cost_estimate=NO_COST,
        name="self_bwd",
    )(meta, queries, grads, context, lse, *kv, *others)


def move_body(index_ref, in_ref, out_ref):
    out_ref[...] = in_ref[...].astype(out_ref.dtype)


def put_blocks(rows, index, dtype):
    count, width = rows.shape
    return pl.pallas_call(
        move_body,
        grid_spec=pltpu.PrefetchScalarGridSpec(
            num_scalar_prefetch=1,
            grid=(count // BLK,),
            in_specs=[pl.BlockSpec((BLK, width), lambda i, s: (i, 0))],
            out_specs=pl.BlockSpec((BLK, width), lambda i, s: (s[i], 0)),
        ),
        out_shape=jax.ShapeDtypeStruct((count, width), dtype),
        cost_estimate=SOME_COST,
        name="put_blocks",
    )(index, rows)


def join_body(whole_ref, passed_ref, *refs):
    total = whole_ref[...].astype(jnp.float32) + passed_ref[...].astype(jnp.float32)
    refs[-1][...] = total.astype(refs[-1].dtype)


def add_half(whole_rows, passed, lower, others):
    half, width = passed.shape
    size = min(half, 256)
    first = half // size if lower else 0
    part = pl.BlockSpec((size, width), lambda i: (first + i, 0))
    return pl.pallas_call(
        join_body,
        grid=(half // size,),
        in_specs=[part, pl.BlockSpec((size, width), lambda i: (i, 0))]
        + [pl.BlockSpec(memory_space=pl.ANY)] * len(others),
        out_specs=part,
        out_shape=jax.ShapeDtypeStruct(whole_rows.shape, whole_rows.dtype),
        input_output_aliases={0: 0},
        cost_estimate=NO_COST,
        name="add_half",
    )(whole_rows, passed, *others)


def grad_body(count, *refs):
    out_ref, start = refs[-1], 0
    for k in range(count):
        terms = contract_rows(refs[2 * k][...], refs[2 * k + 1][...])
        out_ref[:, start : start + terms.shape[1]] = terms.astype(out_ref.dtype)
        start += terms.shape[1]
    for ref in refs[2 * count : -1]:
        out_ref[:, start : start + ref.shape[1]] = ref[...]
        start += ref.shape[1]


def grad_columns(pairs, others, tiles=1):
    flat = [array for pair in pairs for array in pair]
    width = pairs[0][0].shape[1]
    columns = sum(right.shape[1] for _, right in pairs) + sum(array.shape[1] for array in others)
    size = pairs[0][1].shape[0]
    if tiles == 1:
        specs = [pl.BlockSpec(array.shape, lambda i: (0, 0)) for array in flat + others]
    else:
        specs = [
            pl.BlockSpec((size, width), lambda i: (0, 0)),
            pl.BlockSpec((size, columns // tiles), lambda i: (0, i)),
        ]
    return pl.pallas_call(
        partial(grad_body, len(pairs)),
        grid=(tiles,),
        in_specs=specs,
        out_specs=pl.BlockSpec((width, columns // tiles), lambda i: (0, i)),
        out_shape=jax.ShapeDtypeStruct((width, columns), jnp.bfloat16),
        compiler_params=pltpu.CompilerParams(vmem_limit_bytes=VMEM_BYTES),
        cost_estimate=NO_COST,
        name="grad_columns",
    )(*flat, *others)


def plane_body(plane_ref, *refs):
    start = 0
    for ref in refs[:-1]:
        refs[-1][:, start : start + ref.shape[1]] = ref[...]
        start += ref.shape[1]


def by_plane_order(arrays, plane, depth):
    size = arrays[0].shape[0]
    widths = [array.shape[1] // depth for array in arrays]
    return pl.pallas_call(
        plane_body,
        grid_spec=pltpu.PrefetchScalarGridSpec(
            num_scalar_prefetch=1,
            grid=(depth,),
            in_specs=[pl.BlockSpec((size, width), lambda p, s: (0, s[0] ^ p)) for width in widths],
            out_specs=pl.BlockSpec((size, sum(widths)), lambda p, s: (0, p)),
        ),
        out_shape=jax.ShapeDtypeStruct((size, depth * sum(widths)), arrays[0].dtype),
        cost_estimate=NO_COST,
        name="by_plane_order",
    )(plane.reshape(1).astype(jnp.int32), *arrays)


ANYWHERE = pl.BlockSpec(memory_space=pl.ANY)


def sum_body(count, *refs):
    out_ref, column_ref = refs[-2:]
    added = reduce(jnp.add, [ref[...].astype(jnp.float32) for ref in refs[:count]])
    rounded = added.astype(out_ref.dtype)
    out_ref[...] = rounded

    @pl.when(pl.program_id(0) == 0)
    def _():
        column_ref[...] = jnp.zeros_like(column_ref)

    column_ref[...] += jnp.sum(rounded.astype(jnp.float32), axis=0, keepdims=True)


def sum_terms(terms, others, cost=SOME_COST):
    count, width = terms[0].shape
    size = 256
    tile = pl.BlockSpec((size, width), lambda i: (i, 0))
    return pl.pallas_call(
        partial(sum_body, len(terms)),
        grid=(count // size,),
        in_specs=[tile] * len(terms) + [ANYWHERE] * len(others),
        out_specs=[tile, pl.BlockSpec((1, width), lambda i: (0, 0))],
        out_shape=[
            jax.ShapeDtypeStruct((count, width), jnp.bfloat16),
            jax.ShapeDtypeStruct((1, width), jnp.float32),
        ],
        cost_estimate=cost,
        name="sum_terms",
    )(*terms, *others)


def share_body(depth, parts, extra, plane_ref, *refs):
    rows = [ref[...] for ref in refs[:parts]]
    merged = rows[0] if parts == 1 else jnp.concatenate(rows, axis=1)
    own = pl.program_id(0) == plane_ref[0]
    for j in range(depth):
        term = contract_cols(merged, refs[parts + j][...])
        if extra:
            term = term + jnp.where(own, refs[parts + depth + j][...], 0.0)
        refs[len(refs) - depth + j][...] = term.astype(jnp.bfloat16)


def plane_shares(arrays, weight, plane, depth, extra, others, cost=SOME_COST):
    count, size = arrays[-1].shape[0], 256 if extra is None else extra.shape[0]
    part = weight.shape[0] // depth
    last = pl.BlockSpec((size, arrays[-1].shape[1]), lambda i, s: (i, 0))
    specs = [last]
    if len(arrays) == 2:
        specs = [pl.BlockSpec((size, arrays[0].shape[1]), lambda i, s: (s[0] ^ i, 0)), last]
    for j in range(depth):
        specs.append(
            pl.BlockSpec((part, weight.shape[1]), partial(lambda j, i, s: (s[0] ^ j, 0), j))
        )
    inputs = [*arrays, *[weight] * depth]
    if extra is not None:
        for j in range(depth):
            specs.append(pl.BlockSpec((size, part), partial(lambda j, i, s: (0, s[0] ^ j), j)))
        inputs += [extra] * depth
    return pl.pallas_call(
        partial(share_body, depth, len(arrays), extra is not None),
        grid_spec=pltpu.PrefetchScalarGridSpec(
            num_scalar_prefetch=1,
            grid=(count // size,),
            in_specs=specs + [ANYWHERE] * len(others),
            out_specs=[pl.BlockSpec((size, part), lambda i, s: (i, 0))] * depth,
        ),
        out_shape=[jax.ShapeDtypeStruct((count, part), jnp.bfloat16)] * depth,
        compiler_params=pltpu.CompilerParams(vmem_limit_bytes=VMEM_BYTES),
        cost_estimate=cost,
        name="plane_shares",
    )(plane.reshape(1).astype(jnp.int32), *inputs, *others)


def gather_grad_body(parts, adds, plane_ref, left_ref, *refs):
    out_ref, acc_ref = refs[-2:]
    step = pl.program_id(0)

    @pl.when(step == 0)
    def _():
        acc_ref[...] = jnp.zeros_like(acc_ref)

    start = 0
    for ref in refs[:parts]:
        stop = start + ref.shape[1]
        acc_ref[:, start:stop] += contract_rows(left_ref[...], ref[...])
        start = stop

    @pl.when(step == pl.num_programs(0) - 1)
    def _():
        out_ref[:, :start] = acc_ref[...].astype(out_ref.dtype)
        at = start
        for ref in refs[parts : parts + adds]:
            out_ref[:, at : at + ref.shape[1]] = ref[...]
            at += ref.shape[1]


def weight_grad(left, arrays, adds, plane, size, others, cost=SOME_COST):
    count, width = left.shape
    last = pl.BlockSpec((size, arrays[-1].shape[1]), lambda i, s: (i, 0))
    specs = [pl.BlockSpec((size, width), lambda i, s: (i, 0)), last]
    if len(arrays) == 2:
        specs.insert(1, pl.BlockSpec((size, arrays[0].shape[1]), lambda i, s: (s[0] ^ i, 0)))
    made = sum(array.shape[1] for array in arrays)
    columns = made + sum(array.shape[1] for array in adds)
    specs += [whole(array.shape) for array in adds] + [ANYWHERE] * len(others)
    return pl.pallas_call(
        partial(gather_grad_body, len(arrays), len(adds)),
        grid_spec=pltpu.PrefetchScalarGridSpec(
            num_scalar_prefetch=1,
            grid=(count // size,),
            in_specs=specs,
            out_specs=pl.BlockSpec((width, columns), lambda i, s: (0, 0)),
            scratch_shapes=[pltpu.VMEM((width, made), jnp.float32)],
        ),
        out_shape=jax.ShapeDtypeStruct((width, columns), jnp.bfloat16),
        compiler_params=pltpu.CompilerParams(vmem_limit_bytes=VMEM_BYTES),
        cost_estimate=cost,
        name="weight_grad",
    )(plane.reshape(1).astype(jnp.int32), left, *arrays, *adds, *others)


def normalize(hidden, gain_row, shift_row):
    centred = hidden - jnp.mean(hidden, axis=-1, keepdims=True)
    factor = lax.rsqrt(jnp.mean(centred * centred, axis=-1, keepdims=True) + NORM_EPS)
    unit_rows = centred * factor
    return (unit_rows * gain_row + shift_row, unit_rows, factor)


def normalize_back(incoming, unit_rows, factor, gain_row):
    scaled = incoming * gain_row
    centred_grad = (
        scaled
        - jnp.mean(scaled, axis=-1, keepdims=True)
        - unit_rows * jnp.mean(scaled * unit_rows, axis=-1, keepdims=True)
    )
    return (factor * centred_grad, jnp.sum(incoming * unit_rows, axis=0), jnp.sum(incoming, axis=0))


def adamw_step(master, gradient, first_moment, second_moment, step_rate, weight_decay):
    first_moment = BETA * first_moment + (1.0 - BETA) * gradient
    second_moment = BETA * second_moment + (1.0 - BETA) * gradient * gradient
    correction = 1.0 - BETA**STEP
    update = first_moment / correction / (jnp.sqrt(second_moment / correction) + ADAM_EPS)
    return (master - step_rate * (update + weight_decay * master), first_moment, second_moment)
def swap(value, axis, j):
    return lax.ppermute(value, axis, [(i, i ^ j) for i in range(lax.axis_size(axis))])


def spread(blocks, axis):
    return [blocks[0]] + [swap(blocks[j], axis, j) for j in range(1, len(blocks))]


def total(blocks):
    return reduce(jnp.add, [block.astype(jnp.float32) for block in blocks])


def column_blocks(array, count):
    size = array.shape[1] // count
    return [array[:, j * size : (j + 1) * size] for j in range(count)]


def row_blocks(array, count):
    size = array.shape[0] // count
    return [array[j * size : (j + 1) * size] for j in range(count)]


def pick_rows(array, index, size):
    return lax.dynamic_slice_in_dim(array, index * size, size, 0)


def by_shard(flat, shard_rows):
    shards, used = flat.shape
    flat = jnp.pad(flat, ((0, 0), (0, -used % 128))).reshape(shards, -1, 128)
    return jnp.pad(flat, ((0, 0), (0, shard_rows - flat.shape[1]), (0, 0))).reshape(-1, 128)


def relay_gather(block, others=()):
    near, far = swap(block, C, 1), swap(block, C, 2)
    if others:
        near, far = after([near, far], others)
    half = block.shape[0] // 2
    return [block, near, far, swap(far[:half], C, 1), swap(near[half:], C, 2)]


def relay_start(upper, lower):
    return swap(upper, C, 1), swap(lower, C, 2)


def relay_join(terms, passed, others=()):
    own, near, far = terms[:3]
    return own, add_half(near, passed[1], True, others), add_half(far, passed[0], False, others)


def relay_finish(joined):
    own, near, far = joined
    return [own, swap(near, C, 1), swap(far, C, 2)]


def per_device(tokens, encoder, cotangent, lengths, order, *params):
    masters, firsts, seconds = params[:7], params[7:14], params[14:]
    in_proj, out_proj, w_up, w_down, head_bias, up_bias, vectors = masters
    low, wide = jnp.bfloat16, jnp.float32
    groups, member = lax.axis_size(C), lax.axis_index(C)
    depth, plane = lax.axis_size(T), lax.axis_index(T)
    shards, shard_index = lax.axis_size(SHARD), lax.axis_index(SHARD)
    row_count, model_width = tokens.shape
    head_width, hidden_width = in_proj.shape[2], w_up.shape[1]
    heads = head_width // HEAD
    shard_rows = in_proj.shape[1]
    rounds = row_count // BLK
    rows = row_count // depth
    per_slice, per_member = rows // BLK, rounds // groups
    all_heads, all_hidden = depth * head_width, depth * hidden_width

    n_vec, n_head, n_up = vectors.size, head_bias.size, up_bias.size
    small = jnp.concatenate([vectors.reshape(-1), head_bias.reshape(-1)])
    first_part = jnp.concatenate(
        [in_proj[0], in_proj[1], in_proj[2], by_shard(small[None], shard_rows)], axis=1
    )
    first_part = lax.all_gather(first_part.astype(low), SHARD, axis=0, tiled=True)
    biases = jnp.concatenate([head_bias[2].reshape(-1), up_bias.reshape(-1)])
    proj_pack = jnp.concatenate(
        [out_proj[0].T, out_proj[1].T, in_proj[3], by_shard(biases[None], shard_rows)], axis=1
    ).astype(low)
    ffn_pack = jnp.concatenate([w_up, w_down.T], axis=1).astype(low)

    def from_planes(array):
        return [array] + [swap(array, T, j) for j in range(1, depth)]

    proj_packs = from_planes(proj_pack)
    w_enc = jnp.concatenate([in_proj[4], in_proj[5]], axis=1).astype(low)
    (w_enc,) = after([w_enc], proj_packs[1:])
    w_enc = lax.all_gather(w_enc, SHARD, axis=0, tiled=True)
    w_self = first_part[:, : 3 * head_width]
    used = -(-(n_vec + n_head) // 128)
    small = first_part.reshape(shards, shard_rows, -1)[:, :used, 3 * head_width :]
    small = small.reshape(shards, -1)
    vec_all = small[:, :n_vec].reshape(shards, 9, -1).transpose(1, 0, 2).reshape(9, -1)
    vec_all = vec_all.astype(wide)

    def by_columns(flat, count):
        return flat.reshape(shards, count, -1).transpose(1, 2, 0).reshape(count, -1).astype(wide)

    bias_heads = by_columns(small[:, n_vec : n_vec + n_head], 4)

    bases = order[0].reshape(groups, rounds, BLK)[:, :, 0]
    cut = lengths[0, 0]
    near = member ^ jnp.arange(groups)
    spot = jnp.arange(rounds)
    q_rounds = (plane ^ (spot // per_slice)) * per_slice + spot % per_slice
    q_bases = jnp.take(lax.dynamic_index_in_dim(bases, member, 0, keepdims=False), q_rounds)
    seg = jnp.stack(
        [
            (q_bases >= cut).astype(jnp.int32),
            (q_bases + BLK - 1 >= cut).astype(jnp.int32),
            jnp.clip(cut - q_bases, 0, BLK),
            jnp.pad(near, (0, rounds - groups)),
            (member * encoder.shape[0] // ENC) ^ jnp.minimum(spot, 1),
        ]
    ).astype(jnp.int32)
    near_bases = jnp.take(bases, near, axis=0)
    meta = jnp.concatenate(
        [
            near_bases,
            q_bases[None],
            jnp.where(q_bases >= cut, cut // (groups * BLK), 0)[None],
            q_rounds[None],
            jnp.full((1, rounds), cut),
        ],
        axis=0,
    ).astype(jnp.int32)
    places = (
        lax.dynamic_slice_in_dim(near_bases, member * per_member, per_member, 1) // BLK
        - member * rounds
    ).reshape(-1)

    qkv = product(tokens, w_self)
    queries = (qkv[:, :head_width] + bias_heads[0]).astype(low)
    queries = jnp.concatenate([pick_rows(queries, plane ^ j, rows) for j in range(depth)])
    no_bias = jnp.zeros((head_width,), wide)
    kv = (qkv[:, head_width:] + jnp.concatenate([no_bias, bias_heads[1]])).astype(low)
    kv = relay_gather(kv)
    ffn_packs = from_planes(after([ffn_pack], kv[:1])[0])
    (w_enc,) = after([w_enc], kv[:1])
    enc_kv = product(encoder, w_enc) + jnp.concatenate([no_bias, bias_heads[3]])
    enc_kv = enc_kv.astype(low)
    *kv[3:], w_kept = after([*kv[3:], w_self], [enc_kv])

    def side_by_side(packs, bounds):
        return jnp.concatenate([pack[:, a:b] for a, b in bounds for pack in packs], axis=1)

    proj_bounds = [(i * head_width, (i + 1) * head_width) for i in range(3)]
    proj_bounds.append((3 * head_width, proj_pack.shape[1]))
    w_proj = side_by_side(proj_packs, proj_bounds)
    w_proj = lax.all_gather(w_proj, SHARD, axis=0, tiled=True)
    (enc_kv,) = after([enc_kv], kv[3:])
    ffn_packs = after(ffn_packs, kv[3:])
    w_one = side_by_side(ffn_packs, [(0, hidden_width)])
    w_one = lax.all_gather(w_one, SHARD, axis=0, tiled=True)
    w_two = side_by_side(ffn_packs, [(hidden_width, 2 * hidden_width)])
    w_two = lax.all_gather(w_two, SHARD, axis=0, tiled=True)
    w_out = w_proj[:, :all_heads], w_proj[:, all_heads : 2 * all_heads]
    w_cross = w_proj[:, 2 * all_heads : 3 * all_heads]
    used = -(-(n_head // 4 + n_up) // 128)
    biases = w_proj.reshape(shards, shard_rows, -1)[:, :used, 3 * all_heads :]
    biases = biases.reshape(shards, used, depth, 128).transpose(0, 2, 1, 3)
    biases = biases.reshape(shards, depth, -1)[:, :, : n_head // 4 + n_up]
    biases = biases.transpose(1, 2, 0).astype(wide)
    bias_cross = biases[:, : n_head // 4].reshape(-1)
    bias_up = biases[:, n_head // 4 :].reshape(-1)

    def heads_to_rows(array):
        return jnp.concatenate(spread(row_blocks(array, depth), T), axis=1)

    def to_heads(array):
        return spread(column_blocks(array, depth), T)

    def rows_to_heads(array):
        return jnp.concatenate(to_heads(array), axis=0)

    def owned(gradient):
        return lax.psum_scatter(gradient.astype(low), SHARD, scatter_dimension=0, tiled=True)

    def updated(index, gradient, scale=None):
        old = masters[index], gradient, firsts[index], seconds[index]
        master, first, second = adamw_step(*old, RATES[index], DECAYS[index])
        if scale is not None:
            master = master * scale
        return master, first, second, master.astype(low)

    self_context, self_lse, peaks = self_fwd(queries, kv, meta)
    self_all = heads_to_rows(self_context)
    enc_kv = relay_gather(enc_kv, [self_all])
    own_tokens = pick_rows(tokens, plane, rows).astype(wide)
    hidden_one = own_tokens + contract_cols(self_all, w_out[0]) + vec_all[0]
    normed_one, unit_one, factor_one = normalize(hidden_one, vec_all[3], vec_all[4])
    low_one = normed_one.astype(low)
    cross_queries = rows_to_heads((product(low_one, w_cross) + bias_cross).astype(low))
    holder = plane * groups // depth
    outgoing = []
    for j in range(groups):
        wanted = lax.dynamic_slice_in_dim(near_bases[j], plane * per_slice, per_slice)
        wanted = jnp.clip(wanted // BLK - member * rounds, 0, rounds - 1)
        picked = [pick_rows(cotangent, wanted[i], BLK) for i in range(per_slice)]
        outgoing.append(jnp.concatenate(picked))
    (peaks,) = after([peaks], [cross_queries])
    top_all = jnp.max(peaks.reshape(-1, heads, BLK), axis=(0, 2))
    for axis in (C, F):
        step = 1
        while step < lax.axis_size(axis):
            top_all = jnp.maximum(top_all, swap(top_all, axis, step))
            step *= 2
    enc_kv[3:] = after(enc_kv[3:], [cross_queries, top_all])
    outgoing = after(outgoing, enc_kv[3:])
    incoming = jnp.where(member == holder, outgoing[0], jnp.zeros_like(outgoing[0]))
    for j in range(1, groups):
        pairs = []
        for level in range(depth):
            source = level * groups // depth
            pairs.append((source * depth + level, (source ^ j) * depth + level))
        incoming = incoming + lax.ppermute(outgoing[j], (C, T), pairs)
    cross_context, cross_lse = cross_fwd(cross_queries, enc_kv, seg)
    cross_all = heads_to_rows(cross_context)
    hidden_two = normed_one + contract_cols(cross_all, w_out[1]) + vec_all[1]
    normed_two, unit_two, factor_two = normalize(hidden_two, vec_all[5], vec_all[6])
    low_two = normed_two.astype(low)
    upward = product(low_two, w_one) + bias_up
    below = 0.5 * (1.0 + lax.erf(upward * 0.5**0.5))
    activated = (upward * below).astype(low)
    slope = below + upward * jnp.exp(-0.5 * upward * upward) * (0.5 / jnp.pi) ** 0.5
    hidden_three = normed_two + contract_cols(activated, w_two) + vec_all[2]
    normed_three, unit_three, factor_three = normalize(hidden_three, vec_all[7], vec_all[8])

    grad_three, gain_three, shift_three = normalize_back(
        incoming.astype(wide), unit_three, factor_three, vec_all[7]
    )
    mlp_grad = grad_three.astype(low)
    grad_w_two = contract_rows(mlp_grad, activated).astype(low)
    act_grad = product(after([mlp_grad], [grad_w_two])[0], w_two).astype(low)
    up_grad = (act_grad.astype(wide) * slope).astype(low)
    grad_up_bias = jnp.sum(up_grad.astype(wide), axis=0)
    grad_two, gain_two, shift_two = normalize_back(
        grad_three + contract_cols(up_grad, w_one), unit_two, factor_two, vec_all[5]
    )
    low_grad_two = grad_two.astype(low)
    cross_grads = product(low_grad_two, w_out[1]).astype(low)
    (up_late,) = after([up_grad], [cross_grads])
    grad_w_one = grad_columns([(low_two, up_late)], [], depth)
    cross_grads = rows_to_heads(cross_grads)
    own_down, own_up = owned(grad_w_two), owned(grad_w_one)
    out_rows = from_planes(after([normed_three.astype(low)], [cross_grads])[0])
    saved = seg, cross_grads, cross_context, cross_lse
    cross_q_grad, far, *halves = cross_bwd(
        1, cross_queries, enc_kv, *saved, cross_queries, [grad_w_two, grad_w_one]
    )
    enc_passed = relay_start(*halves)
    cross_q_grad, *enc_terms = cross_bwd(0, cross_queries, enc_kv, *saved, cross_q_grad, [])
    (cross_q_grad,) = after([cross_q_grad], [*out_rows[1:], *enc_passed, own_down])
    cross_q_all = heads_to_rows(cross_q_grad)
    grad_one, gain_one, shift_one = normalize_back(
        grad_two + contract_cols(cross_q_all, w_cross), unit_one, factor_one, vec_all[3]
    )
    low_grad_one = grad_one.astype(low)
    self_grads = product(low_grad_one, w_out[0]).astype(low)
    grad_vectors = jnp.stack(
        [
            jnp.sum(grad_one, axis=0),
            jnp.sum(grad_two, axis=0),
            jnp.sum(grad_three, axis=0),
            gain_one,
            shift_one,
            gain_two,
            shift_two,
            gain_three,
            shift_three,
        ]
    )
    vec_part = grad_vectors.reshape(9, shards, -1).transpose(1, 0, 2).reshape(shards, -1)
    up_part = grad_up_bias.reshape(depth, -1, shards).transpose(2, 0, 1)
    small_part = [jnp.concatenate([vec_part, up_part[:, j]], axis=1) for j in range(depth)]
    small_part = jnp.concatenate([by_shard(part, shard_rows) for part in small_part], axis=1)
    self_grads = rows_to_heads(self_grads)
    enc_joined = relay_join([*enc_terms, far], enc_passed, [cross_q_all])
    own_down, own_up = after([own_down, own_up], [self_grads, *enc_joined[1:]])
    by_plane = by_plane_order([own_up, own_down], plane, depth)
    ffn = lax.psum_scatter(by_plane, T, scatter_dimension=1, tiled=True)
    enc_terms = relay_finish(enc_joined)
    q_grad, *kv_terms = self_bwd(
        queries, kv, meta, self_grads, self_context, self_lse, [*enc_joined[1:], by_plane]
    )
    kv_passed = relay_start(*kv_terms[3:])
    (cross_late,) = after([cross_q_all], [q_grad])
    grad_proj = grad_columns(
        [(low_grad_two, cross_all), (low_grad_one, self_all), (low_one, cross_late)],
        [small_part.astype(low)],
    )
    own_proj = owned(grad_proj)
    enc_grad, enc_columns = sum_terms(enc_terms, [q_grad])

    enc_parts = plane_shares([enc_grad], w_enc, plane, depth, None, [])
    enc_sent = spread(enc_parts, T)
    grad_w_enc = weight_grad(encoder, [enc_grad], [], plane, 512, enc_parts)
    kv_joined = relay_join(kv_terms, kv_passed, [ffn, grad_w_enc])

    out_rows = after(out_rows, kv_joined[1:])
    out_rows = jnp.stack(out_rows)[plane ^ jnp.arange(depth)].reshape(row_count, model_width)
    portion = row_count // groups
    returned = [pick_rows(out_rows, near[j], portion) for j in range(groups)]
    ffn = after([ffn], kv_joined[1:])[0].astype(wide)
    (down_grad,) = after([ffn[:, hidden_width:].T], kv_joined[1:])
    ffn_new = updated(2, ffn[:, :hidden_width]) + updated(3, down_grad)

    kv_grad, kv_columns = sum_terms(relay_finish(kv_joined), [grad_w_enc, enc_sent[1], *ffn_new, *returned], SOME_COST)
    returned = spread(after(returned, [kv_grad]), C)
    grad_head_bias = jnp.stack(
        [
            jnp.sum(q_grad.astype(wide), axis=0),
            kv_columns[0, head_width:],
            jnp.sum(cross_q_grad.astype(wide), axis=0),
            enc_columns[0, head_width:],
        ]
    )
    head_part = grad_head_bias.reshape(4, -1, shards).transpose(2, 0, 1).reshape(shards, -1)
    head_part = by_shard(head_part, shard_rows).astype(low)
    adds = [head_part, grad_w_enc]
    grad_first = weight_grad(tokens, [q_grad, kv_grad], adds, plane, rows, [], SOME_COST)
    (grad_first,) = after([grad_first], [own_proj])
    token_terms = plane_shares(
        [q_grad, kv_grad], w_kept, plane, depth, grad_one, [grad_first, *enc_sent[2:]], SOME_COST
    )
    token_sent = spread(token_terms, T)
    own_first = owned(grad_first)
    cuts = [0, all_heads, 2 * all_heads, 3 * all_heads, own_proj.shape[1]]
    own_proj = [own_proj[:, a:b] for a, b in zip(cuts, cuts[1:])]
    proj_parts = [column_blocks(part, depth) for part in own_proj]
    proj_parts = [jnp.concatenate([p[j] for p in proj_parts], axis=1) for j in range(depth)]
    proj_parts = after(proj_parts, token_sent[1:2])
    (own_first,) = after([own_first], token_sent[1:])
    own_first = own_first.astype(wide)
    proj = total(spread(proj_parts, T))
    result = put_blocks(jnp.concatenate(returned), places, wide)
    (token_sent[0],) = after(token_sent[:1], [result])
    grad_tokens = total(token_sent)
    grad_encoder = total(after(enc_sent, [result]))

    out_cross, out_self, in_cross = [
        proj[:, i * head_width : (i + 1) * head_width] for i in range(3)
    ]
    small_part = proj[:, 3 * head_width :].reshape(-1)
    gradients = {
        0: jnp.stack(
            column_blocks(own_first[:, : 3 * head_width], 3)
            + [in_cross]
            + column_blocks(own_first[:, 3 * head_width + 128 :], 2)
        ),
        1: after([jnp.stack([out_self.T, out_cross.T])], token_sent[1:])[0],
        4: own_first[:, 3 * head_width : 3 * head_width + 128].reshape(-1)[:n_head].reshape(head_bias.shape),
        5: small_part[n_vec : n_vec + n_up].reshape(up_bias.shape),
        6: small_part[:n_vec].reshape(vectors.shape),
    }
    clip_factor = CLIP_LIMIT / jnp.maximum(top_all, CLIP_LIMIT)
    root_factor = jnp.sqrt(clip_factor)
    column_roots = jnp.repeat(root_factor, HEAD)
    in_scale = jnp.concatenate(
        [column_roots[None], column_roots[None], jnp.ones((4, head_width), wide)], axis=0
    )[:, None, :]
    slot_heads = (jnp.arange(head_bias.shape[1]) * shards + shard_index) // HEAD
    picked = jnp.sum(
        jnp.where(slot_heads[:, None] == jnp.arange(heads)[None, :], root_factor[None, :], 0.0),
        axis=1,
    )
    bias_scale = jnp.concatenate([picked[None], jnp.ones((3, picked.shape[0]), wide)], axis=0)
    scales = {0: in_scale, 4: bias_scale[:, :, None]}
    results = [result, grad_tokens, grad_encoder, clip_factor]
    for index in range(7):
        if index in gradients:
            results += updated(index, gradients[index], scales.get(index))
        else:
            results += ffn_new[4 * (index - 2) : 4 * (index - 1)]
    return tuple(results)


def solution(mesh):
    rows, table = P(SHARD, None), P(F, None)
    weights = (
        P(None, SHARD, T),
        P(None, T, SHARD),
        P(SHARD, T),
        P(T, SHARD),
        P(None, T, SHARD),
        P(T, SHARD),
        P(None, SHARD),
    )
    by_columns = P(SHARD, T)
    updates = tuple(spec for spec in weights for _ in range(4))
    return jax.shard_map(
        per_device,
        mesh=mesh,
        in_specs=(rows, rows, rows, table, table) + weights * 3,
        out_specs=(rows, by_columns, by_columns, P(T)) + updates,
        check_vma=False,
    )
```
